32 devices in a mesh: dp: 8 (over z, y), seq: 4 (over x, core).
Axes of the slice: x: 2, y: 2, z: 4, core: 2. Of those that a mesh axis runs over, the one named last changes fastest.
Arguments:
- x_short: bfloat16 [16, 256, 512], P('dp', 'seq'), may hold values from -6 to 6
- x_long: bfloat16 [8, 512, 512], P('dp', 'seq'), may hold values from -6 to 6
- len_short: int32 [16], P('dp'), may hold values from 64 to 256, as said below
- len_long: int32 [8], P('dp'), may hold values from 128 to 512, as said below
- w_qkv: bfloat16 [2, 512, 1536], replicated, may hold values from -0.25 to 0.25
- w_out: bfloat16 [2, 512, 512], replicated, may hold values from -1.5 to 1.5
- w_up: bfloat16 [2, 512, 2048], replicated, may hold values from -0.25 to 0.25
- w_down: bfloat16 [2, 2048, 512], replicated, may hold values from -0.125 to 0.125
- pos_table: bfloat16 [2, 512, 512], replicated, may hold values from -3 to 3
- norm_gain: float32 [2, 2, 512], replicated, may hold values from 0.5 to 1.5
- norm_bias: float32 [2, 2, 512], replicated, may hold values from -1.5 to 1.5
- cot_short: bfloat16 [16, 256, 512], P('dp', 'seq'), may hold values from -6 to 6
- cot_long: bfloat16 [8, 512, 512], P('dp', 'seq'), may hold values from -6 to 6
Outputs:
- act_short: bfloat16 [16, 256, 512], P('dp', 'seq')
- act_long: bfloat16 [8, 512, 512], P('dp', 'seq')
- grad_in_short: bfloat16 [16, 256, 512], P('dp', 'seq')
- grad_in_long: bfloat16 [8, 512, 512], P('dp', 'seq')
- grad_qkv: float32 [2, 512, 1536], P(None, 'dp', 'seq')
- grad_out: float32 [2, 512, 512], P(None, 'dp', 'seq')
- grad_up: float32 [2, 512, 2048], P(None, 'dp', 'seq')
- grad_down: float32 [2, 2048, 512], P(None, 'dp', 'seq')
- grad_pos: float32 [2, 512, 512], P(None, 'dp', 'seq')
- grad_gain: float32 [2, 2, 512], P(None, None, 'dp')
- grad_bias: float32 [2, 2, 512], P(None, None, 'dp')
The draws below stay inside these ranges and needn't reach their ends.
Inputs may be any that keep to these rules, and one draw needn't show every extreme that they name: `len_short`: of each consecutive pair of short windows (0 and 1, 2 and 3, ...), one has the full length 256. `len_long`: some long window has the full length 512.
All inputs are finite; a program needn't handle non-finite values.
Results may differ from the reference program's by a relative error of at most 0.03.
Values may be sent and summed in bfloat16 or wider, within the bound.
No kernel may reach another device: no remote copies, remote signals or barrier semaphores. Data moves between devices by JAX's collectives and lax.ppermute only.
A program may use at most 128 MiB of HBM per device.

```python
import math
import jax
import jax.numpy as jnp
from jax import lax

D = 512
H = 8
FF = 2048
LAYERS = 2
LS = 256
LL = 512
SW_GRP = 2
HD = 64
NS = 16
NL = 8


def draw_len_short(key, part):
    key = jax.random.fold_in(key, 11)
    first_key, second_key = jax.random.split(key)
    lengths = jax.random.randint(first_key, (NS,), LS // 4, LS + 1)
    chosen = jax.random.randint(second_key, (NS // SW_GRP,), 0, SW_GRP)
    within = jnp.arange(NS, dtype=jnp.int32) % SW_GRP
    return jnp.where(within == jnp.repeat(chosen, SW_GRP), LS, lengths).astype(jnp.int32)


def draw_len_long(key, part):
    key = jax.random.fold_in(key, 23)
    first_key, second_key = jax.random.split(key)
    lengths = jax.random.randint(first_key, (NL,), LL // 4, LL + 1)
    chosen = jax.random.randint(second_key, (), 0, NL)
    return jnp.where(jnp.arange(NL, dtype=jnp.int32) == chosen, LL, lengths).astype(jnp.int32)


def block_levels(stream_key, dims, cuts, low, largest):
    def one(axis_at, blocks):
        heights = jax.random.uniform(jax.random.fold_in(jax.random.fold_in(stream_key, 6), axis_at), (blocks,), jnp.float32, low / len(cuts), largest / len(cuts))
        return jnp.repeat(jnp.exp(heights), dims[axis_at] // blocks).reshape((-1,) + (1,) * (len(dims) - axis_at - 1))

    loudness = one(*cuts[0])
    for cut in cuts[1:]:
        loudness = loudness * one(*cut)
    return loudness


def normal_values(rng, extent, width, reach, cuts=(), kind=jnp.bfloat16):
    result = width * jax.random.normal(rng, extent, jnp.float32)
    if cuts:
        result = result * block_levels(rng, extent, cuts, -0.22, 0.18)
    return jnp.clip(result, -reach, reach).astype(kind)


def setup_inputs(seed: int = 0) -> dict:
    seeds = jax.random.split(jax.random.key(seed), 14)
    x_short = normal_values(seeds[0], (NS, LS, D), 1.0, 6.0, ((0, 8), (1, 4)))
    x_long = normal_values(seeds[1], (NL, LL, D), 1.0, 6.0, ((0, 8), (1, 4)))
    len_short = draw_len_short(jax.random.fold_in(seeds[13], 71), 0)
    len_long = draw_len_long(jax.random.fold_in(seeds[13], 71), 0)
    w_qkv = normal_values(seeds[4], (LAYERS, D, 3 * D), D ** -0.5, 0.25)
    w_out = normal_values(seeds[5], (LAYERS, D, D), (D // 32) ** -0.5, 1.5)
    w_up = normal_values(seeds[6], (LAYERS, D, FF), D ** -0.5, 0.25)
    w_down = normal_values(seeds[7], (LAYERS, FF, D), FF ** -0.5, 0.125)
    pos_table = normal_values(seeds[8], (LAYERS, LL, D), 0.5, 3.0)
    norm_gain = jnp.clip(1.0 + 0.1 * jax.random.normal(seeds[9], (LAYERS, 2, D), jnp.float32), 0.5, 1.5)
    norm_bias = normal_values(seeds[10], (LAYERS, 2, D), 0.3, 1.5, (), jnp.float32)
    cot_short = normal_values(seeds[11], (NS, LS, D), 1.0, 6.0, ((0, 8), (1, 4)))
    cot_long = normal_values(seeds[12], (NL, LL, D), 1.0, 6.0, ((0, 8), (1, 4)))
    return dict(x_short=x_short, x_long=x_long, len_short=len_short, len_long=len_long, w_qkv=w_qkv, w_out=w_out, w_up=w_up, w_down=w_down, pos_table=pos_table, norm_gain=norm_gain, norm_bias=norm_bias, cot_short=cot_short, cot_long=cot_long)


@jax.custom_vjp
def low(v):
    return lax.optimization_barrier(v.astype(jnp.bfloat16)).astype(jnp.float32)

@jax.custom_vjp
def low_back(v):
    return v

def low_keep(v):
    return (low(v), None)

def low_pass(kept, grad):
    return (grad,)

def back_keep(v):
    return (v, None)

def back_low(kept, grad):
    return (low(grad),)
low.defvjp(low_keep, low_pass)
low_back.defvjp(back_keep, back_low)

def product(left, right, form):
    return jnp.einsum(form, left, right, precision=lax.Precision.HIGHEST)

def normalize(values_in, gain_row, shift_row):
    centre = lax.optimization_barrier(jnp.mean(values_in, axis=-1, keepdims=True))
    centred = values_in - centre
    spread = lax.optimization_barrier(jnp.mean(centred * centred, axis=-1, keepdims=True))
    return centred * lax.rsqrt(spread + 1e-05) * gain_row + shift_row

def attend(queries, key_heads, value_heads, live_lengths):
    length = queries.shape[1]
    scores = product(queries, key_heads, 'wqhe,wkhe->whqk') / math.sqrt(HD)
    row_ids = jnp.arange(length, dtype=jnp.int32)[:, None]
    col_ids = jnp.arange(length, dtype=jnp.int32)[None, :]
    allowed = (col_ids <= row_ids)[None, None] & (col_ids[None, None] < live_lengths[:, None, None, None])
    scores = low_back(jnp.where(allowed, scores, -1000000000.0))
    softened = low(jax.nn.softmax(scores, axis=-1))
    return product(softened, value_heads, 'whqk,wkhe->wqhe')

def one_layer(inputs, live_lengths, layer_at, params):
    w_qkv, w_out, w_up, w_down, pos_table, norm_gain, norm_bias = params
    windows, length = (inputs.shape[0], inputs.shape[1])
    hidden = inputs + pos_table[layer_at, :length][None]
    rounded = low(hidden)
    mixed = low_back(low(product(rounded, w_qkv[layer_at], 'wld,de->wle')))
    heads = mixed.reshape(windows, length, 3, H, HD)
    attended = low_back(low(attend(heads[:, :, 0], heads[:, :, 1], heads[:, :, 2], live_lengths)))
    branch = low_back(product(attended.reshape(windows, length, D), w_out[layer_at], 'wld,de->wle'))
    settled = normalize(hidden + branch, norm_gain[layer_at, 0], norm_bias[layer_at, 0])
    inner_pre = low_back(product(low(settled), w_up[layer_at], 'wld,df->wlf'))
    active = low(jax.nn.gelu(inner_pre, approximate=False))
    feed = low_back(product(active, w_down[layer_at], 'wlf,fd->wld'))
    return normalize(settled + feed, norm_gain[layer_at, 1], norm_bias[layer_at, 1])

def run_group(inputs, live_lengths, params):
    windows, length = (inputs.shape[0], inputs.shape[1])
    count = math.gcd(windows, max(1, 4096 // length))
    blocks = inputs.reshape(windows // count, count, length, D)
    block_lengths = live_lengths.reshape(windows // count, count)

    def both_layers(pair):
        current = pair[0]
        for layer_at in range(LAYERS):
            if layer_at > 0:
                current = low(current)
            current = one_layer(current, pair[1], layer_at, params)
        return current
    return lax.map(jax.checkpoint(both_layers), (blocks, block_lengths)).reshape(windows, length, D)

def reference(x_short, x_long, len_short, len_long, w_qkv, w_out, w_up, w_down, pos_table, norm_gain, norm_bias, cot_short, cot_long):

    def forward(short_in, long_in, qkv_f, out_f, up_f, down_f, pos_f, gain_f, bias_f):
        params = (qkv_f, out_f, up_f, down_f, pos_f, gain_f, bias_f)
        return (run_group(short_in, len_short, params), run_group(long_in, len_long, params))
    outputs, pullback = jax.vjp(forward, x_short.astype(jnp.float32), x_long.astype(jnp.float32), w_qkv.astype(jnp.float32), w_out.astype(jnp.float32), w_up.astype(jnp.float32), w_down.astype(jnp.float32), pos_table.astype(jnp.float32), norm_gain.astype(jnp.float32), norm_bias.astype(jnp.float32))
    gradients = pullback((cot_short.astype(jnp.float32), cot_long.astype(jnp.float32)))
    return (outputs[0].astype(jnp.bfloat16), outputs[1].astype(jnp.bfloat16), gradients[0].astype(jnp.bfloat16), gradients[1].astype(jnp.bfloat16), gradients[2], gradients[3], gradients[4], gradients[5], gradients[6], gradients[7], gradients[8])
```

```python
import functools
import math

import jax
import jax.numpy as jnp
from jax import lax
from jax.sharding import PartitionSpec as P

LAYERS = 2
HD = 64


def normalize(values_in, gain_row, shift_row):
    centre = jnp.mean(values_in, axis=-1, keepdims=True)
    centred = values_in - centre
    spread = jnp.mean(centred * centred, axis=-1, keepdims=True)
    return centred * lax.rsqrt(spread + 1e-05) * gain_row + shift_row


def norm_back(values_in, gain_row, shift_row, gradient):
    unused, pullback = jax.vjp(normalize, values_in, gain_row, shift_row)
    return pullback(gradient)


def project_front(inputs, table_layer, weight):
    windows, local_len = (inputs.shape[0], inputs.shape[1])
    row_start = lax.axis_index("seq") * local_len
    pos_rows = lax.dynamic_slice_in_dim(table_layer, row_start, local_len, 0).astype(jnp.float32)
    hidden = inputs.astype(jnp.float32) + pos_rows[None]
    rounded = hidden.astype(jnp.bfloat16)
    mixed = jnp.einsum("wld,de->wle", rounded, weight, preferred_element_type=jnp.float32)
    packed = mixed.astype(jnp.bfloat16).reshape(windows, local_len, 3, lax.axis_size("seq"), -1)
    return (hidden, rounded, packed)


def split_heads(heads):
    windows, length = (heads.shape[0], heads.shape[1])
    split_up = heads.reshape(windows, length, 3, -1, HD)
    return (split_up[:, :, 0], split_up[:, :, 1], split_up[:, :, 2])


def masked_scores(queries, key_heads, live_lengths):
    length = queries.shape[1]
    scores = jnp.einsum(
        "wqhe,wkhe->whqk", queries, key_heads, preferred_element_type=jnp.float32
    ) / math.sqrt(HD)
    row_ids = lax.broadcasted_iota(jnp.int32, (length, length), 0)
    col_ids = lax.broadcasted_iota(jnp.int32, (length, length), 1)
    allowed = (col_ids <= row_ids)[None, None] & (
        col_ids[None, None] < live_lengths[:, None, None, None]
    )
    return (jnp.where(allowed, scores, -1000000000.0), allowed)


def attend(heads, live_lengths):
    windows, length = (heads.shape[0], heads.shape[1])
    queries, key_heads, value_heads = split_heads(heads)
    scores, allowed = masked_scores(queries, key_heads, live_lengths)
    row_max = jnp.max(scores, axis=-1, keepdims=True)
    lifted = jnp.exp(scores - row_max)
    row_sum = jnp.sum(lifted, axis=-1, keepdims=True)
    softened = (lifted / row_sum).astype(jnp.bfloat16)
    output = jnp.einsum(
        "whqk,wkhe->wqhe", softened, value_heads, preferred_element_type=jnp.float32
    )
    return (output.astype(jnp.bfloat16).reshape(windows, length, 1, -1), row_max + jnp.log(row_sum))


def dense_tail(hidden, tokens, out_weight, up_weight, down_weight, gain_rows, shift_rows):
    pre_first = hidden + jnp.einsum(
        "wld,de->wle", tokens, out_weight, preferred_element_type=jnp.float32
    )
    settled = normalize(pre_first, gain_rows[0], shift_rows[0])
    rounded_mid = settled.astype(jnp.bfloat16)
    inner_pre = jnp.einsum(
        "wld,df->wlf", rounded_mid, up_weight, preferred_element_type=jnp.float32
    )
    active = jax.nn.gelu(inner_pre, approximate=False).astype(jnp.bfloat16)
    second = settled + jnp.einsum(
        "wlf,fd->wld", active, down_weight, preferred_element_type=jnp.float32
    )
    return (
        (pre_first, settled, rounded_mid, inner_pre, active, second),
        normalize(second, gain_rows[1], shift_rows[1]),
    )


def layer_forward(layer_at, inputs, lengths, weights):
    w_qkv, w_out, w_up, w_down, pos_table, norm_gain, norm_bias = weights
    hid_short, low_short, pack_short = project_front(
        inputs[0], pos_table[layer_at], w_qkv[layer_at]
    )
    hid_long, low_long, pack_long = project_front(inputs[1], pos_table[layer_at], w_qkv[layer_at])
    heads_short, heads_long = (
        lax.all_to_all(pack_short, "seq", split_axis=3, concat_axis=1, tiled=True),
        lax.all_to_all(pack_long, "seq", split_axis=3, concat_axis=1, tiled=True),
    )
    out_short, lse_short = attend(heads_short, lengths[0])
    out_long, lse_long = attend(heads_long, lengths[1])
    tok_short, tok_long = (
        lax.all_to_all(out_short, "seq", split_axis=1, concat_axis=2, tiled=True),
        lax.all_to_all(out_long, "seq", split_axis=1, concat_axis=2, tiled=True),
    )
    tok_short = tok_short.reshape(tok_short.shape[0], tok_short.shape[1], -1)
    tok_long = tok_long.reshape(tok_long.shape[0], tok_long.shape[1], -1)
    kept_short, y_short = dense_tail(
        hid_short,
        tok_short,
        w_out[layer_at],
        w_up[layer_at],
        w_down[layer_at],
        norm_gain[layer_at],
        norm_bias[layer_at],
    )
    kept_long, y_long = dense_tail(
        hid_long,
        tok_long,
        w_out[layer_at],
        w_up[layer_at],
        w_down[layer_at],
        norm_gain[layer_at],
        norm_bias[layer_at],
    )
    state_short = (low_short, heads_short, lse_short, tok_short, kept_short)
    state_long = (low_long, heads_long, lse_long, tok_long, kept_long)
    return ((y_short, y_long), (state_short, state_long))


def tail_back(saved_state, gradient, out_weight, up_weight, down_weight, gain_rows, shift_rows):
    tokens = saved_state[3]
    pre_first, settled, rounded_mid, inner_pre, active, second = saved_state[4]
    d_second, gain_late, shift_late = norm_back(second, gain_rows[1], shift_rows[1], gradient)
    d_feed = d_second.astype(jnp.bfloat16)
    g_down = jnp.einsum("wlf,wld->fd", active, d_feed, preferred_element_type=jnp.float32)
    d_active = jnp.einsum("wld,fd->wlf", d_feed, down_weight, preferred_element_type=jnp.float32)
    unused, gelu_back = jax.vjp(functools.partial(jax.nn.gelu, approximate=False), inner_pre)
    d_inner = gelu_back(d_active)[0].astype(jnp.bfloat16)
    g_up = jnp.einsum("wld,wlf->df", rounded_mid, d_inner, preferred_element_type=jnp.float32)
    d_settled = d_second + jnp.einsum(
        "wlf,df->wld", d_inner, up_weight, preferred_element_type=jnp.float32
    )
    d_first, gain_early, shift_early = norm_back(pre_first, gain_rows[0], shift_rows[0], d_settled)
    d_branch = d_first.astype(jnp.bfloat16)
    g_out = jnp.einsum("wld,wle->de", tokens, d_branch, preferred_element_type=jnp.float32)
    d_tokens = jnp.einsum(
        "wle,de->wld", d_branch, out_weight, preferred_element_type=jnp.float32
    ).astype(jnp.bfloat16)
    d_gains = jnp.stack([gain_early, gain_late])
    d_shifts = jnp.stack([shift_early, shift_late])
    return (d_first, d_tokens, g_out, g_up, g_down, d_gains, d_shifts)


def attend_back(heads, live_lengths, log_sums, d_out):
    windows, length = (heads.shape[0], heads.shape[1])
    queries, key_heads, value_heads = split_heads(heads)
    gradient = d_out.reshape(windows, length, -1, HD)
    scores, allowed = masked_scores(queries, key_heads, live_lengths)
    softened = jnp.where(allowed, jnp.exp(scores - log_sums), 0.0)
    d_probs = jnp.einsum(
        "wqhe,wkhe->whqk", gradient, value_heads, preferred_element_type=jnp.float32
    )
    d_values = jnp.einsum(
        "whqk,wqhe->wkhe",
        softened.astype(jnp.bfloat16),
        gradient,
        preferred_element_type=jnp.float32,
    )
    d_scores = softened * (d_probs - jnp.sum(softened * d_probs, axis=-1, keepdims=True))
    d_scores = d_scores.astype(jnp.bfloat16)
    d_queries = jnp.einsum(
        "whqk,wkhe->wqhe", d_scores, key_heads, preferred_element_type=jnp.float32
    ) / math.sqrt(HD)
    d_keys = jnp.einsum(
        "whqk,wqhe->wkhe", d_scores, queries, preferred_element_type=jnp.float32
    ) / math.sqrt(HD)
    stacked = jnp.stack([d_queries, d_keys, d_values], axis=2).astype(jnp.bfloat16)
    return stacked.reshape(windows, length, 3, 1, -1)


def front_back(rounded, back_qkv, d_first, weight, table_rows):
    windows, local_len = (rounded.shape[0], rounded.shape[1])
    d_qkv = back_qkv.reshape(windows, local_len, -1)
    g_qkv = jnp.einsum("wld,wle->de", rounded, d_qkv, preferred_element_type=jnp.float32)
    d_hidden = d_first + jnp.einsum(
        "wle,de->wld", d_qkv, weight, preferred_element_type=jnp.float32
    )
    row_sums = jnp.sum(d_hidden, axis=0)
    blank_table = jnp.zeros((table_rows, row_sums.shape[1]), jnp.float32)
    g_pos = lax.dynamic_update_slice_in_dim(
        blank_table, row_sums, lax.axis_index("seq") * local_len, 0
    )
    return (g_qkv, d_hidden, g_pos)


def layer_backward(layer_at, saved_states, cotangents, lengths, weights):
    w_qkv, w_out, w_up, w_down, pos_table, norm_gain, norm_bias = weights
    back_short = tail_back(
        saved_states[0],
        cotangents[0],
        w_out[layer_at],
        w_up[layer_at],
        w_down[layer_at],
        norm_gain[layer_at],
        norm_bias[layer_at],
    )
    back_long = tail_back(
        saved_states[1],
        cotangents[1],
        w_out[layer_at],
        w_up[layer_at],
        w_down[layer_at],
        norm_gain[layer_at],
        norm_bias[layer_at],
    )
    send_short = back_short[1].reshape(
        back_short[1].shape[0], back_short[1].shape[1], lax.axis_size("seq"), -1
    )
    send_long = back_long[1].reshape(
        back_long[1].shape[0], back_long[1].shape[1], lax.axis_size("seq"), -1
    )
    d_heads_short, d_heads_long = (
        lax.all_to_all(send_short, "seq", split_axis=2, concat_axis=1, tiled=True),
        lax.all_to_all(send_long, "seq", split_axis=2, concat_axis=1, tiled=True),
    )
    dqkv_short = attend_back(saved_states[0][1], lengths[0], saved_states[0][2], d_heads_short)
    dqkv_long = attend_back(saved_states[1][1], lengths[1], saved_states[1][2], d_heads_long)
    back_qkv_short, back_qkv_long = (
        lax.all_to_all(dqkv_short, "seq", split_axis=1, concat_axis=3, tiled=True),
        lax.all_to_all(dqkv_long, "seq", split_axis=1, concat_axis=3, tiled=True),
    )
    table_rows = pos_table.shape[1]
    front_short = front_back(
        saved_states[0][0], back_qkv_short, back_short[0], w_qkv[layer_at], table_rows
    )
    front_long = front_back(
        saved_states[1][0], back_qkv_long, back_long[0], w_qkv[layer_at], table_rows
    )
    layer_grads = (
        front_short[0] + front_long[0],
        back_short[2] + back_long[2],
        back_short[3] + back_long[3],
        back_short[4] + back_long[4],
        front_short[2] + front_long[2],
        back_short[5] + back_long[5],
        back_short[6] + back_long[6],
    )
    return ((front_short[1], front_long[1]), layer_grads)


def bits_of(size):
    return range(size.bit_length() - 1)


def halve(blocks, axis, bit):
    size = lax.axis_size(axis)
    mine = (lax.axis_index(axis) >> bit) & 1
    sent = lax.dynamic_index_in_dim(blocks, 1 - mine, 0, keepdims=False)
    kept = lax.dynamic_index_in_dim(blocks, mine, 0, keepdims=False)
    got = lax.ppermute(sent, axis, [(at, at ^ (1 << bit)) for at in range(size)])
    return kept + got


def scatter_sum(matrix, seq_last):
    rows, columns = matrix.shape
    n_dp, n_seq = lax.axis_size("dp"), lax.axis_size("seq")
    dp_bits, seq_bits = list(bits_of(n_dp)), list(bits_of(n_seq))
    shape = [2] * len(dp_bits) + [rows // n_dp] + [2] * len(seq_bits) + [columns // n_seq]
    blocks = matrix.astype(jnp.bfloat16).reshape(shape)
    places = {("dp", bit): len(dp_bits) - 1 - bit for bit in dp_bits}
    places.update({("seq", bit): len(shape) - 2 - bit for bit in seq_bits})
    late = [("seq", bit) for bit in seq_bits[1:]]
    middle = [("dp", bit) for bit in dp_bits]
    steps = [("seq", 0)] + (middle + late if seq_last else late + middle)
    order = [places[step] for step in steps] + [len(dp_bits), len(shape) - 1]
    blocks = blocks.transpose(order)
    for axis, bit in steps:
        blocks = halve(blocks, axis, bit)
    return blocks


def local(
    x_short,
    x_long,
    len_short,
    len_long,
    w_qkv,
    w_out,
    w_up,
    w_down,
    pos_table,
    norm_gain,
    norm_bias,
    cot_short,
    cot_long,
):
    weights = (w_qkv, w_out, w_up, w_down, pos_table, norm_gain, norm_bias)
    lengths = (len_short, len_long)
    layer_inputs = []
    kept_states = []
    current = (x_short, x_long)
    for layer_at in range(LAYERS):
        layer_inputs.append(current)
        outputs, saved_state = layer_forward(layer_at, current, lengths, weights)
        kept_states.append(saved_state)
        current = (outputs[0].astype(jnp.bfloat16), outputs[1].astype(jnp.bfloat16))
    cotangents = (cot_short.astype(jnp.float32), cot_long.astype(jnp.float32))
    per_layer = [None] * LAYERS
    for layer_at in reversed(range(LAYERS)):
        unused, saved_state = layer_forward(layer_at, layer_inputs[layer_at], lengths, weights)
        cotangents, layer_grads = layer_backward(
            layer_at, saved_state, cotangents, lengths, weights
        )
        per_layer[layer_at] = layer_grads
    summed = []
    for slot in range(5):
        entries = [
            scatter_sum(per_layer[layer_at][slot], slot in (3, 4)) for layer_at in range(LAYERS)
        ]
        summed.append(jnp.stack(entries).astype(jnp.float32))
    totals = [jnp.stack([entry[slot] for entry in per_layer]) for slot in range(7)]
    gain_sum, bias_sum = lax.psum((totals[5], totals[6]), ("dp", "seq"))
    share_width = gain_sum.shape[2] // lax.axis_size("dp")
    share_start = lax.axis_index("dp") * share_width
    gain_share = lax.dynamic_slice_in_dim(gain_sum, share_start, share_width, 2)
    bias_share = lax.dynamic_slice_in_dim(bias_sum, share_start, share_width, 2)
    return (
        current[0],
        current[1],
        cotangents[0].astype(jnp.bfloat16),
        cotangents[1].astype(jnp.bfloat16),
        summed[0],
        summed[1],
        summed[2],
        summed[3],
        summed[4],
        gain_share,
        bias_share,
    )


def solution(mesh):
    return jax.shard_map(
        local,
        mesh=mesh,
        in_specs=(
            P("dp", "seq", None),
            P("dp", "seq", None),
            P("dp"),
            P("dp"),
            P(),
            P(),
            P(),
            P(),
            P(),
            P(),
            P(),
            P("dp", "seq", None),
            P("dp", "seq", None),
        ),
        out_specs=(
            P("dp", "seq", None),
            P("dp", "seq", None),
            P("dp", "seq", None),
            P("dp", "seq", None),
            P(None, "dp", "seq"),
            P(None, "dp", "seq"),
            P(None, "dp", "seq"),
            P(None, "dp", "seq"),
            P(None, "dp", "seq"),
            P(None, None, "dp"),
            P(None, None, "dp"),
        ),
        check_vma=False,
    )
```

```python
import functools

import jax
import jax.numpy as jnp
from jax import lax
from jax.experimental import pallas as pl
from jax.experimental.pallas import tpu as pltpu
from jax.sharding import PartitionSpec as P

LAYERS = 2
HD = 64
F32 = jnp.float32
BF16 = jnp.bfloat16
NEG = -1000000000.0
VMEM_BYTES = 56 * 1024 * 1024


def dot(left, right):
    return lax.dot_general(left, right, (((1,), (0,)), ((), ())), preferred_element_type=F32)


def dot_nt(left, right):
    return lax.dot_general(left, right, (((1,), (1,)), ((), ())), preferred_element_type=F32)


def dot_tn(left, right):
    return lax.dot_general(left, right, (((0,), (0,)), ((), ())), preferred_element_type=F32)


ME, LIVE, Y = 0, 1, 2


def aligned(value, step):
    return pl.multiple_of(value, step)


def block_start(info, block, core, size):
    is_long = info[ME] < 2
    return aligned(jnp.where(is_long, (2 * block + core) * size, block * size), size)


def norm_forward(values, gain, shift):
    centre = jnp.mean(values, axis=-1, keepdims=True)
    centred = values - centre
    spread = jnp.mean(centred * centred, axis=-1, keepdims=True)
    scale = lax.rsqrt(spread + 1e-05)
    unit = centred * scale
    return unit, scale, unit * gain + shift


def norm_backward(unit, scale, gain, gradient):
    d_gain = jnp.sum(gradient * unit, axis=0, keepdims=True)
    d_shift = jnp.sum(gradient, axis=0, keepdims=True)
    scaled = gradient * gain
    mean_one = jnp.mean(scaled, axis=-1, keepdims=True)
    mean_two = jnp.mean(scaled * unit, axis=-1, keepdims=True)
    return scale * (scaled - mean_one - unit * mean_two), d_gain, d_shift


def positions(info, rows, core, size):
    is_long = info[ME] < 2
    spread = (rows // size) * (2 * size) + core * size + rows % size
    return jnp.where(is_long, spread, rows)


def fill_bias(info, bias_near, bias_far, size):
    core = info[ME] % 2
    is_long = info[ME] < 2
    half = bias_near.shape[1]
    for at, ref in ((0, bias_near), (1, bias_far)):
        queries = positions(info, lax.broadcasted_iota(jnp.int32, (half, half), 1) + at * half, core, size)
        for part in range(2 * (at + 1)):
            rows = lax.broadcasted_iota(jnp.int32, (half, half), 0) + (part // 2) * half
            if part % 2 == 0:
                keys = positions(info, rows, core, size)
            else:
                keys = jnp.where(is_long, positions(info, rows, 1 - core, size), 1 << 20)
            allowed = (keys <= queries) & (keys < info[LIVE])
            ref[pl.ds(part * half, half), :] = jnp.where(allowed, 0.0, NEG)


def interleave(near, far, columns, half):
    return jnp.concatenate(
        [near[:half, columns], far[:half, columns], near[half:, columns], far[half:, columns]], axis=0
    )


def lane_masks(half):
    lanes = lax.broadcasted_iota(jnp.int32, (half, 2 * HD), 1)
    first = jnp.where(lanes < HD, 1.0, 0.0).astype(BF16)
    return first, (1.0 - first.astype(F32)).astype(BF16)


def both_heads(rows, masks):
    return jnp.concatenate([rows * masks[0], rows * masks[1]], axis=0)


def attend_forward(query, kv_near, kv_far, bias_near, bias_far, probs_near, probs_far, attended):
    width = query.shape[1]
    half = query.shape[0] // 2
    masks = lane_masks(half)
    for pair in range(width // (2 * HD)):
        columns = slice(pair * 2 * HD, (pair + 1) * 2 * HD)
        keys = interleave(kv_near, kv_far, columns, half)
        values = interleave(kv_near, kv_far, slice(columns.start + width, columns.stop + width), half)
        for at, bias, probs in ((0, bias_near, probs_near), (1, bias_far, probs_far)):
            count = bias.shape[0]
            pair_query = both_heads(query[pl.ds(at * half, half), columns], masks)
            scores = dot_nt(keys[:count], pair_query) + jnp.concatenate([bias[...], bias[...]], axis=1)
            peak = jnp.max(scores, axis=0, keepdims=True)
            lifted = jnp.exp(scores - peak)
            total = jnp.sum(lifted, axis=0, keepdims=True)
            softened = (lifted * (1.0 / total)).astype(BF16)
            probs[pair] = softened
            turned = dot_tn(values[:count], softened)
            turned = jnp.concatenate([turned[:HD, :half], turned[HD:, half:]], axis=0)
            attended[pl.ds(at * half, half), columns] = turned.T.astype(BF16)


def attend_backward(query, kv_near, kv_far, probs_near, probs_far, d_att, d_query, d_kv_near, d_kv_far):
    width = query.shape[1]
    half = query.shape[0] // 2
    masks = lane_masks(half)
    for pair in range(width // (2 * HD)):
        columns = slice(pair * 2 * HD, (pair + 1) * 2 * HD)
        late = slice(columns.start + width, columns.stop + width)
        keys = interleave(kv_near, kv_far, columns, half)
        values = interleave(kv_near, kv_far, late, half)
        d_keys, d_values = [], []
        for at, probs_ref in ((0, probs_near), (1, probs_far)):
            count = probs_ref.shape[1]
            pair_query = both_heads(query[pl.ds(at * half, half), columns], masks)
            pair_grad = both_heads(d_att[pl.ds(at * half, half), columns], masks)
            softened = probs_ref[pair]
            probs = softened.astype(F32)
            d_probs = dot_nt(values[:count], pair_grad)
            row_sum = jnp.sum(probs * d_probs, axis=0, keepdims=True)
            d_scores = (probs * (d_probs - row_sum)).astype(BF16)
            d_values.append(dot(softened, pair_grad))
            d_keys.append(dot(d_scores, pair_query))
            turned = dot_tn(keys[:count], d_scores)
            turned = jnp.concatenate([turned[:HD, :half], turned[HD:, half:]], axis=0)
            d_query[pl.ds(at * half, half), columns] = (turned.T * (1.0 / HD**0.5)).astype(BF16)
        for parts, place in ((d_keys, columns), (d_values, late)):
            first = (parts[0] + parts[1][: 2 * half]).astype(BF16)
            second = parts[1][2 * half :].astype(BF16)
            d_kv_near[:half, place] = first[:half]
            d_kv_far[:half, place] = first[half:]
            d_kv_near[half:, place] = second[:half]
            d_kv_far[half:, place] = second[half:]


def project(rounded, w_qkv, query, kv):
    width = query.shape[1]
    for at in range(3):
        mixed = dot(rounded, w_qkv[:, at * width : (at + 1) * width]).astype(BF16)
        if at == 0:
            query[...] = mixed * jnp.asarray(1.0 / HD**0.5, BF16)
        else:
            kv[:, (at - 1) * width : at * width] = mixed


def tail_forward(hidden, attended, w_out, w_up, w_down, gains, shifts, active, slope, settled_low, units, scales, waits):
    inner_width = w_up.shape[1]
    step = 512
    waits[0]()
    pre_first = hidden[...] + dot(attended[...], w_out[...])
    unit, scale, settled = norm_forward(pre_first, gains[0], shifts[0])
    units[0], scales[0] = unit, scale
    rounded = settled.astype(BF16)
    settled_low[...] = rounded
    second = settled
    waits[1]()
    for at in range(inner_width // step):
        span = slice(at * step, (at + 1) * step)
        inner = dot(rounded, w_up[:, span])
        area = 0.5 + 0.5 * lax.erf(inner * (0.5**0.5))
        bell = jnp.exp(inner * inner * -0.5) * ((2.0 * jnp.pi) ** -0.5)
        glow = (inner * area).astype(BF16)
        active[:, span] = glow
        slope[:, span] = (area + inner * bell).astype(BF16)
        if at == 0:
            waits[2]()
        second = second + dot(glow, w_down[span, :])
    unit, scale, result = norm_forward(second, gains[1], shifts[1])
    units[1], scales[1] = unit, scale
    return result


def tail_backward(info, gradient, w_out, w_up, w_down, gains, slope, units, scales, kept, sent, norm_grads, d_first_out, d_att):
    inner_width = w_up.shape[1]
    width = w_up.shape[0]
    shards = 4
    step, part = inner_width // shards, width // shards
    core = info[ME] % 2
    d_second, d_gain, d_shift = norm_backward(units[1], scales[1], gains[1], gradient)
    norm_grads[1:2, :] = d_gain
    norm_grads[3:4, :] = d_shift
    d_feed = d_second.astype(BF16)
    d_settled = d_second

    def place(at, columns, value):
        @pl.when(at % 2 == core)
        def _():
            kept[at // 2, :, columns] = value

        @pl.when(at % 2 != core)
        def _():
            sent[at // 2, :, columns] = value

    for at in range(shards):
        span = slice(at * step, (at + 1) * step)
        d_active = dot_nt(d_feed, w_down[span, :])
        d_inner = (d_active * slope[:, span].astype(F32)).astype(BF16)
        place(at, slice(0, step), d_inner)
        place(at, slice(step, step + part), d_feed[:, at * part : (at + 1) * part])
        d_settled = d_settled + dot_nt(d_inner, w_up[:, span])
    d_first, d_gain, d_shift = norm_backward(units[0], scales[0], gains[0], d_settled)
    norm_grads[0:1, :] = d_gain
    norm_grads[2:3, :] = d_shift
    d_first_out[...] = d_first
    d_branch = d_first.astype(BF16)
    for at in range(shards):
        place(at, slice(step + part, step + 2 * part), d_branch[:, at * part : (at + 1) * part])
    d_att[...] = dot_nt(d_branch, w_out[...]).astype(BF16)


def fetches(pairs, sems):
    copies = [pltpu.make_async_copy(source, target, sems.at[at]) for at, (source, target) in enumerate(pairs)]
    for copy in copies:
        copy.start()
    return [copy.wait for copy in copies]


def add_table(info, table, layer_at, get_rows, hidden):
    core = info[ME] % 2
    size = hidden.shape[0] // 4
    for block in range(4):
        start = block_start(info, block, core, size)
        rows = table[layer_at, pl.ds(start, size), :].astype(F32)
        hidden[block * size : (block + 1) * size, :] = get_rows(block) + rows


def split_kernel(info, x_short, x_long, cot_short, cot_long, *outs):
    size = x_short.shape[1]
    for short, long, refs in ((x_short, x_long, outs[:4]), (cot_short, cot_long, outs[4:])):
        for delta in range(4):
            target = info[ME] ^ delta

            @pl.when(target < 2)
            def _():
                refs[delta][...] = long[0, pl.ds(aligned(jnp.minimum(target, 1) * size, size), size), :]

            @pl.when(target >= 2)
            def _():
                refs[delta][...] = short[jnp.maximum(target - 2, 0)]


def join_kernel(info, *refs):
    size = refs[0].shape[0]
    short, long = refs[4], refs[5]
    for delta in range(4):
        source = info[ME] ^ delta

        @pl.when(source < 2)
        def _():
            long[0, pl.ds(aligned(jnp.minimum(source, 1) * size, size), size), :] = refs[delta][...]

        @pl.when(source >= 2)
        def _():
            short[jnp.maximum(source - 2, 0)] = refs[delta][...]


def front_kernel(info, r0, r1, r2, r3, table, w_qkv, hidden, rounded, query, kv):
    size = r0.shape[0]
    core = info[ME] % 2
    for delta, ref in enumerate((r0, r1, r2, r3)):
        block = info[ME] ^ delta
        start = block_start(info, block, core, size)
        rows = ref[...].astype(F32) + table[0, pl.ds(start, size), :].astype(F32)
        hidden[pl.ds(aligned(block * size, size), size), :] = rows
    low = hidden[...].astype(BF16)
    rounded[...] = low
    project(low, w_qkv.at[0], query, kv)


def first_kernel(
    info, query, kv_near, kv_far, hidden, rounded, table, gains, shifts, w_qkv, w_out, w_up, w_down,
    probs_near, probs_far, slope, kept_x, units, scales, hidden_next, rounded_next, query_next, kv_next,
    bias_near, bias_far, v_out, v_up, v_down, v_qkv, sems,
):
    waits = fetches(((w_out.at[0], v_out), (w_up.at[0], v_up), (w_down.at[0], v_down), (w_qkv.at[1], v_qkv)), sems)
    width, inner = v_up.shape
    size = query.shape[0] // 4
    fill_bias(info, bias_near, bias_far, size)
    attended = kept_x.at[:, inner + width : inner + 2 * width]
    attend_forward(query, kv_near, kv_far, bias_near, bias_far, probs_near, probs_far, attended)
    kept_x[:, inner + 2 * width :] = rounded[...]
    result = tail_forward(
        hidden, attended, v_out, v_up, v_down, gains[0], shifts[0],
        kept_x.at[:, :inner], slope, kept_x.at[:, inner : inner + width], units, scales, waits,
    ).astype(BF16).astype(F32)
    add_table(info, table, 1, lambda block: result[block * size : (block + 1) * size], hidden_next)
    low = hidden_next[...].astype(BF16)
    rounded_next[...] = low
    waits[3]()
    project(low, v_qkv, query_next, kv_next)


def second_kernel(
    info, query, kv_near, kv_far, hidden, rounded, c0, c1, c2, c3, gains, shifts, w_out, w_up, w_down,
    probs_near, probs_far, kept_x, a0, a1, a2, a3, bx_kept, bx_sent, norm_grads, d_first, d_att,
    bias_near, bias_far, units, scales, slope, cot, result, v_out, v_up, v_down, sems,
):
    waits = fetches(((w_out.at[1], v_out), (w_up.at[1], v_up), (w_down.at[1], v_down)), sems)
    width, inner = v_up.shape
    size = c0.shape[0]
    fill_bias(info, bias_near, bias_far, size)
    attended = kept_x.at[:, inner + width : inner + 2 * width]
    attend_forward(query, kv_near, kv_far, bias_near, bias_far, probs_near, probs_far, attended)
    kept_x[:, inner + 2 * width :] = rounded[...]
    result[...] = tail_forward(
        hidden, attended, v_out, v_up, v_down, gains[1], shifts[1],
        kept_x.at[:, :inner], slope, kept_x.at[:, inner : inner + width], units, scales, waits,
    ).astype(BF16)
    for delta, (cot_part, act) in enumerate(((c0, a0), (c1, a1), (c2, a2), (c3, a3))):
        rows = pl.ds(aligned((info[ME] ^ delta) * size, size), size)
        cot[rows, :] = cot_part[...].astype(F32)
        act[...] = result[rows, :]
    tail_backward(
        info, cot[...], v_out, v_up, v_down, gains[1], slope, units, scales,
        bx_kept, bx_sent, norm_grads, d_first, d_att,
    )


def attend_back_kernel(query, kv_near, kv_far, probs_near, probs_far, d_att, d_query, d_kv_near, d_kv_far):
    attend_backward(query, kv_near, kv_far, probs_near, probs_far, d_att, d_query, d_kv_near, d_kv_far)


def close_layer(info, d_query, d_kv, d_kv_far, d_first, w_qkv, kept, sent):
    shards = 4
    width = d_query.shape[1]
    core = info[ME] % 2
    total = (d_kv[...].astype(F32) + d_kv_far[...].astype(F32)).astype(BF16)
    d_qkv = jnp.concatenate([d_query[...], total], axis=1)
    d_hidden = d_first[...] + dot_nt(d_qkv, w_qkv[...])
    low = d_hidden.astype(BF16)
    step, part = 3 * width // shards, width // shards
    for at in range(shards):
        pieces = (
            (slice(0, step), d_qkv[:, at * step : (at + 1) * step]),
            (slice(step, step + part), low[:, at * part : (at + 1) * part]),
        )

        @pl.when(at % 2 == core)
        def _():
            for columns, value in pieces:
                kept[at // 2, :, columns] = value

        @pl.when(at % 2 != core)
        def _():
            for columns, value in pieces:
                sent[at // 2, :, columns] = value

    return d_hidden, low


def middle_kernel(
    info, d_query, d_kv, d_kv_far, d_first, w_qkv, gains, slope, units, scales, w_out, w_up, w_down,
    qx_kept, qx_sent, bx_kept, bx_sent, norm_grads, d_first_out, d_att, v_out, v_up, v_down, sems,
):
    waits = fetches(((w_down.at[0], v_down), (w_up.at[0], v_up), (w_out.at[0], v_out)), sems)
    d_hidden, unused = close_layer(info, d_query, d_kv, d_kv_far, d_first, w_qkv.at[0], qx_kept, qx_sent)
    for wait in waits:
        wait()
    tail_backward(
        info, d_hidden, v_out, v_up, v_down, gains[0], slope, units, scales,
        bx_kept, bx_sent, norm_grads, d_first_out, d_att,
    )


def last_kernel(info, d_query, d_kv, d_kv_far, d_first, w_qkv, qx_kept, qx_sent, g0, g1, g2, g3, low_ref):
    size = g0.shape[0]
    unused, low = close_layer(info, d_query, d_kv, d_kv_far, d_first, w_qkv.at[0], qx_kept, qx_sent)
    low_ref[...] = low
    for delta, ref in enumerate((g0, g1, g2, g3)):
        ref[...] = low_ref[pl.ds(aligned((info[ME] ^ delta) * size, size), size), :]


def feed_grad_kernel(info, x_near, x_far, b_near, b_far, up_kept, up_sent, down_kept, down_sent, down):
    width = up_kept.shape[0]
    step = up_kept.shape[1]
    inner = down.shape[0]
    part = down.shape[1] // 2
    my_x = info[ME] // 2
    for ref, at in ((up_sent, 1 - my_x), (up_kept, my_x)):
        total = dot_tn(x_near[:, inner : inner + width], b_near[at, :, :step])
        total = total + dot_tn(x_far[:, inner : inner + width], b_far[at, :, :step])
        ref[...] = total.astype(BF16)
    feeds = [
        jnp.concatenate([ref[0, :, step : step + part], ref[1, :, step : step + part]], axis=1)
        for ref in (b_near, b_far)
    ]
    for at in range(inner // 512):
        span = slice(at * 512, (at + 1) * 512)
        turned = dot_tn(feeds[0], x_near[:, span]) + dot_tn(feeds[1], x_far[:, span])
        down[span, :] = turned.astype(BF16).T
    blocks, rows = down_kept.shape[0], down_kept.shape[1]
    for at in range(blocks):
        for ref, bit in ((down_kept, info[Y]), (down_sent, 1 - info[Y])):
            ref[at] = down[pl.ds(aligned((2 * at + bit) * rows, rows), rows), :]


def attend_grad_kernel(info, x_near, x_far, b_near, b_far, q_near, q_far, kept, sent, table):
    width = kept.shape[0]
    inner = x_near.shape[1] - 3 * width
    step = q_near.shape[2] - width // 4
    part = width // 4
    feed = b_near.shape[2] - part
    core = info[ME] % 2
    my_x = info[ME] // 2
    size = x_near.shape[0] // 4
    for ref, at in ((sent, 1 - my_x), (kept, my_x)):
        lows = slice(inner + 2 * width, inner + 3 * width)
        total = dot_tn(x_near[:, lows], q_near[at, :, :step]) + dot_tn(x_far[:, lows], q_far[at, :, :step])
        ref[:, :step] = total.astype(BF16)
        outs = slice(inner + width, inner + 2 * width)
        total = dot_tn(x_near[:, outs], b_near[at, :, feed:]) + dot_tn(x_far[:, outs], b_far[at, :, feed:])
        ref[:, step : step + part] = total.astype(BF16)
        table[...] = jnp.zeros_like(table)
        for source, place in ((q_near, core), (q_far, 1 - core)):
            for block in range(4):
                rows = pl.ds(block_start(info, block, place, size), size)
                table[rows, :] += source[at, block * size : (block + 1) * size, step:].astype(F32)
        ref[:, step + part :] = table[...].astype(BF16)


SMEM = pl.BlockSpec(memory_space=pltpu.SMEM)
VMEM = pl.BlockSpec(memory_space=pltpu.VMEM)
ANY = pl.BlockSpec(memory_space=pl.ANY)


def one(array, layer_at):
    return pl.BlockSpec((1,) + array.shape[1:], lambda *unused: (layer_at,) + (0,) * (array.ndim - 1))


def call(kernel, outs, specs, args, scratch=(), flops=0):
    shapes = [jax.ShapeDtypeStruct(shape, kind) for shape, kind in outs]
    size = sum(shape.size * shape.dtype.itemsize for shape in shapes)
    return pl.pallas_call(
        kernel,
        grid=(1,),
        in_specs=specs,
        out_specs=[pl.BlockSpec(shape.shape, functools.partial(lambda n, i: (0,) * n, len(shape.shape))) for shape in shapes],
        out_shape=shapes,
        scratch_shapes=list(scratch),
        compiler_params=pltpu.CompilerParams(vmem_limit_bytes=VMEM_BYTES),
        cost_estimate=pl.CostEstimate(flops=flops, bytes_accessed=2 * size, transcendentals=0),
        name=kernel.__name__,
    )(*args)


def whole(array):
    return pl.BlockSpec(array.shape, lambda *unused: (0,) * array.ndim)


def flip(array, axis, bit):
    size = lax.axis_size(axis)
    return lax.ppermute(array, axis, [(at, at ^ bit) for at in range(size)])


def halve(kept, got, axis, bit, place):
    mine = (lax.axis_index(axis) >> bit) & 1
    halves = []
    for at in (1 - mine, mine):
        halves.append(
            lax.dynamic_index_in_dim(kept, at, place, keepdims=False)
            + lax.dynamic_index_in_dim(got, at, place, keepdims=False)
        )
    return halves


def row_steps(kept, sent, bits, rows):
    columns = kept.shape[-1]
    got = flip(sent, "dp", 1 << bits[0])
    for bit in bits[1:]:
        shape = (-1, 2, rows, columns)
        sent, kept = halve(kept.reshape(shape), got.reshape(shape), "dp", bit, 1)
        got = flip(sent, "dp", 1 << bit)
    return kept.reshape(rows, columns), got.reshape(rows, columns)


def columns_first(kept, sent):
    n_dp = lax.axis_size("dp")
    rows = kept.shape[0] // n_dp
    columns = kept.shape[1]
    got = flip(sent, "seq", 2)
    shape = (-1, 2, rows, columns)
    sent, kept = halve(kept.reshape(shape), got.reshape(shape), "dp", 0, 1)
    kept, got = row_steps(kept, sent, list(range(n_dp.bit_length() - 1)), rows)
    return kept.astype(F32) + got.astype(F32)


def rows_first(kept, sent):
    n_dp = lax.axis_size("dp")
    rows, columns = kept.shape[1], kept.shape[2]
    kept, got = row_steps(kept, sent, list(range(n_dp.bit_length() - 1)), rows)
    shape = (rows, 2, columns // 2)
    sent, kept = halve(kept.reshape(shape), got.reshape(shape), "seq", 1, 1)
    got = flip(sent, "seq", 2)
    return kept.astype(F32) + got.astype(F32)


def local(
    x_short, x_long, len_short, len_long, w_qkv, w_out, w_up, w_down, pos_table, norm_gain, norm_bias, cot_short, cot_long
):
    n_dp = lax.axis_size("dp")
    me = lax.axis_index("seq")
    live = jnp.where(me < 2, len_long[0], len_short[jnp.maximum(me - 2, 0)])
    info = jnp.stack([me, live, lax.axis_index("dp") & 1]).astype(jnp.int32)
    width = x_short.shape[2]
    size = x_short.shape[1]
    tokens = 4 * size
    half = tokens // 2
    inner = w_up.shape[2]
    pairs = width // (2 * HD)
    part = ((size, width), BF16)

    def gather(parts):
        return [parts[0]] + [flip(parts[delta], "seq", delta) for delta in (1, 2, 3)]

    def near(array):
        return flip(array, "seq", 1)

    pieces = call(
        split_kernel, [part] * 8, [SMEM] + [whole(a) for a in (x_short, x_long, cot_short, cot_long)],
        (info, x_short, x_long, cot_short, cot_long),
    )
    rows_in = gather(pieces[:4])
    cot_in = gather(pieces[4:])
    hidden_kind = ((tokens, width), F32)
    low_kind = ((tokens, width), BF16)
    kv_kind = ((tokens, 2 * width), BF16)
    hidden0, rounded0, query0, kv0 = call(
        front_kernel, [hidden_kind, low_kind, low_kind, kv_kind],
        [SMEM] + [whole(a) for a in rows_in] + [one(pos_table, 0), one(w_qkv, 0)],
        (info, *rows_in, pos_table, w_qkv),
    )
    probs_kinds = [((pairs, 2 * half, 2 * half), BF16), ((pairs, 4 * half, 2 * half), BF16)]
    slope_kind = ((tokens, inner), BF16)
    x_kind = ((tokens, inner + 3 * width), BF16)
    units_kind = ((2, tokens, width), F32)
    scales_kind = ((2, tokens, 1), F32)
    biases = [pltpu.VMEM((2 * half, half), F32), pltpu.VMEM((4 * half, half), F32)]
    weights = [pltpu.VMEM(w_out.shape[1:], BF16), pltpu.VMEM(w_up.shape[1:], BF16), pltpu.VMEM(w_down.shape[1:], BF16)]
    kv0_far = near(kv0)
    ins = (query0, kv0, kv0_far, hidden0, rounded0, pos_table, norm_gain, norm_bias)
    probs_near0, probs_far0, slope0, x0, units0, scales0, hidden1, rounded1, query1, kv1 = call(
        first_kernel,
        probs_kinds + [slope_kind, x_kind, units_kind, scales_kind, hidden_kind, low_kind, low_kind, kv_kind],
        [SMEM] + [whole(a) for a in ins] + [ANY] * 4,
        (info, *ins, w_qkv, w_out, w_up, w_down),
        biases + weights + [pltpu.VMEM(w_qkv.shape[1:], BF16), pltpu.SemaphoreType.DMA((4,))],
    )
    kv1_far = near(kv1)
    x0_far = near(x0)
    bx_kind = ((2, tokens, inner // 4 + width // 2), BF16)
    grads_kind = ((4, width), F32)
    ins = (query1, kv1, kv1_far, hidden1, rounded1, *cot_in, norm_gain, norm_bias)
    outs = call(
        second_kernel,
        probs_kinds + [x_kind] + [part] * 4 + [bx_kind, bx_kind, grads_kind, hidden_kind, low_kind],
        [SMEM] + [whole(a) for a in ins] + [ANY] * 3,
        (info, *ins, w_out, w_up, w_down),
        biases
        + [pltpu.VMEM(*units_kind), pltpu.VMEM(*scales_kind), pltpu.VMEM(*slope_kind), pltpu.VMEM(*hidden_kind), pltpu.VMEM(*low_kind)]
        + weights
        + [pltpu.SemaphoreType.DMA((3,))],
    )
    probs_near1, probs_far1, x1 = outs[:3]
    acts = outs[3:7]
    bx1, bx1_sent, norms1, d_first1, d_att1 = outs[7:]
    x1_far = near(x1)
    bx1_far = near(bx1_sent)
    act_parts = gather(acts)

    def attend_back(query, kv, kv_far, probs_near, probs_far, d_att):
        ins = (query, kv, kv_far, probs_near, probs_far, d_att)
        return call(attend_back_kernel, [low_kind, kv_kind, kv_kind], [whole(a) for a in ins], ins)

    d_query1, d_kv1, d_kv1_sent = attend_back(query1, kv1, kv1_far, probs_near1, probs_far1, d_att1)
    d_kv1_far = near(d_kv1_sent)

    def feed_grad(x_near, x_far, b_near, b_far):
        ins = (x_near, x_far, b_near, b_far)
        up_kind = ((width, inner // 4), BF16)
        down_kind = ((n_dp // 2, inner // n_dp, width // 2), BF16)
        outs = call(
            feed_grad_kernel, [up_kind, up_kind, down_kind, down_kind], [SMEM] + [whole(a) for a in ins], (info, *ins),
            [pltpu.VMEM((inner, width // 2), BF16)],
        )
        return columns_first(outs[0], outs[1]), rows_first(outs[2], outs[3])

    def attend_grad(x_near, x_far, b_near, b_far, q_near, q_far):
        ins = (x_near, x_far, b_near, b_far, q_near, q_far)
        kind = ((width, width + width // 4), BF16)
        outs = call(
            attend_grad_kernel, [kind, kind], [SMEM] + [whole(a) for a in ins], (info, *ins),
            [pltpu.VMEM((width, width // 4), F32)],
        )
        total = columns_first(*outs)
        edge = 3 * width // 4
        return total[:, :edge], total[:, edge : edge + width // 4], total[:, edge + width // 4 :]

    g_up1, g_down1 = feed_grad(x1, x1_far, bx1, bx1_far)
    qx_kind = ((2, tokens, width), BF16)
    ins = (d_query1, d_kv1, d_kv1_far, d_first1)
    tail_ins = (norm_gain, slope0, units0, scales0)
    qx1, qx1_sent, bx0, bx0_sent, norms0, d_first0, d_att0 = call(
        middle_kernel, [qx_kind, qx_kind, bx_kind, bx_kind, grads_kind, hidden_kind, low_kind],
        [SMEM] + [whole(a) for a in ins] + [one(w_qkv, 1)] + [whole(a) for a in tail_ins] + [ANY] * 3,
        (info, *ins, w_qkv, *tail_ins, w_out, w_up, w_down),
        weights + [pltpu.SemaphoreType.DMA((3,))],
    )
    qx1_far, bx0_far = near(qx1_sent), near(bx0_sent)
    d_query0, d_kv0, d_kv0_sent = attend_back(query0, kv0, kv0_far, probs_near0, probs_far0, d_att0)
    d_kv0_far = near(d_kv0_sent)
    g_qkv1, g_out1, g_pos1 = attend_grad(x1, x1_far, bx1, bx1_far, qx1, qx1_far)
    g_up0, g_down0 = feed_grad(x0, x0_far, bx0, bx0_far)
    ins = (d_query0, d_kv0, d_kv0_far, d_first0)
    outs = call(
        last_kernel, [qx_kind, qx_kind] + [part] * 4,
        [SMEM] + [whole(a) for a in ins] + [one(w_qkv, 0)],
        (info, *ins, w_qkv), [pltpu.VMEM(*low_kind)],
    )
    qx0, qx0_sent = outs[:2]
    qx0_far = near(qx0_sent)
    in_parts = gather(outs[2:])
    g_qkv0, g_out0, g_pos0 = attend_grad(x0, x0_far, bx0, bx0_far, qx0, qx0_far)

    def join(parts):
        return call(
            join_kernel, [(x_short.shape, BF16), (x_long.shape, BF16)], [SMEM] + [whole(a) for a in parts], (info, *parts)
        )

    act_short, act_long = join(act_parts)
    grad_short, grad_long = join(in_parts)
    norms = jnp.concatenate([norms0, norms1], axis=0)
    norms = norms + flip(norms, "seq", 1)
    norms = norms + flip(norms, "seq", 2)
    share = width // n_dp
    blocks = norms.reshape(8, n_dp, share).transpose(1, 0, 2)
    for bit in range(n_dp.bit_length() - 1):
        blocks = blocks.reshape((-1, 2, 8, share))
        mine = (lax.axis_index("dp") >> bit) & 1
        sent = lax.dynamic_index_in_dim(blocks, 1 - mine, 1, keepdims=False)
        blocks = lax.dynamic_index_in_dim(blocks, mine, 1, keepdims=False) + flip(sent, "dp", 1 << bit)
    blocks = blocks.reshape(2, 2, 2, share)
    return (
        act_short, act_long, grad_short, grad_long,
        jnp.stack([g_qkv0, g_qkv1]), jnp.stack([g_out0, g_out1]), jnp.stack([g_up0, g_up1]),
        jnp.stack([g_down0, g_down1]), jnp.stack([g_pos0, g_pos1]), blocks[:, 0], blocks[:, 1],
    )


def solution(mesh):
    rows = P("dp", "seq", None)
    grads = P(None, "dp", "seq")
    norms = P(None, None, "dp")
    return jax.shard_map(
        local,
        mesh=mesh,
        in_specs=(rows, rows, P("dp"), P("dp")) + (P(),) * 7 + (rows, rows),
        out_specs=(rows,) * 4 + (grads,) * 5 + (norms, norms),
        check_vma=False,
    )
```

```python
import functools

import jax
import jax.numpy as jnp
from jax import lax
from jax.experimental import pallas as pl
from jax.experimental.pallas import tpu as pltpu
from jax.sharding import PartitionSpec as P

LAYERS = 2
HD = 64
F32 = jnp.float32
BF16 = jnp.bfloat16
NEG = -1000000000.0


def dot(left, right):
    return lax.dot_general(left, right, (((1,), (0,)), ((), ())), preferred_element_type=F32)


def dot_nt(left, right):
    return lax.dot_general(left, right, (((1,), (1,)), ((), ())), preferred_element_type=F32)


def dot_tn(left, right):
    return lax.dot_general(left, right, (((0,), (0,)), ((), ())), preferred_element_type=F32)


ME, LIVE, DP = 0, 1, 2


def aligned(value, step):
    return pl.multiple_of(value, step)


def block_start(info, block, core, size):
    is_long = info[ME] < 2
    return aligned(jnp.where(is_long, (2 * block + core) * size, block * size), size)


def norm_forward(values, gain, shift):
    centre = jnp.mean(values, axis=-1, keepdims=True)
    centred = values - centre
    spread = jnp.mean(centred * centred, axis=-1, keepdims=True)
    scale = lax.rsqrt(spread + 1e-05)
    unit = centred * scale
    return unit, scale, unit * gain + shift


def norm_backward(unit, scale, gain, gradient):
    d_gain = jnp.sum(gradient * unit, axis=0, keepdims=True)
    d_shift = jnp.sum(gradient, axis=0, keepdims=True)
    scaled = gradient * gain
    mean_one = jnp.mean(scaled, axis=-1, keepdims=True)
    mean_two = jnp.mean(scaled * unit, axis=-1, keepdims=True)
    return scale * (scaled - mean_one - unit * mean_two), d_gain, d_shift


def positions(info, rows, core, size):
    is_long = info[ME] < 2
    spread = (rows // size) * (2 * size) + core * size + rows % size
    return jnp.where(is_long, spread, rows)


def fill_bias(info, bias_near, bias_far, size):
    core = info[ME] % 2
    is_long = info[ME] < 2
    half = bias_near.shape[1]
    for at, ref in ((0, bias_near), (1, bias_far)):
        queries = positions(info, lax.broadcasted_iota(jnp.int32, (half, half), 1) + at * half, core, size)
        for part in range(2 * (at + 1)):
            rows = lax.broadcasted_iota(jnp.int32, (half, half), 0) + (part // 2) * half
            if part % 2 == 0:
                keys = positions(info, rows, core, size)
            else:
                keys = jnp.where(is_long, positions(info, rows, 1 - core, size), 1 << 20)
            allowed = (keys <= queries) & (keys < info[LIVE])
            ref[pl.ds(part * half, half), :] = jnp.where(allowed, 0.0, NEG)


def interleave(near, far, columns, half):
    return jnp.concatenate(
        [near[:half, columns], far[:half, columns], near[half:, columns], far[half:, columns]], axis=0
    )


def lane_masks(half):
    lanes = lax.broadcasted_iota(jnp.int32, (half, 2 * HD), 1)
    first = jnp.where(lanes < HD, 1.0, 0.0).astype(BF16)
    return first, (1.0 - first.astype(F32)).astype(BF16)


def both_heads(rows, masks):
    return jnp.concatenate([rows * masks[0], rows * masks[1]], axis=0)


def attend_forward(query, kv_near, kv_far, bias_near, bias_far, probs_near, probs_far, attended):
    width = query.shape[1]
    half = query.shape[0] // 2
    masks = lane_masks(half)

    def scores_of(pair, at):
        columns = slice(pair * 2 * HD, (pair + 1) * 2 * HD)
        bias = (bias_near, bias_far)[at]
        keys = interleave(kv_near, kv_far, columns, half)
        pair_query = both_heads(query[pl.ds(at * half, half), columns], masks)
        return dot_nt(keys[: bias.shape[0]], pair_query) + jnp.concatenate([bias[...], bias[...]], axis=1)

    def finish(pair, at, softened):
        columns = slice(pair * 2 * HD, (pair + 1) * 2 * HD)
        values = interleave(kv_near, kv_far, slice(columns.start + width, columns.stop + width), half)
        turned = dot_tn(values[: softened.shape[0]], softened)
        turned = jnp.concatenate([turned[:HD, :half], turned[HD:, half:]], axis=0)
        attended[pl.ds(at * half, half), columns] = turned.T.astype(BF16)

    units = [(pair, at) for pair in range(width // (2 * HD)) for at in range(2)]
    ready = scores_of(*units[0])
    waiting = None
    for index, (pair, at) in enumerate(units):
        scores = ready
        if index + 1 < len(units):
            ready = scores_of(*units[index + 1])
        if waiting is not None:
            finish(*waiting)
        peak = jnp.max(scores, axis=0, keepdims=True)
        lifted = jnp.exp(scores - peak)
        total = jnp.sum(lifted, axis=0, keepdims=True)
        softened = (lifted * (1.0 / total)).astype(BF16)
        (probs_near, probs_far)[at][pair] = softened
        waiting = (pair, at, softened)
    finish(*waiting)


def attend_backward(query, kv_near, kv_far, probs_near, probs_far, d_att, d_query, d_kv_near, d_kv_far):
    width = query.shape[1]
    half = query.shape[0] // 2
    masks = lane_masks(half)

    def d_probs_of(pair, at):
        columns = slice(pair * 2 * HD, (pair + 1) * 2 * HD)
        values = interleave(kv_near, kv_far, slice(columns.start + width, columns.stop + width), half)
        pair_grad = both_heads(d_att[pl.ds(at * half, half), columns], masks)
        return pair_grad, dot_nt(values[: (probs_near, probs_far)[at].shape[1]], pair_grad)

    def finish(pair, at, pair_grad, softened, d_scores):
        columns = slice(pair * 2 * HD, (pair + 1) * 2 * HD)
        keys = interleave(kv_near, kv_far, columns, half)
        pair_query = both_heads(query[pl.ds(at * half, half), columns], masks)
        parts[at] = (dot(d_scores, pair_query), dot(softened, pair_grad))
        turned = dot_tn(keys[: softened.shape[0]], d_scores)
        turned = jnp.concatenate([turned[:HD, :half], turned[HD:, half:]], axis=0)
        d_query[pl.ds(at * half, half), columns] = (turned.T * (1.0 / HD**0.5)).astype(BF16)
        if at == 1:
            for kind, start in ((0, columns.start), (1, columns.start + width)):
                place = slice(start, start + 2 * HD)
                first = (parts[0][kind] + parts[1][kind][: 2 * half]).astype(BF16)
                second = parts[1][kind][2 * half :].astype(BF16)
                d_kv_near[:half, place] = first[:half]
                d_kv_far[:half, place] = first[half:]
                d_kv_near[half:, place] = second[:half]
                d_kv_far[half:, place] = second[half:]

    units = [(pair, at) for pair in range(width // (2 * HD)) for at in range(2)]
    parts = {}
    ready = d_probs_of(*units[0])
    waiting = None
    for index, (pair, at) in enumerate(units):
        pair_grad, d_probs = ready
        if index + 1 < len(units):
            ready = d_probs_of(*units[index + 1])
        if waiting is not None:
            finish(*waiting)
        softened = (probs_near, probs_far)[at][pair]
        probs = softened.astype(F32)
        row_sum = jnp.sum(probs * d_probs, axis=0, keepdims=True)
        waiting = (pair, at, pair_grad, softened, (probs * (d_probs - row_sum)).astype(BF16))
    finish(*waiting)


def project(rounded, w_qkv, query, kv):
    width = query.shape[1]
    for at in range(3):
        mixed = dot(rounded, w_qkv[:, at * width : (at + 1) * width]).astype(BF16)
        if at == 0:
            query[...] = mixed * jnp.asarray(1.0 / HD**0.5, BF16)
        else:
            kv[:, (at - 1) * width : at * width] = mixed


def normal_area(value):
    area = 0.5 + 0.5 * lax.erf(value * (0.5**0.5))
    bell = jnp.exp(value * value * -0.5) * ((2.0 * jnp.pi) ** -0.5)
    return area, bell


def tail_forward(hidden, attended, w_out, w_up, w_down, gains, shifts, active, slope, settled_low, units, scales):
    inner_width = w_up.shape[1]
    step = 512
    pre_first = hidden[...] + dot(attended[...], w_out[...])
    unit, scale, settled = norm_forward(pre_first, gains[0], shifts[0])
    units[0], scales[0] = unit, scale
    rounded = settled.astype(BF16)
    settled_low[...] = rounded
    second = settled
    count = inner_width // step
    ready = dot(rounded, w_up[:, :step])
    for at in range(count):
        span = slice(at * step, (at + 1) * step)
        inner = ready
        if at + 1 < count:
            ready = dot(rounded, w_up[:, (at + 1) * step : (at + 2) * step])
        area, bell = normal_area(inner)
        glow = (inner * area).astype(BF16)
        active[:, span] = glow
        slope[:, span] = (area + inner * bell).astype(BF16)
        second = second + dot(glow, w_down[span, :])
    unit, scale, result = norm_forward(second, gains[1], shifts[1])
    units[1], scales[1] = unit, scale
    return result


def tail_backward(info, gradient, w_out, w_up, w_down, gains, slope, units, scales, kept, sent, norm_grads, d_first_out, d_att):
    inner_width = w_up.shape[1]
    width = w_up.shape[0]
    shards = 4
    step, part = inner_width // shards, width // shards
    core = info[ME] % 2
    d_second, d_gain, d_shift = norm_backward(units[1], scales[1], gains[1], gradient)
    norm_grads[1:2, :] = d_gain
    norm_grads[3:4, :] = d_shift
    d_feed = d_second.astype(BF16)
    d_settled = d_second

    def place(at, columns, value):
        @pl.when(at % 2 == core)
        def _():
            kept[at // 2, :, columns] = value

        @pl.when(at % 2 != core)
        def _():
            sent[at // 2, :, columns] = value

    ready = dot_nt(d_feed, w_down[:step, :])
    for at in range(shards):
        span = slice(at * step, (at + 1) * step)
        d_active = ready
        if at + 1 < shards:
            ready = dot_nt(d_feed, w_down[(at + 1) * step : (at + 2) * step, :])
        d_inner = (d_active * slope[:, span].astype(F32)).astype(BF16)
        place(at, slice(0, step), d_inner)
        place(at, slice(step, step + part), d_feed[:, at * part : (at + 1) * part])
        d_settled = d_settled + dot_nt(d_inner, w_up[:, span])
    d_first, d_gain, d_shift = norm_backward(units[0], scales[0], gains[0], d_settled)
    norm_grads[0:1, :] = d_gain
    norm_grads[2:3, :] = d_shift
    d_first_out[...] = d_first
    d_branch = d_first.astype(BF16)
    for at in range(shards):
        place(at, slice(step + part, step + 2 * part), d_branch[:, at * part : (at + 1) * part])
    d_att[...] = dot_nt(d_branch, w_out[...]).astype(BF16)


def add_table(info, table, layer_at, get_rows, hidden):
    core = info[ME] % 2
    size = hidden.shape[0] // 4
    for block in range(4):
        start = block_start(info, block, core, size)
        rows = table[layer_at, pl.ds(start, size), :].astype(F32)
        hidden[block * size : (block + 1) * size, :] = get_rows(block) + rows


def split_rows(info, short, long, parts, sems):
    size = parts[0].shape[0]
    waits = []
    for delta, part in enumerate(parts):
        target = info[ME] ^ delta
        from_long = pltpu.make_async_copy(
            long.at[0, pl.ds(aligned(jnp.minimum(target, 1) * size, size), size), :], part, sems.at[delta]
        )
        from_short = pltpu.make_async_copy(short.at[jnp.maximum(target - 2, 0)], part, sems.at[delta])
        pl.when(target < 2)(from_long.start)
        pl.when(target >= 2)(from_short.start)
        waits.append(from_long.wait)
    return waits


def split_kernel(info, x_short, x_long, *refs):
    for wait in split_rows(info, x_short, x_long, refs[:-1], refs[-1]):
        wait()


def fetch(pairs, sems, parts):
    waits = []
    for source, target in pairs:
        step = target.shape[0] // parts
        for part in range(parts):
            rows = pl.ds(part * step, step)
            copy = pltpu.make_async_copy(source.at[rows], target.at[rows], sems.at[len(waits)])
            copy.start()
            waits.append(copy.wait)
    return waits


def load_kernel(info, table, w_qkv, w_out, w_up, w_down, *refs):
    sources = (table.at[0], table.at[1], w_qkv.at[0], w_out.at[0], w_up.at[0], w_down.at[0])
    targets = (refs[0].at[0], refs[0].at[1], *refs[1:5])
    for wait in fetch(zip(sources, targets), refs[5], 4):
        wait()


def load_late_kernel(info, w_one, w_two, one, two, sems):
    for wait in fetch(((w_one.at[1], one), (w_two.at[1], two)), sems, 4):
        wait()


def load_and_split_kernel(info, w_one, w_two, cot_short, cot_long, one, two, c0, c1, c2, c3, sems, split_sems):
    waits = split_rows(info, cot_short, cot_long, (c0, c1, c2, c3), split_sems)
    for wait in waits + fetch(((w_one.at[1], one), (w_two.at[1], two)), sems, 4):
        wait()


def pack_kernel(info, act, grad, *parts):
    size = parts[0].shape[0] // 2
    for delta, part in enumerate(parts):
        rows = pl.ds(aligned((info[ME] ^ delta) * size, size), size)
        part[:size, :] = act[rows, :]
        part[size:, :] = grad[rows, :]


def join_kernel(info, p0, p1, p2, p3, act_short, act_long, grad_short, grad_long):
    size = p0.shape[0] // 2
    for delta, part in enumerate((p0, p1, p2, p3)):
        source = info[ME] ^ delta
        for short, long, rows in ((act_short, act_long, slice(0, size)), (grad_short, grad_long, slice(size, 2 * size))):

            @pl.when(source < 2)
            def _():
                long[0, pl.ds(aligned(jnp.minimum(source, 1) * size, size), size), :] = part[rows, :]

            @pl.when(source >= 2)
            def _():
                short[jnp.maximum(source - 2, 0)] = part[rows, :]


def front_kernel(info, r0, r1, r2, r3, table, w_qkv, hidden, rounded, query, kv):
    size = r0.shape[0]
    core = info[ME] % 2
    for delta, ref in enumerate((r0, r1, r2, r3)):
        block = info[ME] ^ delta
        start = block_start(info, block, core, size)
        rows = ref[...].astype(F32) + table[0, pl.ds(start, size), :].astype(F32)
        hidden[pl.ds(aligned(block * size, size), size), :] = rows
    low = hidden[...].astype(BF16)
    rounded[...] = low
    project(low, w_qkv, query, kv)


def with_live(info, len_short, len_long):
    me = info[ME]
    live = jnp.where(me < 2, len_long[0], len_short[jnp.maximum(me - 2, 0)])
    return (me, live, info[DP])


def first_kernel(
    info, len_short, len_long, query, kv_near, kv_far, hidden, rounded, table, gains, shifts, w_out, w_up, w_down, w_next,
    probs_near, probs_far, slope, kept_x, units, scales, hidden_next, rounded_next, query_next, kv_next,
    bias_near, bias_far,
):
    width, inner = w_up.shape
    size = query.shape[0] // 4
    info = with_live(info, len_short, len_long)
    fill_bias(info, bias_near, bias_far, size)
    attended = kept_x.at[:, inner + width : inner + 2 * width]
    attend_forward(query, kv_near, kv_far, bias_near, bias_far, probs_near, probs_far, attended)
    kept_x[:, inner + 2 * width :] = rounded[...]
    result = tail_forward(
        hidden, attended, w_out, w_up, w_down, gains[0], shifts[0],
        kept_x.at[:, :inner], slope, kept_x.at[:, inner : inner + width], units, scales,
    ).astype(BF16).astype(F32)
    add_table(info, table, 1, lambda block: result[block * size : (block + 1) * size], hidden_next)
    low = hidden_next[...].astype(BF16)
    rounded_next[...] = low
    project(low, w_next, query_next, kv_next)


def second_kernel(
    info, len_short, len_long, query, kv_near, kv_far, hidden, rounded, gains, shifts, w_out, w_up, w_down,
    probs_near, probs_far, slope, kept_x, units, scales, result, bias_near, bias_far,
):
    width, inner = w_up.shape
    info = with_live(info, len_short, len_long)
    fill_bias(info, bias_near, bias_far, query.shape[0] // 4)
    attended = kept_x.at[:, inner + width : inner + 2 * width]
    attend_forward(query, kv_near, kv_far, bias_near, bias_far, probs_near, probs_far, attended)
    kept_x[:, inner + 2 * width :] = rounded[...]
    result[...] = tail_forward(
        hidden, attended, w_out, w_up, w_down, gains[1], shifts[1],
        kept_x.at[:, :inner], slope, kept_x.at[:, inner : inner + width], units, scales,
    ).astype(BF16)


def turn_kernel(
    info, c0, c1, c2, c3, gains, slope, units, scales, w_out, w_up, w_down,
    bx_kept, bx_sent, norm_grads, d_first, d_att, cot,
):
    size = c0.shape[0]
    for delta, cot_part in enumerate((c0, c1, c2, c3)):
        rows = pl.ds(aligned((info[ME] ^ delta) * size, size), size)
        cot[rows, :] = cot_part[...].astype(F32)
    tail_backward(
        info, cot[...], w_out, w_up, w_down, gains[1], slope, units, scales,
        bx_kept, bx_sent, norm_grads, d_first, d_att,
    )


def attend_back_kernel(unused, query, kv_near, kv_far, probs_near, probs_far, d_att, d_query, d_kv_near, d_kv_far):
    attend_backward(query, kv_near, kv_far, probs_near, probs_far, d_att, d_query, d_kv_near, d_kv_far)


def close_layer(info, d_query, d_kv, d_kv_far, d_first, w_qkv, kept, sent, skip=0):
    shards = 4
    width = d_query.shape[1]
    core = info[ME] % 2
    total = (d_kv[...].astype(F32) + d_kv_far[...].astype(F32)).astype(BF16)
    d_qkv = jnp.concatenate([d_query[...], total], axis=1)
    d_hidden = d_first[...] + dot_nt(d_qkv, w_qkv[...])
    low = d_hidden.astype(BF16)
    step, part = 3 * width // shards, width // shards
    for at in range(shards):
        pieces = (
            (slice(skip, skip + step), d_qkv[:, at * step : (at + 1) * step]),
            (slice(skip + step, skip + step + part), low[:, at * part : (at + 1) * part]),
        )

        @pl.when(at % 2 == core)
        def _():
            for columns, value in pieces:
                kept[at // 2, :, columns] = value

        @pl.when(at % 2 != core)
        def _():
            for columns, value in pieces:
                sent[at // 2, : value.shape[0], columns] = value

    return d_hidden, low


def middle_kernel(
    info, d_query, d_kv, d_kv_far, d_first, w_qkv, gains, slope, units, scales, w_out, w_up, w_down, norms_late,
    qx_kept, qx_sent, bx_kept, bx_sent, norm_grads, d_first_out, d_att,
):
    d_hidden, unused = close_layer(info, d_query, d_kv, d_kv_far, d_first, w_qkv, qx_kept, qx_sent)
    norm_grads[4:, :] = norms_late[...]
    tail_backward(
        info, d_hidden, w_out, w_up, w_down, gains[0], slope, units, scales,
        bx_kept, bx_sent, norm_grads, d_first_out, d_att,
    )


def last_kernel(info, d_query, d_kv, d_kv_far, d_first, w_qkv, norms, qx_kept, qx_sent, grad):
    unused, low = close_layer(info, d_query, d_kv, d_kv_far, d_first, w_qkv, qx_kept, qx_sent)
    grad[...] = low
    tokens = d_query.shape[0]
    padded = jnp.concatenate([norms[...], jnp.zeros(norms.shape, F32)], axis=0)
    qx_sent[0, tokens:, :] = padded.astype(BF16)
    qx_sent[1, tokens:, :] = jnp.zeros(padded.shape, BF16)


def split_blocks(info, places, whole_ref, kept, sent):
    def split(place):
        bit, axis, at = place
        mine = (info[axis] >> at) & 1
        for ref, value in ((sent, 1 - mine), (kept, mine)):
            for index in range(ref.shape[0]):
                low = index & ((1 << bit) - 1)
                source = ((index >> bit) << (bit + 1)) + low + (value << bit)
                total = whole_ref[0][source]
                for other in whole_ref[1:]:
                    total = total + other[source]
                ref[index] = total

    if places[0] == places[1]:
        split(places[0])
    else:
        for core in range(2):
            pl.when(info[ME] % 2 == core)(functools.partial(split, places[core]))


def fold_kernel(places, info, kept, got, new_kept, new_sent):
    split_blocks(info, places, (kept, got), new_kept, new_sent)


def put(pieces, whole, name, x, value):
    for at, (tiles, unused) in enumerate(pieces):
        if name in tiles:
            lanes = value.shape[2]
            start = tiles.index(name) * lanes
            n_dp = value.shape[0]
            whole[at][x * n_dp : (x + 1) * n_dp, :, start : start + lanes] = value.astype(BF16)


def by_blocks(value, n_dp):
    return value.reshape(n_dp, value.shape[0] // n_dp, value.shape[1])


def feed_grad_kernel(pieces, info, x_near, x_far, b_near, b_far, *refs):
    count = len(pieces)
    outs, whole = refs[: 2 * count], refs[2 * count :]
    n_dp, rows = outs[0].shape[0], outs[0].shape[1]
    width = n_dp * rows
    inner = x_near.shape[1] - 3 * width
    step, part = inner // 4, width // 4
    for x in range(2):
        total = dot_tn(x_near[:, inner : inner + width], b_near[x, :, :step])
        total = total + dot_tn(x_far[:, inner : inner + width], b_far[x, :, :step])
        for tile in range(step // part):
            put(pieces, whole, ("up", tile), x, by_blocks(total[:, tile * part : (tile + 1) * part], n_dp))
    feeds = [
        jnp.concatenate([ref[0, :, step : step + part], ref[1, :, step : step + part]], axis=1)
        for ref in (b_near, b_far)
    ]
    span_size = 512
    fold = inner // width
    for at in range(inner // span_size):
        span = slice(at * span_size, (at + 1) * span_size)
        total = dot_tn(feeds[0], x_near[:, span]) + dot_tn(feeds[1], x_far[:, span])
        total = total.astype(BF16).T if rows % 16 == 0 else total.T
        for group in range(span_size // rows):
            block, tile = divmod(at * (span_size // rows) + group, fold)
            for index, (tiles, unused) in enumerate(pieces):
                if ("down", tile) in tiles:
                    start = tiles.index(("down", tile)) * part
                    for x in range(2):
                        value = total[group * rows : (group + 1) * rows, x * part : (x + 1) * part]
                        whole[index][x * n_dp + block, :, start : start + part] = value.astype(BF16)
    for at, (unused, places) in enumerate(pieces):
        split_blocks(info, places, (whole[at],), outs[2 * at], outs[2 * at + 1])


def attend_grad_kernel(pieces, with_norms, info, x_near, x_far, b_near, b_far, q_near, q_far, *refs):
    count = len(pieces)
    norms = None
    if with_norms:
        norms, refs = refs[0], refs[1:]
    outs, whole, table = refs[: 2 * count], refs[2 * count : -1], refs[-1]
    n_dp, rows = outs[0].shape[0], outs[0].shape[1]
    width = n_dp * rows
    part = width // 4
    tokens = x_near.shape[0]
    inner = x_near.shape[1] - 3 * width
    step = 3 * part
    feed = inner // 4 + part
    skip = q_near.shape[2] - width
    core = info[ME] % 2
    size = tokens // 4
    for x in range(2):
        lows = slice(inner + 2 * width, inner + 3 * width)
        total = dot_tn(x_near[:, lows], q_near[x, :, skip : skip + step])
        total = total + dot_tn(x_far[:, lows], q_far[x, :tokens, skip : skip + step])
        for tile in range(step // part):
            put(pieces, whole, ("qkv", tile), x, by_blocks(total[:, tile * part : (tile + 1) * part], n_dp))
        outs_at = slice(inner + width, inner + 2 * width)
        total = dot_tn(x_near[:, outs_at], b_near[x, :, feed : feed + part])
        total = total + dot_tn(x_far[:, outs_at], b_far[x, :, feed : feed + part])
        put(pieces, whole, ("out", 0), x, by_blocks(total, n_dp))
        table[...] = jnp.zeros_like(table)
        for source, place in ((q_near, core), (q_far, 1 - core)):
            for block in range(4):
                span = pl.ds(block_start(info, block, place, size), size)
                table[span, :] += source[x, block * size : (block + 1) * size, skip + step :].astype(F32)
        put(pieces, whole, ("pos", 0), x, by_blocks(table[...], n_dp))
    if with_norms:
        sums = norms[...] + q_far[0, tokens:, :].astype(F32)[: norms.shape[0]]
        share = width // n_dp
        for block in range(n_dp):
            value = sums[:, block * share : (block + 1) * share]
            value = jnp.concatenate([value, jnp.zeros((value.shape[0], part - share), F32)], axis=1)
            if rows > value.shape[0]:
                value = jnp.concatenate([value, jnp.zeros((rows - value.shape[0], part), F32)], axis=0)
            for at, (tiles, unused) in enumerate(pieces):
                if ("norm", 0) in tiles:
                    start = tiles.index(("norm", 0)) * part
                    for x in range(2):
                        whole[at][x * n_dp + block, :, start : start + part] = value.astype(BF16)
    for at, (unused, places) in enumerate(pieces):
        split_blocks(info, places, (whole[at],), outs[2 * at], outs[2 * at + 1])


def final_kernel(pieces, info, *refs):
    ins, (*sums, gain, shift) = refs[: 2 * len(pieces)], refs[2 * len(pieces) :]
    outs = dict(zip(("qkv", "out", "up", "down", "pos"), sums))
    for at, (layer_at, tiles) in enumerate(pieces):
        kept, got = ins[2 * at], ins[2 * at + 1]
        rows = kept.shape[1]
        part = outs["out"].shape[2]
        for index, (name, tile) in enumerate(tiles):
            lanes = slice(index * part, (index + 1) * part)
            total = kept[0, :, lanes].astype(F32) + got[0, :, lanes].astype(F32)
            if name == "norm":
                share = gain.shape[2]
                for row in range(8):
                    ref = (gain, shift)[row // 2 % 2]
                    ref[row // 4, row % 2 : row % 2 + 1, :] = total[row : row + 1, :share]
            elif name == "down":
                outs[name][layer_at, tile * rows : (tile + 1) * rows, :] = total
            else:
                outs[name][layer_at, :, tile * part : (tile + 1) * part] = total


MB = 1024 * 1024
TOKEN = ((8, 128), F32)
SMEM = pl.BlockSpec(memory_space=pltpu.SMEM)
VMEM = pl.BlockSpec(memory_space=pltpu.VMEM)
HBM = pl.BlockSpec(memory_space=pltpu.HBM)

FLOPS = 10**10
COSTS = dict(feed1=0, middle=0, back=0, rest1=0, feed0=0, last=0, rest0=0, fold=10000000000, pack=10000000000, tick=0)


def pin(array):
    return pltpu.with_memory_space_constraint(array, pltpu.VMEM)


class Line:
    def __init__(self):
        self.token = None
        self.trail = []
        self.used = set()

    def flip(self, array, axis, bit):
        size = lax.axis_size(axis)
        self.trail.append(lax.ppermute(array, axis, [(at, at ^ bit) for at in range(size)]))
        return self.trail[-1]

    def cross(self, array, steps):
        n_dp, n_seq = lax.axis_size("dp"), lax.axis_size("seq")
        pairs = []
        for dp in range(n_dp):
            for seq in range(n_seq):
                step = steps[seq % 2]
                other = (dp, seq ^ 2) if step == "x" else (dp ^ (1 << step), seq)
                pairs.append((dp * n_seq + seq, other[0] * n_seq + other[1]))
        self.trail.append(lax.ppermute(array, ("dp", "seq"), pairs))
        return self.trail[-1]

    def near(self, array):
        return self.flip(array, "seq", 1)

    def gather(self, parts):
        return [parts[0]] + [self.flip(parts[delta], "seq", delta) for delta in (1, 2, 3)]

    def past(self, used=True):
        return [array for array in self.trail if (id(array) in self.used) == used]

    def tick(self, after=()):
        self.call("tick", lambda info: None, [], (), after=after)

    def call(self, name, kernel, outs, args, scratch=(), limit=8, smem=0, hbm=0, final=False, after=(), past=()):
        self.used.update(id(arg) for arg in (*args, *after))
        tokens = [] if self.token is None else [self.token]
        skip = len(past)
        shapes = [jax.ShapeDtypeStruct(*kind) if final else pltpu.VMEM(*kind) for kind in outs] + [pltpu.VMEM(*TOKEN)]
        count, extra = len(args), len(tokens) + len(after)

        def body(*refs):
            refs = refs[skip:]
            given = refs[:count]
            made = refs[count + extra : count + extra + len(outs)]
            refs[count + extra + len(outs)][...] = jnp.zeros(TOKEN[0], F32)
            info = (lax.axis_index("seq"), None, lax.axis_index("dp"))
            kernel(info, *given, *made, *refs[count + extra + len(outs) + 1 :])

        far = smem + hbm
        operands = [pin(array) for array in past] + list(args[:smem]) + [pltpu.with_memory_space_constraint(arg, pltpu.HBM) for arg in args[smem:far]]
        operands += [pin(arg) for arg in args[far:]]
        operands += [pin(array) for array in (*after, *tokens)]
        results = pl.pallas_call(
            body,
            in_specs=[VMEM] * skip + [SMEM] * smem + [HBM] * hbm + [VMEM] * (count - far + extra),
            out_specs=[VMEM] * (len(outs) + 1),
            out_shape=shapes,
            scratch_shapes=list(scratch),
            compiler_params=pltpu.CompilerParams(vmem_limit_bytes=limit * MB),
            cost_estimate=pl.CostEstimate(flops=COSTS.get(name, FLOPS), bytes_accessed=0, transcendentals=0),
            name=name,
        )(*operands)
        self.token = results[-1]
        return list(results[:-1])


FEED = tuple(("up", at) for at in range(4)) + tuple(("down", at) for at in range(4))
REST = (("qkv", 0), ("qkv", 1), ("qkv", 2), ("out", 0), ("pos", 0))
LAST = REST + (("norm", 0),)
PIECES = dict(
    a=(1, "feed1", FEED, "yhxl", "lxhy"),
    b=(1, "rest1", REST, "lyxh", "xhyl"),
    c=(0, "feed0", FEED, "ylxh", "lyhx"),
    d=(0, "rest0", LAST, "yhxl", "xylh"),
)
ORDER = (
    "feed1", "middle", "back", "rest1", "feed0", "a", "last", "rest0", "b", "a", "c", "d", "pack", "take", "b", "c",
    "d", "a", "b", "d", "c",
)


class Sum:
    def __init__(self, name, n_bits):
        self.layer_at, self.maker, self.tiles, *paths = PIECES[name]
        letters = {"x": ["x"], "y": [0], "l": [1], "h": list(range(2, n_bits))}
        self.steps = [[bit for letter in path for bit in letters[letter] if bit == "x" or bit < n_bits] for path in paths]
        self.bits = [[*range(n_bits), "x"] for unused in paths]

    def left(self):
        return len(self.steps[0])

    def place(self):
        places = []
        for steps, bits in zip(self.steps, self.bits):
            where = bits.index(steps[0])
            places.append((where, ME, 1) if steps[0] == "x" else (where, DP, steps[0]))
        return places

    def start(self, line, kept, sent):
        now = [steps.pop(0) for steps in self.steps]
        for bits, step in zip(self.bits, now):
            bits.remove(step)
        self.kept = kept
        self.got = line.cross(sent, now)

    def fold(self, line):
        blocks, rows, columns = self.kept.shape
        kind = ((blocks // 2, rows, columns), BF16)
        self.start(line, *line.call("fold", functools.partial(fold_kernel, self.place()), [kind, kind], (self.kept, self.got)))


def local(
    x_short, x_long, len_short, len_long, w_qkv, w_out, w_up, w_down, pos_table, norm_gain, norm_bias, cot_short, cot_long
):
    n_dp = lax.axis_size("dp")
    n_bits = n_dp.bit_length() - 1
    width = x_short.shape[2]
    size = x_short.shape[1]
    tokens = 4 * size
    half = tokens // 2
    inner = w_up.shape[2]
    pairs = width // (2 * HD)
    rows = width // n_dp
    part = ((size, width), BF16)
    hidden_kind = ((tokens, width), F32)
    low_kind = ((tokens, width), BF16)
    kv_kind = ((tokens, 2 * width), BF16)
    probs_kinds = [((pairs, 2 * half, 2 * half), BF16), ((pairs, 4 * half, 2 * half), BF16)]
    slope_kind = ((tokens, inner), BF16)
    x_kind = ((tokens, inner + 3 * width), BF16)
    units_kind = ((2, tokens, width), F32)
    scales_kind = ((2, tokens, 1), F32)
    bx_kind = ((2, tokens, inner // 4 + width // 2), BF16)
    qx_kind = ((2, tokens, width), BF16)
    biases = [pltpu.VMEM((2 * half, half), F32), pltpu.VMEM((4 * half, half), F32)]
    lens = (len_short, len_long)
    line = Line()
    sums = {name: Sum(name, n_bits) for name in PIECES}

    four = [pltpu.SemaphoreType.DMA((4,))]
    rows_in = line.gather(line.call("split", split_kernel, [part] * 4, (x_short, x_long), four, hbm=2))
    stacks = (w_qkv, w_out, w_up, w_down)
    kinds = [(array.shape[1:], BF16) for array in stacks]
    table, w_qkv0, w_out0, w_up0, w_down0 = line.call(
        "load", load_kernel, [(pos_table.shape, BF16)] + kinds, (pos_table, *stacks), [pltpu.SemaphoreType.DMA((24,))], hbm=5
    )
    hidden0, rounded0, query0, kv0 = line.call(
        "front", front_kernel, [hidden_kind, low_kind, low_kind, kv_kind], (*rows_in, table, w_qkv0)
    )
    kv0_far = line.near(kv0)
    eight = [pltpu.SemaphoreType.DMA((8,))]
    w_qkv1, w_out1, *cots = line.call(
        "load", load_and_split_kernel, [kinds[0], kinds[1]] + [part] * 4, (w_qkv, w_out, cot_short, cot_long),
        eight + four, hbm=4,
    )
    layer_kinds = probs_kinds + [slope_kind, x_kind, units_kind, scales_kind]
    probs_near0, probs_far0, slope0, x0, units0, scales0, hidden1, rounded1, query1, kv1 = line.call(
        "first", first_kernel, layer_kinds + [hidden_kind, low_kind, low_kind, kv_kind],
        (
            *lens, query0, kv0, kv0_far, hidden0, rounded0, table, norm_gain, norm_bias,
            w_out0, w_up0, w_down0, w_qkv1,
        ),
        biases, limit=16, smem=2,
    )
    kv1_far = line.near(kv1)
    cot_in = line.gather(cots)
    x0_far = line.near(x0)
    w_up1, w_down1 = line.call("load", load_late_kernel, [kinds[2], kinds[3]], (w_up, w_down), eight, hbm=2)
    probs_near1, probs_far1, slope1, x1, units1, scales1, act = line.call(
        "second", second_kernel, layer_kinds + [low_kind],
        (*lens, query1, kv1, kv1_far, hidden1, rounded1, norm_gain, norm_bias, w_out1, w_up1, w_down1),
        biases, limit=16, smem=2,
    )
    x1_far = line.near(x1)
    bx1, bx1_sent, norms1, d_first1, d_att1 = line.call(
        "turn", turn_kernel, [bx_kind, bx_kind, ((4, width), F32), hidden_kind, low_kind],
        (*cot_in, norm_gain, slope1, units1, scales1, w_out1, w_up1, w_down1), [pltpu.VMEM(*hidden_kind)],
    )
    bx1_far = line.near(bx1_sent)

    def grads(maker, kernel, args, scratch=()):
        made = [each for each in sums.values() if each.maker == maker]
        pieces = [(each.tiles, each.place()) for each in made]
        columns = [len(each.tiles) * (width // 4) for each in made]
        outs = line.call(
            maker, functools.partial(kernel, pieces),
            [((n_dp, rows, count), BF16) for count in columns for unused in range(2)],
            args, [pltpu.VMEM((2 * n_dp, rows, count), BF16) for count in columns] + list(scratch), limit=12,
        )
        for at, each in enumerate(made):
            each.start(line, outs[2 * at], outs[2 * at + 1])

    table = [pltpu.VMEM((width, width // 4), F32)]
    back_kinds = [low_kind, kv_kind, kv_kind]
    d_query1, d_kv1, d_kv1_sent = line.call(
        "attend_back", attend_back_kernel, back_kinds, (query1, kv1, kv1_far, probs_near1, probs_far1, d_att1), after=[x0_far]
    )
    d_kv1_far = line.near(d_kv1_sent)
    latest = None
    order = list(ORDER)
    while order or any(each.left() for each in sums.values()):
        if not order:
            order = [name for name, each in sums.items() if each.left()]
        task = order.pop(0)
        if task in sums:
            if sums[task].left():
                if task == latest:
                    line.tick()
                sums[task].fold(line)
                latest = task
        elif task == "tick":
            line.tick()
        elif task == "feed1":
            grads("feed1", feed_grad_kernel, (x1, x1_far, bx1, bx1_far))
        elif task == "middle":
            qx1, qx1_sent, bx0, bx0_sent, norms, d_first0, d_att0 = line.call(
                "middle", middle_kernel, [qx_kind, qx_kind, bx_kind, bx_kind, ((8, width), F32), hidden_kind, low_kind],
                (
                    d_query1, d_kv1, d_kv1_far, d_first1, w_qkv1, norm_gain, slope0, units0, scales0, w_out0, w_up0, w_down0,
                    norms1,
                ),
            )
            bx0_far = line.near(bx0_sent)
            qx1_far = line.near(qx1_sent)
        elif task == "back":
            d_query0, d_kv0, d_kv0_sent = line.call(
                "back", attend_back_kernel, back_kinds, (query0, kv0, kv0_far, probs_near0, probs_far0, d_att0)
            )
            d_kv0_far = line.near(d_kv0_sent)
        elif task == "rest1":
            grads(
                "rest1", lambda pieces, *refs: attend_grad_kernel(pieces, False, *refs),
                (x1, x1_far, bx1, bx1_far, qx1, qx1_far), table,
            )
        elif task == "feed0":
            grads("feed0", feed_grad_kernel, (x0, x0_far, bx0, bx0_far))
        elif task == "last":
            longer = ((2, tokens + 16, width), BF16)
            qx0, qx0_sent, grad = line.call(
                "last", last_kernel, [qx_kind, longer, low_kind], (d_query0, d_kv0, d_kv0_far, d_first0, w_qkv0, norms)
            )
            qx0_far = line.near(qx0_sent)
        elif task == "rest0":
            grads(
                "rest0", lambda pieces, *refs: attend_grad_kernel(pieces, True, *refs),
                (x0, x0_far, bx0, bx0_far, qx0, qx0_far, norms), table,
            )
        elif task == "pack":
            parts = line.gather(line.call("pack", pack_kernel, [((2 * size, width), BF16)] * 4, (act, grad)))
            latest = None
        elif task == "take":
            line.tick(after=parts)
    joined = line.call(
        "join", join_kernel, [(x_short.shape, BF16), (x_long.shape, BF16)] * 2, parts, final=True, past=line.past()
    )
    shard = ((LAYERS, rows, width // 4), F32)
    totals = line.call(
        "final", functools.partial(final_kernel, [(each.layer_at, each.tiles) for each in sums.values()]),
        [
            ((LAYERS, rows, 3 * width // 4), F32), shard, ((LAYERS, rows, inner // 4), F32),
            ((LAYERS, inner // n_dp, width // 4), F32), shard,
            ((LAYERS, 2, rows), F32), ((LAYERS, 2, rows), F32),
        ],
        [array for each in sums.values() for array in (each.kept, each.got)], final=True, past=line.past(False),
    )
    return (*joined, *totals)


def solution(mesh):
    rows = P("dp", "seq", None)
    grads = P(None, "dp", "seq")
    norms = P(None, None, "dp")
    return jax.shard_map(
        local,
        mesh=mesh,
        in_specs=(rows, rows, P("dp"), P("dp")) + (P(),) * 7 + (rows, rows),
        out_specs=(rows,) * 4 + (grads,) * 5 + (norms, norms),
        check_vma=False,
    )
```

```python
import functools

import jax
import jax.numpy as jnp
from jax import lax
from jax.experimental import pallas as pl
from jax.experimental.pallas import tpu as pltpu
from jax.sharding import PartitionSpec as P

LAYERS = 2
HD = 64
F32 = jnp.float32
BF16 = jnp.bfloat16
NEG = -1000000000.0


def dot(left, right):
    return lax.dot_general(left, right, (((1,), (0,)), ((), ())), preferred_element_type=F32)


def dot_nt(left, right):
    return lax.dot_general(left, right, (((1,), (1,)), ((), ())), preferred_element_type=F32)


def dot_tn(left, right):
    return lax.dot_general(left, right, (((0,), (0,)), ((), ())), preferred_element_type=F32)


ME, LIVE, DP = 0, 1, 2


def aligned(value, step):
    return pl.multiple_of(value, step)


def block_start(info, block, core, size):
    is_long = info[ME] < 2
    return aligned(jnp.where(is_long, (2 * block + core) * size, block * size), size)


def norm_forward(values, gain, shift):
    centre = jnp.mean(values, axis=-1, keepdims=True)
    centred = values - centre
    spread = jnp.mean(centred * centred, axis=-1, keepdims=True)
    scale = lax.rsqrt(spread + 1e-05)
    unit = centred * scale
    return unit, scale, unit * gain + shift


def norm_backward(unit, scale, gain, gradient):
    d_gain = jnp.sum(gradient * unit, axis=0, keepdims=True)
    d_shift = jnp.sum(gradient, axis=0, keepdims=True)
    scaled = gradient * gain
    mean_one = jnp.mean(scaled, axis=-1, keepdims=True)
    mean_two = jnp.mean(scaled * unit, axis=-1, keepdims=True)
    return scale * (scaled - mean_one - unit * mean_two), d_gain, d_shift


def positions(info, rows, core, size):
    is_long = info[ME] < 2
    spread = (rows // size) * (2 * size) + core * size + rows % size
    return jnp.where(is_long, spread, rows)


def fill_bias(info, bias_near, bias_far, size):
    core = info[ME] % 2
    is_long = info[ME] < 2
    half = bias_near.shape[1]
    for at, ref in ((0, bias_near), (1, bias_far)):
        queries = positions(info, lax.broadcasted_iota(jnp.int32, (half, half), 1) + at * half, core, size)
        for part in range(2 * (at + 1)):
            rows = lax.broadcasted_iota(jnp.int32, (half, half), 0) + (part // 2) * half
            if part % 2 == 0:
                keys = positions(info, rows, core, size)
            else:
                keys = jnp.where(is_long, positions(info, rows, 1 - core, size), 1 << 20)
            allowed = (keys <= queries) & (keys < info[LIVE])
            ref[pl.ds(part * half, half), :] = jnp.where(allowed, 0.0, NEG)


def interleave(near, far, columns, half):
    return jnp.concatenate(
        [near[:half, columns], far[:half, columns], near[half:, columns], far[half:, columns]], axis=0
    )


def lane_masks(half):
    lanes = lax.broadcasted_iota(jnp.int32, (half, 2 * HD), 1)
    first = jnp.where(lanes < HD, 1.0, 0.0).astype(BF16)
    return first, (1.0 - first.astype(F32)).astype(BF16)


def both_heads(rows, masks):
    return jnp.concatenate([rows * masks[0], rows * masks[1]], axis=0)


def attend_forward(query, kv_near, kv_far, bias_near, bias_far, probs_near, probs_far, attended):
    width = query.shape[1]
    half = query.shape[0] // 2
    masks = lane_masks(half)

    def scores_of(pair, at):
        columns = slice(pair * 2 * HD, (pair + 1) * 2 * HD)
        bias = (bias_near, bias_far)[at]
        keys = interleave(kv_near, kv_far, columns, half)
        pair_query = both_heads(query[pl.ds(at * half, half), columns], masks)
        return dot_nt(keys[: bias.shape[0]], pair_query) + jnp.concatenate([bias[...], bias[...]], axis=1)

    def finish(pair, at, softened):
        columns = slice(pair * 2 * HD, (pair + 1) * 2 * HD)
        values = interleave(kv_near, kv_far, slice(columns.start + width, columns.stop + width), half)
        turned = dot_tn(values[: softened.shape[0]], softened)
        turned = jnp.concatenate([turned[:HD, :half], turned[HD:, half:]], axis=0)
        attended[pl.ds(at * half, half), columns] = turned.T.astype(BF16)

    units = [(pair, at) for pair in range(width // (2 * HD)) for at in range(2)]
    ready = scores_of(*units[0])
    waiting = None
    for index, (pair, at) in enumerate(units):
        scores = ready
        if index + 1 < len(units):
            ready = scores_of(*units[index + 1])
        if waiting is not None:
            finish(*waiting)
        peak = jnp.max(scores, axis=0, keepdims=True)
        lifted = jnp.exp(scores - peak)
        total = jnp.sum(lifted, axis=0, keepdims=True)
        softened = (lifted * (1.0 / total)).astype(BF16)
        (probs_near, probs_far)[at][pair] = softened
        waiting = (pair, at, softened)
    finish(*waiting)


def attend_backward(query, kv_near, kv_far, probs_near, probs_far, d_att, d_query, d_kv_near, d_kv_far):
    width = query.shape[1]
    half = query.shape[0] // 2
    masks = lane_masks(half)

    def d_probs_of(pair, at):
        columns = slice(pair * 2 * HD, (pair + 1) * 2 * HD)
        values = interleave(kv_near, kv_far, slice(columns.start + width, columns.stop + width), half)
        pair_grad = both_heads(d_att[pl.ds(at * half, half), columns], masks)
        return pair_grad, dot_nt(values[: (probs_near, probs_far)[at].shape[1]], pair_grad)

    def finish(pair, at, pair_grad, softened, d_scores):
        columns = slice(pair * 2 * HD, (pair + 1) * 2 * HD)
        keys = interleave(kv_near, kv_far, columns, half)
        pair_query = both_heads(query[pl.ds(at * half, half), columns], masks)
        parts[at] = (dot(d_scores, pair_query), dot(softened, pair_grad))
        turned = dot_tn(keys[: softened.shape[0]], d_scores)
        turned = jnp.concatenate([turned[:HD, :half], turned[HD:, half:]], axis=0)
        d_query[pl.ds(at * half, half), columns] = (turned.T * (1.0 / HD**0.5)).astype(BF16)
        if at == 1:
            for kind, start in ((0, columns.start), (1, columns.start + width)):
                place = slice(start, start + 2 * HD)
                first = (parts[0][kind] + parts[1][kind][: 2 * half]).astype(BF16)
                second = parts[1][kind][2 * half :].astype(BF16)
                d_kv_near[:half, place] = first[:half]
                d_kv_far[:half, place] = first[half:]
                d_kv_near[half:, place] = second[:half]
                d_kv_far[half:, place] = second[half:]

    units = [(pair, at) for pair in range(width // (2 * HD)) for at in range(2)]
    parts = {}
    ready = d_probs_of(*units[0])
    waiting = None
    for index, (pair, at) in enumerate(units):
        pair_grad, d_probs = ready
        if index + 1 < len(units):
            ready = d_probs_of(*units[index + 1])
        if waiting is not None:
            finish(*waiting)
        softened = (probs_near, probs_far)[at][pair]
        probs = softened.astype(F32)
        row_sum = jnp.sum(probs * d_probs, axis=0, keepdims=True)
        waiting = (pair, at, pair_grad, softened, (probs * (d_probs - row_sum)).astype(BF16))
    finish(*waiting)


def project(rounded, w_qkv, query, kv):
    width = query.shape[1]
    for at in range(3):
        mixed = dot(rounded, w_qkv[:, at * width : (at + 1) * width]).astype(BF16)
        if at == 0:
            query[...] = mixed * jnp.asarray(1.0 / HD**0.5, BF16)
        else:
            kv[:, (at - 1) * width : at * width] = mixed


def normal_area(value):
    area = 0.5 + 0.5 * lax.erf(value * (0.5**0.5))
    bell = jnp.exp(value * value * -0.5) * ((2.0 * jnp.pi) ** -0.5)
    return area, bell


def tail_forward(hidden, attended, w_out, w_up, w_down, gains, shifts, active, slope, settled_low, units, scales):
    inner_width = w_up.shape[1]
    step = 512
    pre_first = hidden[...] + dot(attended[...], w_out[...])
    unit, scale, settled = norm_forward(pre_first, gains[0], shifts[0])
    units[0], scales[0] = unit, scale
    rounded = settled.astype(BF16)
    settled_low[...] = rounded
    second = settled
    count = inner_width // step
    ready = dot(rounded, w_up[:, :step])
    for at in range(count):
        span = slice(at * step, (at + 1) * step)
        inner = ready
        if at + 1 < count:
            ready = dot(rounded, w_up[:, (at + 1) * step : (at + 2) * step])
        area, bell = normal_area(inner)
        glow = (inner * area).astype(BF16)
        active[:, span] = glow
        slope[:, span] = (area + inner * bell).astype(BF16)
        second = second + dot(glow, w_down[span, :])
    unit, scale, result = norm_forward(second, gains[1], shifts[1])
    units[1], scales[1] = unit, scale
    return result


def tail_backward(info, gradient, w_out, w_up, w_down, gains, slope, units, scales, kept, sent, norm_grads, d_first_out, d_att):
    inner_width = w_up.shape[1]
    width = w_up.shape[0]
    shards = 4
    step, part = inner_width // shards, width // shards
    core = info[ME] % 2
    d_second, d_gain, d_shift = norm_backward(units[1], scales[1], gains[1], gradient)
    norm_grads[1:2, :] = d_gain
    norm_grads[3:4, :] = d_shift
    d_feed = d_second.astype(BF16)
    d_settled = d_second

    def place(at, columns, value):
        @pl.when(at % 2 == core)
        def _():
            kept[at // 2, :, columns] = value

        @pl.when(at % 2 != core)
        def _():
            sent[at // 2, :, columns] = value

    ready = dot_nt(d_feed, w_down[:step, :])
    for at in range(shards):
        span = slice(at * step, (at + 1) * step)
        d_active = ready
        if at + 1 < shards:
            ready = dot_nt(d_feed, w_down[(at + 1) * step : (at + 2) * step, :])
        d_inner = (d_active * slope[:, span].astype(F32)).astype(BF16)
        place(at, slice(0, step), d_inner)
        place(at, slice(step, step + part), d_feed[:, at * part : (at + 1) * part])
        d_settled = d_settled + dot_nt(d_inner, w_up[:, span])
    d_first, d_gain, d_shift = norm_backward(units[0], scales[0], gains[0], d_settled)
    norm_grads[0:1, :] = d_gain
    norm_grads[2:3, :] = d_shift
    d_first_out[...] = d_first
    d_branch = d_first.astype(BF16)
    for at in range(shards):
        place(at, slice(step + part, step + 2 * part), d_branch[:, at * part : (at + 1) * part])
    d_att[...] = dot_nt(d_branch, w_out[...]).astype(BF16)


def add_table(info, table, layer_at, get_rows, hidden):
    core = info[ME] % 2
    size = hidden.shape[0] // 4
    for block in range(4):
        start = block_start(info, block, core, size)
        rows = table[layer_at, pl.ds(start, size), :].astype(F32)
        hidden[block * size : (block + 1) * size, :] = get_rows(block) + rows


def split_rows(info, short, long, parts, sems):
    size = parts[0].shape[0]
    waits = []
    for delta, part in enumerate(parts):
        target = info[ME] ^ delta
        from_long = pltpu.make_async_copy(
            long.at[0, pl.ds(aligned(jnp.minimum(target, 1) * size, size), size), :], part, sems.at[delta]
        )
        from_short = pltpu.make_async_copy(short.at[jnp.maximum(target - 2, 0)], part, sems.at[delta])
        pl.when(target < 2)(from_long.start)
        pl.when(target >= 2)(from_short.start)
        waits.append(from_long.wait)
    return waits


def split_kernel(info, x_short, x_long, *refs):
    for wait in split_rows(info, x_short, x_long, refs[:-1], refs[-1]):
        wait()


def fetch(pairs, sems, parts):
    waits = []
    for source, target in pairs:
        step = target.shape[0] // parts
        for part in range(parts):
            rows = pl.ds(part * step, step)
            copy = pltpu.make_async_copy(source.at[rows], target.at[rows], sems.at[len(waits)])
            copy.start()
            waits.append(copy.wait)
    return waits


def load_kernel(info, table, w_qkv, w_out, w_up, w_down, *refs):
    sources = (table.at[0], table.at[1], w_qkv.at[0], w_out.at[0], w_up.at[0], w_down.at[0])
    targets = (refs[0].at[0], refs[0].at[1], *refs[1:5])
    for wait in fetch(zip(sources, targets), refs[5], 4):
        wait()


def load_late_kernel(info, w_one, w_two, one, two, sems):
    for wait in fetch(((w_one.at[1], one), (w_two.at[1], two)), sems, 4):
        wait()


def load_and_split_kernel(info, w_one, w_two, cot_short, cot_long, one, two, c0, c1, c2, c3, sems, split_sems):
    waits = split_rows(info, cot_short, cot_long, (c0, c1, c2, c3), split_sems)
    for wait in waits + fetch(((w_one.at[1], one), (w_two.at[1], two)), sems, 4):
        wait()


def pack_kernel(info, act, grad, kept, sent):
    size = kept.shape[1] // 2
    chip = info[ME] // 2
    for ref, target in ((sent, 1 - chip), (kept, chip)):
        for core in range(2):
            rows = pl.ds(aligned((2 * target + core) * size, size), size)
            ref[core, :size, :] = act[rows, :]
            ref[core, size:, :] = grad[rows, :]


def swap_kernel(info, kept, got, sent):
    core = info[ME] % 2
    sent[0] = kept[1 - core]
    sent[1] = got[1 - core]


def join_kernel(info, kept, got, swapped, act_short, act_long, grad_short, grad_long):
    size = kept.shape[1] // 2
    core = info[ME] % 2
    for delta, (part, at) in enumerate(((kept, core), (swapped, 0), (got, core), (swapped, 1))):
        source = info[ME] ^ delta
        for short, long, rows in ((act_short, act_long, slice(0, size)), (grad_short, grad_long, slice(size, 2 * size))):

            @pl.when(source < 2)
            def _():
                long[0, pl.ds(aligned(jnp.minimum(source, 1) * size, size), size), :] = part[at, rows, :]

            @pl.when(source >= 2)
            def _():
                short[jnp.maximum(source - 2, 0)] = part[at, rows, :]


def front_kernel(info, r0, r1, r2, r3, table, w_qkv, hidden, rounded, query, kv):
    size = r0.shape[0]
    core = info[ME] % 2
    for delta, ref in enumerate((r0, r1, r2, r3)):
        block = info[ME] ^ delta
        start = block_start(info, block, core, size)
        rows = ref[...].astype(F32) + table[0, pl.ds(start, size), :].astype(F32)
        hidden[pl.ds(aligned(block * size, size), size), :] = rows
    low = hidden[...].astype(BF16)
    rounded[...] = low
    project(low, w_qkv, query, kv)


def with_live(info, len_short, len_long):
    me = info[ME]
    live = jnp.where(me < 2, len_long[0], len_short[jnp.maximum(me - 2, 0)])
    return (me, live, info[DP])


def first_kernel(
    info, len_short, len_long, query, kv_near, kv_far, hidden, rounded, table, gains, shifts, w_out, w_up, w_down, w_next,
    probs_near, probs_far, slope, kept_x, units, scales, hidden_next, rounded_next, query_next, kv_next,
    bias_near, bias_far,
):
    width, inner = w_up.shape
    size = query.shape[0] // 4
    info = with_live(info, len_short, len_long)
    fill_bias(info, bias_near, bias_far, size)
    attended = kept_x.at[:, inner + width : inner + 2 * width]
    attend_forward(query, kv_near, kv_far, bias_near, bias_far, probs_near, probs_far, attended)
    kept_x[:, inner + 2 * width :] = rounded[...]
    result = tail_forward(
        hidden, attended, w_out, w_up, w_down, gains[0], shifts[0],
        kept_x.at[:, :inner], slope, kept_x.at[:, inner : inner + width], units, scales,
    ).astype(BF16).astype(F32)
    add_table(info, table, 1, lambda block: result[block * size : (block + 1) * size], hidden_next)
    low = hidden_next[...].astype(BF16)
    rounded_next[...] = low
    project(low, w_next, query_next, kv_next)


def second_kernel(
    info, len_short, len_long, query, kv_near, kv_far, hidden, rounded, gains, shifts, w_out, w_up, w_down,
    probs_near, probs_far, slope, kept_x, units, scales, result, bias_near, bias_far,
):
    width, inner = w_up.shape
    info = with_live(info, len_short, len_long)
    fill_bias(info, bias_near, bias_far, query.shape[0] // 4)
    attended = kept_x.at[:, inner + width : inner + 2 * width]
    attend_forward(query, kv_near, kv_far, bias_near, bias_far, probs_near, probs_far, attended)
    kept_x[:, inner + 2 * width :] = rounded[...]
    result[...] = tail_forward(
        hidden, attended, w_out, w_up, w_down, gains[1], shifts[1],
        kept_x.at[:, :inner], slope, kept_x.at[:, inner : inner + width], units, scales,
    ).astype(BF16)


def turn_kernel(
    info, c0, c1, c2, c3, gains, slope, units, scales, w_out, w_up, w_down,
    bx_kept, bx_sent, norm_grads, d_first, d_att, cot,
):
    size = c0.shape[0]
    for delta, cot_part in enumerate((c0, c1, c2, c3)):
        rows = pl.ds(aligned((info[ME] ^ delta) * size, size), size)
        cot[rows, :] = cot_part[...].astype(F32)
    tail_backward(
        info, cot[...], w_out, w_up, w_down, gains[1], slope, units, scales,
        bx_kept, bx_sent, norm_grads, d_first, d_att,
    )


def attend_back_kernel(unused, query, kv_near, kv_far, probs_near, probs_far, d_att, d_query, d_kv_near, d_kv_far):
    attend_backward(query, kv_near, kv_far, probs_near, probs_far, d_att, d_query, d_kv_near, d_kv_far)


def close_layer(info, d_query, d_kv, d_kv_far, d_first, w_qkv, kept, sent, skip=0):
    shards = 4
    width = d_query.shape[1]
    core = info[ME] % 2
    total = (d_kv[...].astype(F32) + d_kv_far[...].astype(F32)).astype(BF16)
    d_qkv = jnp.concatenate([d_query[...], total], axis=1)
    d_hidden = d_first[...] + dot_nt(d_qkv, w_qkv[...])
    low = d_hidden.astype(BF16)
    step, part = 3 * width // shards, width // shards
    for at in range(shards):
        pieces = (
            (slice(skip, skip + step), d_qkv[:, at * step : (at + 1) * step]),
            (slice(skip + step, skip + step + part), low[:, at * part : (at + 1) * part]),
        )

        @pl.when(at % 2 == core)
        def _():
            for columns, value in pieces:
                kept[at // 2, :, columns] = value

        @pl.when(at % 2 != core)
        def _():
            for columns, value in pieces:
                sent[at // 2, : value.shape[0], columns] = value

    return d_hidden, low


def middle_kernel(
    info, d_query, d_kv, d_kv_far, d_first, w_qkv, gains, slope, units, scales, w_out, w_up, w_down, norms_late,
    qx_kept, qx_sent, bx_kept, bx_sent, norm_grads, d_first_out, d_att,
):
    d_hidden, unused = close_layer(info, d_query, d_kv, d_kv_far, d_first, w_qkv, qx_kept, qx_sent)
    norm_grads[4:, :] = norms_late[...]
    tail_backward(
        info, d_hidden, w_out, w_up, w_down, gains[0], slope, units, scales,
        bx_kept, bx_sent, norm_grads, d_first_out, d_att,
    )


def last_kernel(info, d_query, d_kv, d_kv_far, d_first, w_qkv, norms, qx_kept, qx_sent, grad):
    unused, low = close_layer(info, d_query, d_kv, d_kv_far, d_first, w_qkv, qx_kept, qx_sent)
    grad[...] = low
    tokens = d_query.shape[0]
    padded = jnp.concatenate([norms[...], jnp.zeros(norms.shape, F32)], axis=0)
    qx_sent[0, tokens:, :] = padded.astype(BF16)
    qx_sent[1, tokens:, :] = jnp.zeros(padded.shape, BF16)


def split_blocks(info, places, whole_ref, kept, sent):
    def split(place):
        bit, axis, at = place
        mine = (info[axis] >> at) & 1
        for ref, value in ((sent, 1 - mine), (kept, mine)):
            for index in range(ref.shape[0]):
                low = index & ((1 << bit) - 1)
                source = ((index >> bit) << (bit + 1)) + low + (value << bit)
                total = whole_ref[0][source]
                for other in whole_ref[1:]:
                    total = total + other[source]
                ref[index] = total

    if places[0] == places[1]:
        split(places[0])
    else:
        for core in range(2):
            pl.when(info[ME] % 2 == core)(functools.partial(split, places[core]))


def fold_kernel(places, info, kept, got, new_kept, new_sent):
    split_blocks(info, places, (kept, got), new_kept, new_sent)


def put(pieces, whole, name, x, value):
    for at, (tiles, unused) in enumerate(pieces):
        if name in tiles:
            lanes = value.shape[2]
            start = tiles.index(name) * lanes
            n_dp = value.shape[0]
            whole[at][x * n_dp : (x + 1) * n_dp, :, start : start + lanes] = value.astype(BF16)


def by_blocks(value, n_dp):
    return value.reshape(n_dp, value.shape[0] // n_dp, value.shape[1])


def feed_grad_kernel(pieces, info, x_near, x_far, b_near, b_far, *refs):
    count = len(pieces)
    outs, whole = refs[: 2 * count], refs[2 * count :]
    n_dp, rows = outs[0].shape[0], outs[0].shape[1]
    width = n_dp * rows
    inner = x_near.shape[1] - 3 * width
    step, part = inner // 4, width // 4
    for x in range(2):
        total = dot_tn(x_near[:, inner : inner + width], b_near[x, :, :step])
        total = total + dot_tn(x_far[:, inner : inner + width], b_far[x, :, :step])
        for tile in range(step // part):
            put(pieces, whole, ("up", tile), x, by_blocks(total[:, tile * part : (tile + 1) * part], n_dp))
    feeds = [
        jnp.concatenate([ref[0, :, step : step + part], ref[1, :, step : step + part]], axis=1)
        for ref in (b_near, b_far)
    ]
    span_size = 512
    fold = inner // width
    for at in range(inner // span_size):
        span = slice(at * span_size, (at + 1) * span_size)
        total = dot_tn(feeds[0], x_near[:, span]) + dot_tn(feeds[1], x_far[:, span])
        total = total.astype(BF16).T if rows % 16 == 0 else total.T
        for group in range(span_size // rows):
            block, tile = divmod(at * (span_size // rows) + group, fold)
            for index, (tiles, unused) in enumerate(pieces):
                if ("down", tile) in tiles:
                    start = tiles.index(("down", tile)) * part
                    for x in range(2):
                        value = total[group * rows : (group + 1) * rows, x * part : (x + 1) * part]
                        whole[index][x * n_dp + block, :, start : start + part] = value.astype(BF16)
    for at, (unused, places) in enumerate(pieces):
        split_blocks(info, places, (whole[at],), outs[2 * at], outs[2 * at + 1])


def attend_grad_kernel(pieces, with_norms, info, x_near, x_far, b_near, b_far, q_near, q_far, *refs):
    count = len(pieces)
    norms = None
    if with_norms:
        norms, refs = refs[0], refs[1:]
    outs, whole, table = refs[: 2 * count], refs[2 * count : -1], refs[-1]
    n_dp, rows = outs[0].shape[0], outs[0].shape[1]
    width = n_dp * rows
    part = width // 4
    tokens = x_near.shape[0]
    inner = x_near.shape[1] - 3 * width
    step = 3 * part
    feed = inner // 4 + part
    skip = q_near.shape[2] - width
    core = info[ME] % 2
    size = tokens // 4
    for x in range(2):
        lows = slice(inner + 2 * width, inner + 3 * width)
        total = dot_tn(x_near[:, lows], q_near[x, :, skip : skip + step])
        total = total + dot_tn(x_far[:, lows], q_far[x, :tokens, skip : skip + step])
        for tile in range(step // part):
            put(pieces, whole, ("qkv", tile), x, by_blocks(total[:, tile * part : (tile + 1) * part], n_dp))
        outs_at = slice(inner + width, inner + 2 * width)
        total = dot_tn(x_near[:, outs_at], b_near[x, :, feed : feed + part])
        total = total + dot_tn(x_far[:, outs_at], b_far[x, :, feed : feed + part])
        put(pieces, whole, ("out", 0), x, by_blocks(total, n_dp))
        table[...] = jnp.zeros_like(table)
        for source, place in ((q_near, core), (q_far, 1 - core)):
            for block in range(4):
                span = pl.ds(block_start(info, block, place, size), size)
                table[span, :] += source[x, block * size : (block + 1) * size, skip + step :].astype(F32)
        put(pieces, whole, ("pos", 0), x, by_blocks(table[...], n_dp))
    if with_norms:
        sums = norms[...] + q_far[0, tokens:, :].astype(F32)[: norms.shape[0]]
        share = width // n_dp
        for block in range(n_dp):
            value = sums[:, block * share : (block + 1) * share]
            value = jnp.concatenate([value, jnp.zeros((value.shape[0], part - share), F32)], axis=1)
            if rows > value.shape[0]:
                value = jnp.concatenate([value, jnp.zeros((rows - value.shape[0], part), F32)], axis=0)
            for at, (tiles, unused) in enumerate(pieces):
                if ("norm", 0) in tiles:
                    start = tiles.index(("norm", 0)) * part
                    for x in range(2):
                        whole[at][x * n_dp + block, :, start : start + part] = value.astype(BF16)
    for at, (unused, places) in enumerate(pieces):
        split_blocks(info, places, (whole[at],), outs[2 * at], outs[2 * at + 1])


def final_kernel(pieces, info, *refs):
    ins, (*sums, gain, shift) = refs[: 2 * len(pieces)], refs[2 * len(pieces) :]
    outs = dict(zip(("qkv", "out", "up", "down", "pos"), sums))
    for at, (layer_at, tiles) in enumerate(pieces):
        kept, got = ins[2 * at], ins[2 * at + 1]
        rows = kept.shape[1]
        part = outs["out"].shape[2]
        for index, (name, tile) in enumerate(tiles):
            lanes = slice(index * part, (index + 1) * part)
            total = kept[0, :, lanes].astype(F32) + got[0, :, lanes].astype(F32)
            if name == "norm":
                share = gain.shape[2]
                for row in range(8):
                    ref = (gain, shift)[row // 2 % 2]
                    ref[row // 4, row % 2 : row % 2 + 1, :] = total[row : row + 1, :share]
            elif name == "down":
                outs[name][layer_at, tile * rows : (tile + 1) * rows, :] = total
            else:
                outs[name][layer_at, :, tile * part : (tile + 1) * part] = total


MB = 1024 * 1024
TOKEN = ((8, 128), F32)
SMEM = pl.BlockSpec(memory_space=pltpu.SMEM)
VMEM = pl.BlockSpec(memory_space=pltpu.VMEM)
HBM = pl.BlockSpec(memory_space=pltpu.HBM)

FLOPS = 10**10
COSTS = dict(feed1=0, middle=0, back=0, rest1=0, feed0=0, last=0, rest0=0, fold=10000000000, pack=0, tick=0)


def pin(array):
    return pltpu.with_memory_space_constraint(array, pltpu.VMEM)


class Line:
    def __init__(self):
        self.token = None
        self.trail = []
        self.used = set()

    def flip(self, array, axis, bit):
        size = lax.axis_size(axis)
        self.trail.append(lax.ppermute(array, axis, [(at, at ^ bit) for at in range(size)]))
        return self.trail[-1]

    def cross(self, array, steps):
        n_dp, n_seq = lax.axis_size("dp"), lax.axis_size("seq")
        pairs = []
        for dp in range(n_dp):
            for seq in range(n_seq):
                step = steps[seq % 2]
                other = (dp, seq ^ 2) if step == "x" else (dp ^ (1 << step), seq)
                pairs.append((dp * n_seq + seq, other[0] * n_seq + other[1]))
        self.trail.append(lax.ppermute(array, ("dp", "seq"), pairs))
        return self.trail[-1]

    def near(self, array):
        return self.flip(array, "seq", 1)

    def gather(self, parts):
        return [parts[0]] + [self.flip(parts[delta], "seq", delta) for delta in (1, 2, 3)]

    def past(self, used=True):
        return [array for array in self.trail if (id(array) in self.used) == used]

    def tick(self, after=()):
        self.call("tick", lambda info: None, [], (), after=after)

    def call(self, name, kernel, outs, args, scratch=(), limit=8, smem=0, hbm=0, final=False, after=(), past=()):
        self.used.update(id(arg) for arg in (*args, *after))
        tokens = [] if self.token is None else [self.token]
        skip = len(past)
        shapes = [jax.ShapeDtypeStruct(*kind) if final else pltpu.VMEM(*kind) for kind in outs] + [pltpu.VMEM(*TOKEN)]
        count, extra = len(args), len(tokens) + len(after)

        def body(*refs):
            refs = refs[skip:]
            given = refs[:count]
            made = refs[count + extra : count + extra + len(outs)]
            refs[count + extra + len(outs)][...] = jnp.zeros(TOKEN[0], F32)
            info = (lax.axis_index("seq"), None, lax.axis_index("dp"))
            kernel(info, *given, *made, *refs[count + extra + len(outs) + 1 :])

        far = smem + hbm
        operands = [pin(array) for array in past] + list(args[:smem]) + [pltpu.with_memory_space_constraint(arg, pltpu.HBM) for arg in args[smem:far]]
        operands += [pin(arg) for arg in args[far:]]
        operands += [pin(array) for array in (*after, *tokens)]
        results = pl.pallas_call(
            body,
            in_specs=[VMEM] * skip + [SMEM] * smem + [HBM] * hbm + [VMEM] * (count - far + extra),
            out_specs=[VMEM] * (len(outs) + 1),
            out_shape=shapes,
            scratch_shapes=list(scratch),
            compiler_params=pltpu.CompilerParams(vmem_limit_bytes=limit * MB),
            cost_estimate=pl.CostEstimate(flops=COSTS.get(name, FLOPS), bytes_accessed=0, transcendentals=0),
            name=name,
        )(*operands)
        self.token = results[-1]
        return list(results[:-1])


FEED = tuple(("up", at) for at in range(4)) + tuple(("down", at) for at in range(4))
REST = (("qkv", 0), ("qkv", 1), ("qkv", 2), ("out", 0), ("pos", 0))
LAST = REST + (("norm", 0),)
PIECES = dict(
    a=(1, "feed1", FEED, "xyhl", "lhyx"),
    b=(1, "rest1", REST, "yxhl", "yhlx"),
    c=(0, "feed0", FEED, "lxyh", "xlhy"),
    d=(0, "rest0", LAST, "yxlh", "xlyh"),
)
ORDER = (
    "feed1", "middle", "back", "feed0", "rest1", "last", "a", "rest0", "c", "b", "a", "pack", "d", "c", "swap", "b",
    "d", "c", "a", "d", "take", "b",
)


class Sum:
    def __init__(self, name, n_bits):
        self.layer_at, self.maker, self.tiles, *paths = PIECES[name]
        letters = {"x": ["x"], "y": [0], "l": [1], "h": list(range(2, n_bits))}
        self.steps = [[bit for letter in path for bit in letters[letter] if bit == "x" or bit < n_bits] for path in paths]
        self.bits = [[*range(n_bits), "x"] for unused in paths]

    def left(self):
        return len(self.steps[0])

    def place(self):
        places = []
        for steps, bits in zip(self.steps, self.bits):
            where = bits.index(steps[0])
            places.append((where, ME, 1) if steps[0] == "x" else (where, DP, steps[0]))
        return places

    def start(self, line, kept, sent):
        now = [steps.pop(0) for steps in self.steps]
        for bits, step in zip(self.bits, now):
            bits.remove(step)
        self.kept = kept
        self.got = line.cross(sent, now)

    def fold(self, line):
        blocks, rows, columns = self.kept.shape
        kind = ((blocks // 2, rows, columns), BF16)
        self.start(line, *line.call("fold", functools.partial(fold_kernel, self.place()), [kind, kind], (self.kept, self.got)))


def local(
    x_short, x_long, len_short, len_long, w_qkv, w_out, w_up, w_down, pos_table, norm_gain, norm_bias, cot_short, cot_long
):
    n_dp = lax.axis_size("dp")
    n_bits = n_dp.bit_length() - 1
    width = x_short.shape[2]
    size = x_short.shape[1]
    tokens = 4 * size
    half = tokens // 2
    inner = w_up.shape[2]
    pairs = width // (2 * HD)
    rows = width // n_dp
    part = ((size, width), BF16)
    hidden_kind = ((tokens, width), F32)
    low_kind = ((tokens, width), BF16)
    kv_kind = ((tokens, 2 * width), BF16)
    probs_kinds = [((pairs, 2 * half, 2 * half), BF16), ((pairs, 4 * half, 2 * half), BF16)]
    slope_kind = ((tokens, inner), BF16)
    x_kind = ((tokens, inner + 3 * width), BF16)
    units_kind = ((2, tokens, width), F32)
    scales_kind = ((2, tokens, 1), F32)
    bx_kind = ((2, tokens, inner // 4 + width // 2), BF16)
    qx_kind = ((2, tokens, width), BF16)
    biases = [pltpu.VMEM((2 * half, half), F32), pltpu.VMEM((4 * half, half), F32)]
    lens = (len_short, len_long)
    line = Line()
    sums = {name: Sum(name, n_bits) for name in PIECES}

    four = [pltpu.SemaphoreType.DMA((4,))]
    rows_in = line.gather(line.call("split", split_kernel, [part] * 4, (x_short, x_long), four, hbm=2))
    stacks = (w_qkv, w_out, w_up, w_down)
    kinds = [(array.shape[1:], BF16) for array in stacks]
    table, w_qkv0, w_out0, w_up0, w_down0 = line.call(
        "load", load_kernel, [(pos_table.shape, BF16)] + kinds, (pos_table, *stacks), [pltpu.SemaphoreType.DMA((24,))], hbm=5
    )
    hidden0, rounded0, query0, kv0 = line.call(
        "front", front_kernel, [hidden_kind, low_kind, low_kind, kv_kind], (*rows_in, table, w_qkv0)
    )
    kv0_far = line.near(kv0)
    eight = [pltpu.SemaphoreType.DMA((8,))]
    w_qkv1, w_out1, *cots = line.call(
        "load", load_and_split_kernel, [kinds[0], kinds[1]] + [part] * 4, (w_qkv, w_out, cot_short, cot_long),
        eight + four, hbm=4,
    )
    layer_kinds = probs_kinds + [slope_kind, x_kind, units_kind, scales_kind]
    probs_near0, probs_far0, slope0, x0, units0, scales0, hidden1, rounded1, query1, kv1 = line.call(
        "first", first_kernel, layer_kinds + [hidden_kind, low_kind, low_kind, kv_kind],
        (
            *lens, query0, kv0, kv0_far, hidden0, rounded0, table, norm_gain, norm_bias,
            w_out0, w_up0, w_down0, w_qkv1,
        ),
        biases, limit=16, smem=2,
    )
    kv1_far = line.near(kv1)
    cot_in = line.gather(cots)
    x0_far = line.near(x0)
    w_up1, w_down1 = line.call("load", load_late_kernel, [kinds[2], kinds[3]], (w_up, w_down), eight, hbm=2)
    probs_near1, probs_far1, slope1, x1, units1, scales1, act = line.call(
        "second", second_kernel, layer_kinds + [low_kind],
        (*lens, query1, kv1, kv1_far, hidden1, rounded1, norm_gain, norm_bias, w_out1, w_up1, w_down1),
        biases, limit=16, smem=2,
    )
    x1_far = line.near(x1)
    bx1, bx1_sent, norms1, d_first1, d_att1 = line.call(
        "turn", turn_kernel, [bx_kind, bx_kind, ((4, width), F32), hidden_kind, low_kind],
        (*cot_in, norm_gain, slope1, units1, scales1, w_out1, w_up1, w_down1), [pltpu.VMEM(*hidden_kind)],
    )
    bx1_far = line.near(bx1_sent)

    def grads(maker, kernel, args, scratch=()):
        made = [each for each in sums.values() if each.maker == maker]
        pieces = [(each.tiles, each.place()) for each in made]
        columns = [len(each.tiles) * (width // 4) for each in made]
        outs = line.call(
            maker, functools.partial(kernel, pieces),
            [((n_dp, rows, count), BF16) for count in columns for unused in range(2)],
            args, [pltpu.VMEM((2 * n_dp, rows, count), BF16) for count in columns] + list(scratch), limit=12,
        )
        for at, each in enumerate(made):
            each.start(line, outs[2 * at], outs[2 * at + 1])

    table = [pltpu.VMEM((width, width // 4), F32)]
    back_kinds = [low_kind, kv_kind, kv_kind]
    d_query1, d_kv1, d_kv1_sent = line.call(
        "attend_back", attend_back_kernel, back_kinds, (query1, kv1, kv1_far, probs_near1, probs_far1, d_att1), after=[x0_far]
    )
    d_kv1_far = line.near(d_kv1_sent)
    latest = None
    order = list(ORDER)
    while order or any(each.left() for each in sums.values()):
        if not order:
            order = [name for name, each in sums.items() if each.left()]
        task = order.pop(0)
        if task in sums:
            if sums[task].left():
                if task == latest:
                    line.tick()
                sums[task].fold(line)
                latest = task
        elif task == "tick":
            line.tick()
        elif task == "feed1":
            grads("feed1", feed_grad_kernel, (x1, x1_far, bx1, bx1_far))
        elif task == "middle":
            qx1, qx1_sent, bx0, bx0_sent, norms, d_first0, d_att0 = line.call(
                "middle", middle_kernel, [qx_kind, qx_kind, bx_kind, bx_kind, ((8, width), F32), hidden_kind, low_kind],
                (
                    d_query1, d_kv1, d_kv1_far, d_first1, w_qkv1, norm_gain, slope0, units0, scales0, w_out0, w_up0, w_down0,
                    norms1,
                ),
            )
            bx0_far = line.near(bx0_sent)
            qx1_far = line.near(qx1_sent)
        elif task == "back":
            d_query0, d_kv0, d_kv0_sent = line.call(
                "back", attend_back_kernel, back_kinds, (query0, kv0, kv0_far, probs_near0, probs_far0, d_att0)
            )
            d_kv0_far = line.near(d_kv0_sent)
        elif task == "rest1":
            grads(
                "rest1", lambda pieces, *refs: attend_grad_kernel(pieces, False, *refs),
                (x1, x1_far, bx1, bx1_far, qx1, qx1_far), table,
            )
        elif task == "feed0":
            grads("feed0", feed_grad_kernel, (x0, x0_far, bx0, bx0_far))
        elif task == "last":
            longer = ((2, tokens + 16, width), BF16)
            qx0, qx0_sent, grad = line.call(
                "last", last_kernel, [qx_kind, longer, low_kind], (d_query0, d_kv0, d_kv0_far, d_first0, w_qkv0, norms)
            )
            qx0_far = line.near(qx0_sent)
        elif task == "rest0":
            grads(
                "rest0", lambda pieces, *refs: attend_grad_kernel(pieces, True, *refs),
                (x0, x0_far, bx0, bx0_far, qx0, qx0_far, norms), table,
            )
        elif task == "pack":
            own_rows, rows_sent = line.call("pack", pack_kernel, [((2, 2 * size, width), BF16)] * 2, (act, grad))
            chip_rows = line.flip(rows_sent, "seq", 2)
        elif task == "swap":
            (rows_sent,) = line.call("pack", swap_kernel, [((2, 2 * size, width), BF16)], (own_rows, chip_rows))
            core_rows = line.near(rows_sent)
        elif task == "take":
            line.tick(after=[core_rows])
    joined = line.call(
        "join", join_kernel, [(x_short.shape, BF16), (x_long.shape, BF16)] * 2, (own_rows, chip_rows, core_rows), final=True,
        past=line.past(),
    )
    shard = ((LAYERS, rows, width // 4), F32)
    totals = line.call(
        "final", functools.partial(final_kernel, [(each.layer_at, each.tiles) for each in sums.values()]),
        [
            ((LAYERS, rows, 3 * width // 4), F32), shard, ((LAYERS, rows, inner // 4), F32),
            ((LAYERS, inner // n_dp, width // 4), F32), shard,
            ((LAYERS, 2, rows), F32), ((LAYERS, 2, rows), F32),
        ],
        [array for each in sums.values() for array in (each.kept, each.got)], final=True, past=line.past(False),
    )
    return (*joined, *totals)


def solution(mesh):
    rows = P("dp", "seq", None)
    grads = P(None, "dp", "seq")
    norms = P(None, None, "dp")
    return jax.shard_map(
        local,
        mesh=mesh,
        in_specs=(rows, rows, P("dp"), P("dp")) + (P(),) * 7 + (rows, rows),
        out_specs=(rows,) * 4 + (grads,) * 5 + (norms, norms),
        check_vma=False,
    )
```

```python
import functools

import jax
import jax.numpy as jnp
from jax import lax
from jax.experimental import pallas as pl
from jax.experimental.pallas import tpu as pltpu
from jax.sharding import PartitionSpec as P

LAYERS = 2
HD = 64
F32 = jnp.float32
BF16 = jnp.bfloat16
NEG = -1000000000.0


def dot(left, right):
    return lax.dot_general(left, right, (((1,), (0,)), ((), ())), preferred_element_type=F32)


def dot_nt(left, right):
    return lax.dot_general(left, right, (((1,), (1,)), ((), ())), preferred_element_type=F32)


def dot_tn(left, right):
    return lax.dot_general(left, right, (((0,), (0,)), ((), ())), preferred_element_type=F32)


ME, LIVE, DP = 0, 1, 2


def aligned(value, step):
    return pl.multiple_of(value, step)


def block_start(info, block, core, size):
    is_long = info[ME] < 2
    return aligned(jnp.where(is_long, (2 * block + core) * size, block * size), size)


def norm_forward(values, gain, shift):
    centre = jnp.mean(values, axis=-1, keepdims=True)
    centred = values - centre
    spread = jnp.mean(centred * centred, axis=-1, keepdims=True)
    scale = lax.rsqrt(spread + 1e-05)
    unit = centred * scale
    return unit, scale, unit * gain + shift


def norm_backward(unit, scale, gain, gradient):
    d_gain = jnp.sum(gradient * unit, axis=0, keepdims=True)
    d_shift = jnp.sum(gradient, axis=0, keepdims=True)
    scaled = gradient * gain
    mean_one = jnp.mean(scaled, axis=-1, keepdims=True)
    mean_two = jnp.mean(scaled * unit, axis=-1, keepdims=True)
    return scale * (scaled - mean_one - unit * mean_two), d_gain, d_shift


def positions(info, rows, core, size):
    is_long = info[ME] < 2
    spread = (rows // size) * (2 * size) + core * size + rows % size
    return jnp.where(is_long, spread, rows)


def fill_bias(info, bias_near, bias_far, size):
    core = info[ME] % 2
    is_long = info[ME] < 2
    half = bias_near.shape[1]
    for at, ref in ((0, bias_near), (1, bias_far)):
        queries = positions(info, lax.broadcasted_iota(jnp.int32, (half, half), 1) + at * half, core, size)
        for part in range(2 * (at + 1)):
            rows = lax.broadcasted_iota(jnp.int32, (half, half), 0) + (part // 2) * half
            if part % 2 == 0:
                keys = positions(info, rows, core, size)
            else:
                keys = jnp.where(is_long, positions(info, rows, 1 - core, size), 1 << 20)
            allowed = (keys <= queries) & (keys < info[LIVE])
            ref[pl.ds(part * half, half), :] = jnp.where(allowed, 0.0, NEG)


def interleave(near, far, columns, half):
    return jnp.concatenate(
        [near[:half, columns], far[:half, columns], near[half:, columns], far[half:, columns]], axis=0
    )


def lane_masks(half):
    lanes = lax.broadcasted_iota(jnp.int32, (half, 2 * HD), 1)
    first = jnp.where(lanes < HD, 1.0, 0.0).astype(BF16)
    return first, (1.0 - first.astype(F32)).astype(BF16)


def both_heads(rows, masks):
    return jnp.concatenate([rows * masks[0], rows * masks[1]], axis=0)


def attend_forward(query, kv_near, kv_far, bias_near, bias_far, probs_near, probs_far, attended):
    width = query.shape[1]
    half = query.shape[0] // 2
    masks = lane_masks(half)

    def scores_of(pair, at):
        columns = slice(pair * 2 * HD, (pair + 1) * 2 * HD)
        bias = (bias_near, bias_far)[at]
        keys = interleave(kv_near, kv_far, columns, half)
        pair_query = both_heads(query[pl.ds(at * half, half), columns], masks)
        return dot_nt(keys[: bias.shape[0]], pair_query) + jnp.concatenate([bias[...], bias[...]], axis=1)

    def finish(pair, at, softened):
        columns = slice(pair * 2 * HD, (pair + 1) * 2 * HD)
        values = interleave(kv_near, kv_far, slice(columns.start + width, columns.stop + width), half)
        turned = dot_tn(values[: softened.shape[0]], softened)
        turned = jnp.concatenate([turned[:HD, :half], turned[HD:, half:]], axis=0)
        attended[pl.ds(at * half, half), columns] = turned.T.astype(BF16)

    units = [(pair, at) for pair in range(width // (2 * HD)) for at in range(2)]
    ready = scores_of(*units[0])
    waiting = None
    for index, (pair, at) in enumerate(units):
        scores = ready
        if index + 1 < len(units):
            ready = scores_of(*units[index + 1])
        if waiting is not None:
            finish(*waiting)
        peak = jnp.max(scores, axis=0, keepdims=True)
        lifted = jnp.exp(scores - peak)
        total = jnp.sum(lifted, axis=0, keepdims=True)
        softened = (lifted * (1.0 / total)).astype(BF16)
        (probs_near, probs_far)[at][pair] = softened
        waiting = (pair, at, softened)
    finish(*waiting)


def attend_backward(query, kv_near, kv_far, probs_near, probs_far, d_att, d_query, d_kv_near, d_kv_far):
    width = query.shape[1]
    half = query.shape[0] // 2
    masks = lane_masks(half)

    def d_probs_of(pair, at):
        columns = slice(pair * 2 * HD, (pair + 1) * 2 * HD)
        values = interleave(kv_near, kv_far, slice(columns.start + width, columns.stop + width), half)
        pair_grad = both_heads(d_att[pl.ds(at * half, half), columns], masks)
        return pair_grad, dot_nt(values[: (probs_near, probs_far)[at].shape[1]], pair_grad)

    def finish(pair, at, pair_grad, softened, d_scores):
        columns = slice(pair * 2 * HD, (pair + 1) * 2 * HD)
        keys = interleave(kv_near, kv_far, columns, half)
        pair_query = both_heads(query[pl.ds(at * half, half), columns], masks)
        parts[at] = (dot(d_scores, pair_query), dot(softened, pair_grad))
        turned = dot_tn(keys[: softened.shape[0]], d_scores)
        turned = jnp.concatenate([turned[:HD, :half], turned[HD:, half:]], axis=0)
        d_query[pl.ds(at * half, half), columns] = (turned.T * (1.0 / HD**0.5)).astype(BF16)
        if at == 1:
            for kind, start in ((0, columns.start), (1, columns.start + width)):
                place = slice(start, start + 2 * HD)
                first = (parts[0][kind] + parts[1][kind][: 2 * half]).astype(BF16)
                second = parts[1][kind][2 * half :].astype(BF16)
                d_kv_near[:half, place] = first[:half]
                d_kv_far[:half, place] = first[half:]
                d_kv_near[half:, place] = second[:half]
                d_kv_far[half:, place] = second[half:]

    units = [(pair, at) for pair in range(width // (2 * HD)) for at in range(2)]
    parts = {}
    ready = d_probs_of(*units[0])
    waiting = None
    for index, (pair, at) in enumerate(units):
        pair_grad, d_probs = ready
        if index + 1 < len(units):
            ready = d_probs_of(*units[index + 1])
        if waiting is not None:
            finish(*waiting)
        softened = (probs_near, probs_far)[at][pair]
        probs = softened.astype(F32)
        row_sum = jnp.sum(probs * d_probs, axis=0, keepdims=True)
        waiting = (pair, at, pair_grad, softened, (probs * (d_probs - row_sum)).astype(BF16))
    finish(*waiting)


def project(rounded, w_qkv, query, kv):
    width = query.shape[1]
    for at in range(3):
        mixed = dot(rounded, w_qkv[:, at * width : (at + 1) * width]).astype(BF16)
        if at == 0:
            query[...] = mixed * jnp.asarray(1.0 / HD**0.5, BF16)
        else:
            kv[:, (at - 1) * width : at * width] = mixed


def normal_area(value):
    area = 0.5 + 0.5 * lax.erf(value * (0.5**0.5))
    bell = jnp.exp(value * value * -0.5) * ((2.0 * jnp.pi) ** -0.5)
    return area, bell


def tail_forward(hidden, attended, w_out, w_up, w_down, gains, shifts, active, slope, settled_low, units, scales):
    inner_width = w_up.shape[1]
    step = 512
    pre_first = hidden[...] + dot(attended[...], w_out[...])
    unit, scale, settled = norm_forward(pre_first, gains[0], shifts[0])
    units[0], scales[0] = unit, scale
    rounded = settled.astype(BF16)
    settled_low[...] = rounded
    second = settled
    count = inner_width // step
    ready = dot(rounded, w_up[:, :step])
    for at in range(count):
        span = slice(at * step, (at + 1) * step)
        inner = ready
        if at + 1 < count:
            ready = dot(rounded, w_up[:, (at + 1) * step : (at + 2) * step])
        area, bell = normal_area(inner)
        glow = (inner * area).astype(BF16)
        active[:, span] = glow
        slope[:, span] = (area + inner * bell).astype(BF16)
        second = second + dot(glow, w_down[span, :])
    unit, scale, result = norm_forward(second, gains[1], shifts[1])
    units[1], scales[1] = unit, scale
    return result


def part_ways(info, every, kept, sent):
    core = info[ME] % 2
    for x in range(2):
        kept[x, : every.shape[1], :] = every[2 * x + core]
        sent[x, : every.shape[1], :] = every[2 * x + 1 - core]


def tail_backward(
    info, gradient, w_out, w_up, w_down, gains, slope, units, scales, kept, sent, norm_grads, d_first_out, d_att, every
):
    inner_width = w_up.shape[1]
    width = w_up.shape[0]
    shards = 4
    step, part = inner_width // shards, width // shards
    d_second, d_gain, d_shift = norm_backward(units[1], scales[1], gains[1], gradient)
    norm_grads[1:2, :] = d_gain
    norm_grads[3:4, :] = d_shift
    d_feed = d_second.astype(BF16)
    d_settled = d_second

    ready = dot_nt(d_feed, w_down[:step, :])
    for at in range(shards):
        span = slice(at * step, (at + 1) * step)
        d_active = ready
        if at + 1 < shards:
            ready = dot_nt(d_feed, w_down[(at + 1) * step : (at + 2) * step, :])
        d_inner = (d_active * slope[:, span].astype(F32)).astype(BF16)
        every[at, :, :step] = d_inner
        every[at, :, step : step + part] = d_feed[:, at * part : (at + 1) * part]
        d_settled = d_settled + dot_nt(d_inner, w_up[:, span])
    d_first, d_gain, d_shift = norm_backward(units[0], scales[0], gains[0], d_settled)
    norm_grads[0:1, :] = d_gain
    norm_grads[2:3, :] = d_shift
    d_first_out[...] = d_first
    d_branch = d_first.astype(BF16)
    for at in range(shards):
        every[at, :, step + part :] = d_branch[:, at * part : (at + 1) * part]
    d_att[...] = dot_nt(d_branch, w_out[...]).astype(BF16)
    part_ways(info, every, kept, sent)


def add_table(info, table, layer_at, get_rows, hidden):
    core = info[ME] % 2
    size = hidden.shape[0] // 4
    for block in range(4):
        start = block_start(info, block, core, size)
        rows = table[layer_at, pl.ds(start, size), :].astype(F32)
        hidden[block * size : (block + 1) * size, :] = get_rows(block) + rows


def split_rows(info, short, long, parts, sems):
    size = parts[0].shape[0]
    waits = []
    for delta, part in enumerate(parts):
        target = info[ME] ^ delta
        from_long = pltpu.make_async_copy(
            long.at[0, pl.ds(aligned(jnp.minimum(target, 1) * size, size), size), :], part, sems.at[delta]
        )
        from_short = pltpu.make_async_copy(short.at[jnp.maximum(target - 2, 0)], part, sems.at[delta])
        pl.when(target < 2)(from_long.start)
        pl.when(target >= 2)(from_short.start)
        waits.append(from_long.wait)
    return waits


def split_kernel(info, x_short, x_long, *refs):
    for wait in split_rows(info, x_short, x_long, refs[:-1], refs[-1]):
        wait()


def fetch(pairs, sems, parts, first):
    waits = []
    for source, target in pairs:
        step = target.shape[0] // parts
        for part in range(parts):
            rows = pl.ds(part * step, step)
            copy = pltpu.make_async_copy(source.at[rows], target.at[rows], sems.at[first + len(waits)])
            copy.start()
            waits.append(copy.wait)
    return waits


def load_kernel(info, table, w_qkv, w_out, w_up, w_down, cot_short, cot_long, *refs):
    sources = (table.at[0], table.at[1], *(w_qkv.at[0], w_out.at[0], w_up.at[0], w_down.at[0]))
    targets = (refs[0].at[0], refs[0].at[1], *refs[1:5])
    waits = fetch(zip(sources, targets), refs[12], 4, 0)
    late = zip((w_qkv.at[1], w_out.at[1], w_up.at[1]), refs[5:8])
    waits += fetch(late, refs[12], 4, len(waits))
    waits += split_rows(info, cot_short, cot_long, refs[8:12], refs[13])
    for wait in waits:
        wait()


def load_late_kernel(info, w_down, target, sems):
    for wait in fetch(((w_down.at[1], target),), sems, 4, 0):
        wait()


def copy_kernel(info, *refs):
    count = len(refs) // 2
    for at in range(count):
        refs[count + at][...] = refs[at][...]


def pack_kernel(info, act, grad, kept, sent):
    size = kept.shape[1] // 2
    chip = info[ME] // 2
    for ref, target in ((sent, 1 - chip), (kept, chip)):
        for core in range(2):
            rows = pl.ds(aligned((2 * target + core) * size, size), size)
            ref[core, :size, :] = act[rows, :]
            ref[core, size:, :] = grad[rows, :]


def swap_kernel(info, kept, got, sent):
    core = info[ME] % 2
    sent[0] = kept[1 - core]
    sent[1] = got[1 - core]


def join_kernel(info, kept, got, swapped, act_short, act_long, grad_short, grad_long):
    size = kept.shape[1] // 2
    core = info[ME] % 2
    for delta, (part, at) in enumerate(((kept, core), (swapped, 0), (got, core), (swapped, 1))):
        source = info[ME] ^ delta
        for short, long, rows in ((act_short, act_long, slice(0, size)), (grad_short, grad_long, slice(size, 2 * size))):

            @pl.when(source < 2)
            def _():
                long[0, pl.ds(aligned(jnp.minimum(source, 1) * size, size), size), :] = part[at, rows, :]

            @pl.when(source >= 2)
            def _():
                short[jnp.maximum(source - 2, 0)] = part[at, rows, :]


def front_kernel(info, r0, r1, r2, r3, table, w_qkv, hidden, rounded, query, kv):
    size = r0.shape[0]
    core = info[ME] % 2
    for delta, ref in enumerate((r0, r1, r2, r3)):
        block = info[ME] ^ delta
        start = block_start(info, block, core, size)
        rows = ref[...].astype(F32) + table[0, pl.ds(start, size), :].astype(F32)
        hidden[pl.ds(aligned(block * size, size), size), :] = rows
    low = hidden[...].astype(BF16)
    rounded[...] = low
    project(low, w_qkv, query, kv)


def with_live(info, len_short, len_long):
    me = info[ME]
    live = jnp.where(me < 2, len_long[0], len_short[jnp.maximum(me - 2, 0)])
    return (me, live, info[DP])


def first_kernel(
    info, len_short, len_long, query, kv_near, kv_far, hidden, rounded, table, gains, shifts, w_out, w_up, w_down, w_next,
    probs_near, probs_far, slope, kept_x, units, scales, hidden_next, rounded_next, query_next, kv_next,
    bias_near, bias_far,
):
    width, inner = w_up.shape
    size = query.shape[0] // 4
    info = with_live(info, len_short, len_long)
    fill_bias(info, bias_near, bias_far, size)
    attended = kept_x.at[:, inner + width : inner + 2 * width]
    attend_forward(query, kv_near, kv_far, bias_near, bias_far, probs_near, probs_far, attended)
    kept_x[:, inner + 2 * width :] = rounded[...]
    result = tail_forward(
        hidden, attended, w_out, w_up, w_down, gains[0], shifts[0],
        kept_x.at[:, :inner], slope, kept_x.at[:, inner : inner + width], units, scales,
    ).astype(BF16).astype(F32)
    add_table(info, table, 1, lambda block: result[block * size : (block + 1) * size], hidden_next)
    low = hidden_next[...].astype(BF16)
    rounded_next[...] = low
    project(low, w_next, query_next, kv_next)


def second_kernel(
    info, len_short, len_long, query, kv_near, kv_far, hidden, rounded, gains, shifts, w_out, w_up, w_down,
    probs_near, probs_far, slope, kept_x, units, scales, result, bias_near, bias_far,
):
    width, inner = w_up.shape
    info = with_live(info, len_short, len_long)
    fill_bias(info, bias_near, bias_far, query.shape[0] // 4)
    attended = kept_x.at[:, inner + width : inner + 2 * width]
    attend_forward(query, kv_near, kv_far, bias_near, bias_far, probs_near, probs_far, attended)
    kept_x[:, inner + 2 * width :] = rounded[...]
    result[...] = tail_forward(
        hidden, attended, w_out, w_up, w_down, gains[1], shifts[1],
        kept_x.at[:, :inner], slope, kept_x.at[:, inner : inner + width], units, scales,
    ).astype(BF16)


def turn_kernel(
    info, c0, c1, c2, c3, gains, slope, units, scales, w_out, w_up, w_down,
    bx_kept, bx_sent, norm_grads, d_first, d_att, cot, every,
):
    size = c0.shape[0]
    for delta, cot_part in enumerate((c0, c1, c2, c3)):
        rows = pl.ds(aligned((info[ME] ^ delta) * size, size), size)
        cot[rows, :] = cot_part[...].astype(F32)
    tail_backward(
        info, cot[...], w_out, w_up, w_down, gains[1], slope, units, scales,
        bx_kept, bx_sent, norm_grads, d_first, d_att, every,
    )


def attend_back_kernel(unused, query, kv_near, kv_far, probs_near, probs_far, d_att, d_query, d_kv_near, d_kv_far):
    attend_backward(query, kv_near, kv_far, probs_near, probs_far, d_att, d_query, d_kv_near, d_kv_far)


def close_layer(info, d_query, d_kv, d_kv_far, d_first, w_qkv, kept, sent, every):
    shards = 4
    width = d_query.shape[1]
    total = (d_kv[...].astype(F32) + d_kv_far[...].astype(F32)).astype(BF16)
    d_qkv = jnp.concatenate([d_query[...], total], axis=1)
    d_hidden = d_first[...] + dot_nt(d_qkv, w_qkv[...])
    low = d_hidden.astype(BF16)
    step, part = 3 * width // shards, width // shards
    for at in range(shards):
        every[at, :, :step] = d_qkv[:, at * step : (at + 1) * step]
        every[at, :, step:] = low[:, at * part : (at + 1) * part]
    part_ways(info, every, kept, sent)
    return d_hidden, low


def middle_kernel(
    info, d_query, d_kv, d_kv_far, d_first, w_qkv, gains, slope, units, scales, w_out, w_up, w_down, norms_late,
    qx_kept, qx_sent, bx_kept, bx_sent, norm_grads, d_first_out, d_att, every_qx, every_bx,
):
    d_hidden, unused = close_layer(info, d_query, d_kv, d_kv_far, d_first, w_qkv, qx_kept, qx_sent, every_qx)
    norm_grads[4:, :] = norms_late[...]
    tail_backward(
        info, d_hidden, w_out, w_up, w_down, gains[0], slope, units, scales,
        bx_kept, bx_sent, norm_grads, d_first_out, d_att, every_bx,
    )


def last_kernel(info, d_query, d_kv, d_kv_far, d_first, w_qkv, norms, qx_kept, qx_sent, grad, every):
    unused, low = close_layer(info, d_query, d_kv, d_kv_far, d_first, w_qkv, qx_kept, qx_sent, every)
    grad[...] = low
    tokens = d_query.shape[0]
    padded = jnp.concatenate([norms[...], jnp.zeros(norms.shape, F32)], axis=0)
    qx_sent[0, tokens:, :] = padded.astype(BF16)
    qx_sent[1, tokens:, :] = jnp.zeros(padded.shape, BF16)


def split_blocks(info, places, whole_ref, kept, sent):
    def split(place):
        bit, axis, at = place
        mine = (info[axis] >> at) & 1
        for ref, value in ((sent, 1 - mine), (kept, mine)):
            for index in range(ref.shape[0]):
                low = index & ((1 << bit) - 1)
                source = ((index >> bit) << (bit + 1)) + low + (value << bit)
                total = whole_ref[0][source]
                for other in whole_ref[1:]:
                    total = total + other[source]
                ref[index] = total

    if places[0] == places[1]:
        split(places[0])
    else:
        for core in range(2):
            pl.when(info[ME] % 2 == core)(functools.partial(split, places[core]))


def fold_kernel(places, info, kept, got, new_kept, new_sent):
    split_blocks(info, places, (kept, got), new_kept, new_sent)


def put(pieces, whole, name, x, value):
    for at, (tiles, unused) in enumerate(pieces):
        if name in tiles:
            lanes = value.shape[2]
            start = tiles.index(name) * lanes
            n_dp = value.shape[0]
            whole[at][x * n_dp : (x + 1) * n_dp, :, start : start + lanes] = value.astype(BF16)


def by_blocks(value, n_dp):
    return value.reshape(n_dp, value.shape[0] // n_dp, value.shape[1])


def feed_grad_kernel(pieces, info, x_near, x_far, b_near, b_far, *refs):
    count = len(pieces)
    outs, whole = refs[: 2 * count], refs[2 * count :]
    n_dp, rows = outs[0].shape[0], outs[0].shape[1]
    width = n_dp * rows
    inner = x_near.shape[1] - 3 * width
    step, part = inner // 4, width // 4
    for x in range(2):
        total = dot_tn(x_near[:, inner : inner + width], b_near[x, :, :step])
        total = total + dot_tn(x_far[:, inner : inner + width], b_far[x, :, :step])
        for tile in range(step // part):
            put(pieces, whole, ("up", tile), x, by_blocks(total[:, tile * part : (tile + 1) * part], n_dp))
    feeds = [
        jnp.concatenate([ref[0, :, step : step + part], ref[1, :, step : step + part]], axis=1)
        for ref in (b_near, b_far)
    ]
    span_size = 512
    fold = inner // width
    for at in range(inner // span_size):
        span = slice(at * span_size, (at + 1) * span_size)
        total = dot_tn(feeds[0], x_near[:, span]) + dot_tn(feeds[1], x_far[:, span])
        total = total.astype(BF16).T if rows % 16 == 0 else total.T
        for group in range(span_size // rows):
            block, tile = divmod(at * (span_size // rows) + group, fold)
            for index, (tiles, unused) in enumerate(pieces):
                if ("down", tile) in tiles:
                    start = tiles.index(("down", tile)) * part
                    for x in range(2):
                        value = total[group * rows : (group + 1) * rows, x * part : (x + 1) * part]
                        whole[index][x * n_dp + block, :, start : start + part] = value.astype(BF16)
    for at, (unused, places) in enumerate(pieces):
        split_blocks(info, places, (whole[at],), outs[2 * at], outs[2 * at + 1])


def attend_grad_kernel(pieces, with_norms, info, x_near, x_far, b_near, b_far, q_near, q_far, *refs):
    count = len(pieces)
    norms = None
    if with_norms:
        norms, refs = refs[0], refs[1:]
    outs, whole, table = refs[: 2 * count], refs[2 * count : -1], refs[-1]
    n_dp, rows = outs[0].shape[0], outs[0].shape[1]
    width = n_dp * rows
    part = width // 4
    tokens = x_near.shape[0]
    inner = x_near.shape[1] - 3 * width
    step = 3 * part
    feed = inner // 4 + part
    skip = q_near.shape[2] - width
    core = info[ME] % 2
    size = tokens // 4
    for x in range(2):
        lows = slice(inner + 2 * width, inner + 3 * width)
        total = dot_tn(x_near[:, lows], q_near[x, :, skip : skip + step])
        total = total + dot_tn(x_far[:, lows], q_far[x, :tokens, skip : skip + step])
        for tile in range(step // part):
            put(pieces, whole, ("qkv", tile), x, by_blocks(total[:, tile * part : (tile + 1) * part], n_dp))
        outs_at = slice(inner + width, inner + 2 * width)
        total = dot_tn(x_near[:, outs_at], b_near[x, :, feed : feed + part])
        total = total + dot_tn(x_far[:, outs_at], b_far[x, :, feed : feed + part])
        put(pieces, whole, ("out", 0), x, by_blocks(total, n_dp))
        table[...] = jnp.zeros_like(table)
        for source, place in ((q_near, core), (q_far, 1 - core)):
            for block in range(4):
                span = pl.ds(block_start(info, block, place, size), size)
                table[span, :] += source[x, block * size : (block + 1) * size, skip + step :].astype(F32)
        put(pieces, whole, ("pos", 0), x, by_blocks(table[...], n_dp))
    if with_norms:
        sums = norms[...] + q_far[0, tokens:, :].astype(F32)[: norms.shape[0]]
        share = width // n_dp
        for block in range(n_dp):
            value = sums[:, block * share : (block + 1) * share]
            value = jnp.concatenate([value, jnp.zeros((value.shape[0], part - share), F32)], axis=1)
            if rows > value.shape[0]:
                value = jnp.concatenate([value, jnp.zeros((rows - value.shape[0], part), F32)], axis=0)
            for at, (tiles, unused) in enumerate(pieces):
                if ("norm", 0) in tiles:
                    start = tiles.index(("norm", 0)) * part
                    for x in range(2):
                        whole[at][x * n_dp + block, :, start : start + part] = value.astype(BF16)
    for at, (unused, places) in enumerate(pieces):
        split_blocks(info, places, (whole[at],), outs[2 * at], outs[2 * at + 1])


def final_kernel(pieces, info, *refs):
    ins, (*sums, gain, shift) = refs[: 2 * len(pieces)], refs[2 * len(pieces) :]
    outs = dict(zip(("qkv", "out", "up", "down", "pos"), sums))
    for at, (layer_at, tiles) in enumerate(pieces):
        kept, got = ins[2 * at], ins[2 * at + 1]
        rows = kept.shape[1]
        part = outs["out"].shape[2]
        for index, (name, tile) in enumerate(tiles):
            lanes = slice(index * part, (index + 1) * part)
            total = kept[0, :, lanes].astype(F32) + got[0, :, lanes].astype(F32)
            if name == "norm":
                share = gain.shape[2]
                for row in range(8):
                    ref = (gain, shift)[row // 2 % 2]
                    ref[row // 4, row % 2 : row % 2 + 1, :] = total[row : row + 1, :share]
            elif name == "down":
                outs[name][layer_at, tile * rows : (tile + 1) * rows, :] = total
            else:
                outs[name][layer_at, :, tile * part : (tile + 1) * part] = total


MB = 1024 * 1024
TOKEN = ((8, 128), F32)
SMEM = pl.BlockSpec(memory_space=pltpu.SMEM)
VMEM = pl.BlockSpec(memory_space=pltpu.VMEM)
HBM = pl.BlockSpec(memory_space=pltpu.HBM)

FLOPS = 10**10
COSTS = dict(feed1=0, middle=0, back=0, rest1=0, feed0=0, last=0, rest0=0, fold=10000000000, pack=0, tick=0)


def pin(array):
    return pltpu.with_memory_space_constraint(array, pltpu.VMEM)


class Line:
    def __init__(self):
        self.token = None
        self.trail = []
        self.used = set()

    def flip(self, array, axis, bit):
        size = lax.axis_size(axis)
        self.trail.append(lax.ppermute(array, axis, [(at, at ^ bit) for at in range(size)]))
        return self.trail[-1]

    def cross(self, array, steps):
        n_dp, n_seq = lax.axis_size("dp"), lax.axis_size("seq")
        pairs = []
        for dp in range(n_dp):
            for seq in range(n_seq):
                step = steps[seq % 2]
                other = (dp, seq ^ 2) if step == "x" else (dp ^ (1 << step), seq)
                pairs.append((dp * n_seq + seq, other[0] * n_seq + other[1]))
        self.trail.append(lax.ppermute(array, ("dp", "seq"), pairs))
        return self.trail[-1]

    def near(self, array):
        return self.flip(array, "seq", 1)

    def gather(self, parts):
        return [parts[0]] + [self.flip(parts[delta], "seq", delta) for delta in (1, 2, 3)]

    def past(self, used=True):
        return [array for array in self.trail if (id(array) in self.used) == used]

    def tick(self, after=()):
        self.call("tick", lambda info: None, [], (), after=after)

    def call(self, name, kernel, outs, args, scratch=(), limit=8, smem=0, hbm=0, final=False, after=(), past=()):
        self.used.update(id(arg) for arg in (*args, *after))
        tokens = [] if self.token is None else [self.token]
        skip = len(past)
        shapes = [jax.ShapeDtypeStruct(*kind) if final else pltpu.VMEM(*kind) for kind in outs] + [pltpu.VMEM(*TOKEN)]
        count, extra = len(args), len(tokens) + len(after)

        def body(*refs):
            refs = refs[skip:]
            given = refs[:count]
            made = refs[count + extra : count + extra + len(outs)]
            refs[count + extra + len(outs)][...] = jnp.zeros(TOKEN[0], F32)
            info = (lax.axis_index("seq"), None, lax.axis_index("dp"))
            kernel(info, *given, *made, *refs[count + extra + len(outs) + 1 :])

        far = smem + hbm
        operands = [pin(array) for array in past] + list(args[:smem]) + [pltpu.with_memory_space_constraint(arg, pltpu.HBM) for arg in args[smem:far]]
        operands += [pin(arg) for arg in args[far:]]
        operands += [pin(array) for array in (*after, *tokens)]
        results = pl.pallas_call(
            body,
            in_specs=[VMEM] * skip + [SMEM] * smem + [HBM] * hbm + [VMEM] * (count - far + extra),
            out_specs=[VMEM] * (len(outs) + 1),
            out_shape=shapes,
            scratch_shapes=list(scratch),
            compiler_params=pltpu.CompilerParams(vmem_limit_bytes=limit * MB),
            cost_estimate=pl.CostEstimate(flops=COSTS.get(name, FLOPS), bytes_accessed=0, transcendentals=0),
            name=name,
        )(*operands)
        self.token = results[-1]
        return list(results[:-1])


FEED = tuple(("up", at) for at in range(4)) + tuple(("down", at) for at in range(4))
REST = (("qkv", 0), ("qkv", 1), ("qkv", 2), ("out", 0), ("pos", 0))
LAST = REST + (("norm", 0),)
PIECES = dict(
    a=(1, "feed1", FEED, "xyhl", "lhyx"),
    b=(1, "rest1", REST, "yxhl", "yhlx"),
    c=(0, "feed0", FEED, "lxyh", "xlhy"),
    d=(0, "rest0", LAST, "yxlh", "xlyh"),
)
ORDER = (
    "feed1", "middle", "back", "feed0", "rest1", "last", "a", "rest0", "c", "b", "a", "pack", "d", "c", "swap", "b",
    "d", "c", "a", "d", "take", "b",
)


class Sum:
    def __init__(self, name, n_bits):
        self.layer_at, self.maker, self.tiles, *paths = PIECES[name]
        letters = {"x": ["x"], "y": [0], "l": [1], "h": list(range(2, n_bits))}
        self.steps = [[bit for letter in path for bit in letters[letter] if bit == "x" or bit < n_bits] for path in paths]
        self.bits = [[*range(n_bits), "x"] for unused in paths]

    def left(self):
        return len(self.steps[0])

    def place(self):
        places = []
        for steps, bits in zip(self.steps, self.bits):
            where = bits.index(steps[0])
            places.append((where, ME, 1) if steps[0] == "x" else (where, DP, steps[0]))
        return places

    def start(self, line, kept, sent):
        now = [steps.pop(0) for steps in self.steps]
        for bits, step in zip(self.bits, now):
            bits.remove(step)
        self.kept = kept
        self.got = line.cross(sent, now)

    def fold(self, line):
        blocks, rows, columns = self.kept.shape
        kind = ((blocks // 2, rows, columns), BF16)
        self.start(line, *line.call("fold", functools.partial(fold_kernel, self.place()), [kind, kind], (self.kept, self.got)))


def local(
    x_short, x_long, len_short, len_long, w_qkv, w_out, w_up, w_down, pos_table, norm_gain, norm_bias, cot_short, cot_long
):
    n_dp = lax.axis_size("dp")
    n_bits = n_dp.bit_length() - 1
    width = x_short.shape[2]
    size = x_short.shape[1]
    tokens = 4 * size
    half = tokens // 2
    inner = w_up.shape[2]
    pairs = width // (2 * HD)
    rows = width // n_dp
    part = ((size, width), BF16)
    hidden_kind = ((tokens, width), F32)
    low_kind = ((tokens, width), BF16)
    kv_kind = ((tokens, 2 * width), BF16)
    probs_kinds = [((pairs, 2 * half, 2 * half), BF16), ((pairs, 4 * half, 2 * half), BF16)]
    slope_kind = ((tokens, inner), BF16)
    x_kind = ((tokens, inner + 3 * width), BF16)
    units_kind = ((2, tokens, width), F32)
    scales_kind = ((2, tokens, 1), F32)
    bx_kind = ((2, tokens, inner // 4 + width // 2), BF16)
    qx_kind = ((2, tokens, width), BF16)
    every_bx = pltpu.VMEM((4, *bx_kind[0][1:]), BF16)
    every_qx = pltpu.VMEM((4, *qx_kind[0][1:]), BF16)
    biases = [pltpu.VMEM((2 * half, half), F32), pltpu.VMEM((4 * half, half), F32)]
    lens = (len_short, len_long)
    line = Line()
    sums = {name: Sum(name, n_bits) for name in PIECES}

    four = [pltpu.SemaphoreType.DMA((4,))]
    rows_in = line.gather(line.call("split", split_kernel, [part] * 4, (x_short, x_long), four, hbm=2))
    stacks = (w_qkv, w_out, w_up, w_down)
    kinds = [(array.shape[1:], BF16) for array in stacks]
    loaded = line.call(
        "load", load_kernel, [(pos_table.shape, BF16)] + kinds + kinds[:3] + [part] * 4,
        (pos_table, *stacks, cot_short, cot_long), [pltpu.SemaphoreType.DMA((36,))] + four, hbm=7,
    )
    table, w_qkv0, w_out0, w_up0, w_down0, w_qkv1, w_out1, w_up1, *cots = loaded
    hidden0, rounded0, query0, kv0 = line.call(
        "front", front_kernel, [hidden_kind, low_kind, low_kind, kv_kind], (*rows_in, table, w_qkv0)
    )
    kv0_far = line.near(kv0)
    (w_down1,) = line.call("load", load_late_kernel, [kinds[3]], (w_down,), four, hbm=1)
    layer_kinds = probs_kinds + [slope_kind, x_kind, units_kind, scales_kind]
    probs_near0, probs_far0, slope0, x0, units0, scales0, hidden1, rounded1, query1, kv1 = line.call(
        "first", first_kernel, layer_kinds + [hidden_kind, low_kind, low_kind, kv_kind],
        (
            *lens, query0, kv0, kv0_far, hidden0, rounded0, table, norm_gain, norm_bias,
            w_out0, w_up0, w_down0, w_qkv1,
        ),
        biases, limit=16, smem=2,
    )
    kv1_far = line.near(kv1)
    cot_in = line.gather(line.call("copy", copy_kernel, [part] * 4, cots))
    x0_far = line.near(x0)
    probs_near1, probs_far1, slope1, x1, units1, scales1, act = line.call(
        "second", second_kernel, layer_kinds + [low_kind],
        (*lens, query1, kv1, kv1_far, hidden1, rounded1, norm_gain, norm_bias, w_out1, w_up1, w_down1),
        biases, limit=16, smem=2,
    )
    x1_far = line.near(x1)
    bx1, bx1_sent, norms1, d_first1, d_att1 = line.call(
        "turn", turn_kernel, [bx_kind, bx_kind, ((4, width), F32), hidden_kind, low_kind],
        (*cot_in, norm_gain, slope1, units1, scales1, w_out1, w_up1, w_down1), [pltpu.VMEM(*hidden_kind), every_bx],
    )
    bx1_far = line.near(bx1_sent)

    def grads(maker, kernel, args, scratch=()):
        made = [each for each in sums.values() if each.maker == maker]
        pieces = [(each.tiles, each.place()) for each in made]
        columns = [len(each.tiles) * (width // 4) for each in made]
        outs = line.call(
            maker, functools.partial(kernel, pieces),
            [((n_dp, rows, count), BF16) for count in columns for unused in range(2)],
            args, [pltpu.VMEM((2 * n_dp, rows, count), BF16) for count in columns] + list(scratch), limit=12,
        )
        for at, each in enumerate(made):
            each.start(line, outs[2 * at], outs[2 * at + 1])

    table = [pltpu.VMEM((width, width // 4), F32)]
    back_kinds = [low_kind, kv_kind, kv_kind]
    d_query1, d_kv1, d_kv1_sent = line.call(
        "attend_back", attend_back_kernel, back_kinds, (query1, kv1, kv1_far, probs_near1, probs_far1, d_att1), after=[x0_far]
    )
    d_kv1_far = line.near(d_kv1_sent)
    latest = None
    order = list(ORDER)
    while order or any(each.left() for each in sums.values()):
        if not order:
            order = [name for name, each in sums.items() if each.left()]
        task = order.pop(0)
        if task in sums:
            if sums[task].left():
                if task == latest:
                    line.tick()
                sums[task].fold(line)
                latest = task
        elif task == "tick":
            line.tick()
        elif task == "feed1":
            grads("feed1", feed_grad_kernel, (x1, x1_far, bx1, bx1_far))
        elif task == "middle":
            qx1, qx1_sent, bx0, bx0_sent, norms, d_first0, d_att0 = line.call(
                "middle", middle_kernel, [qx_kind, qx_kind, bx_kind, bx_kind, ((8, width), F32), hidden_kind, low_kind],
                (
                    d_query1, d_kv1, d_kv1_far, d_first1, w_qkv1, norm_gain, slope0, units0, scales0, w_out0, w_up0, w_down0,
                    norms1,
                ),
                [every_qx, every_bx],
            )
            bx0_far = line.near(bx0_sent)
            qx1_far = line.near(qx1_sent)
        elif task == "back":
            d_query0, d_kv0, d_kv0_sent = line.call(
                "back", attend_back_kernel, back_kinds, (query0, kv0, kv0_far, probs_near0, probs_far0, d_att0)
            )
            d_kv0_far = line.near(d_kv0_sent)
        elif task == "rest1":
            grads(
                "rest1", lambda pieces, *refs: attend_grad_kernel(pieces, False, *refs),
                (x1, x1_far, bx1, bx1_far, qx1, qx1_far), table,
            )
        elif task == "feed0":
            grads("feed0", feed_grad_kernel, (x0, x0_far, bx0, bx0_far))
        elif task == "last":
            longer = ((2, tokens + 16, width), BF16)
            qx0, qx0_sent, grad = line.call(
                "last", last_kernel, [qx_kind, longer, low_kind], (d_query0, d_kv0, d_kv0_far, d_first0, w_qkv0, norms),
                [every_qx],
            )
            qx0_far = line.near(qx0_sent)
        elif task == "rest0":
            grads(
                "rest0", lambda pieces, *refs: attend_grad_kernel(pieces, True, *refs),
                (x0, x0_far, bx0, bx0_far, qx0, qx0_far, norms), table,
            )
        elif task == "pack":
            own_rows, rows_sent = line.call("pack", pack_kernel, [((2, 2 * size, width), BF16)] * 2, (act, grad))
            chip_rows = line.flip(rows_sent, "seq", 2)
        elif task == "swap":
            (rows_sent,) = line.call("pack", swap_kernel, [((2, 2 * size, width), BF16)], (own_rows, chip_rows))
            core_rows = line.near(rows_sent)
        elif task == "take":
            line.tick(after=[core_rows])
    joined = line.call(
        "join", join_kernel, [(x_short.shape, BF16), (x_long.shape, BF16)] * 2, (own_rows, chip_rows, core_rows), final=True,
        past=line.past(),
    )
    shard = ((LAYERS, rows, width // 4), F32)
    totals = line.call(
        "final", functools.partial(final_kernel, [(each.layer_at, each.tiles) for each in sums.values()]),
        [
            ((LAYERS, rows, 3 * width // 4), F32), shard, ((LAYERS, rows, inner // 4), F32),
            ((LAYERS, inner // n_dp, width // 4), F32), shard,
            ((LAYERS, 2, rows), F32), ((LAYERS, 2, rows), F32),
        ],
        [array for each in sums.values() for array in (each.kept, each.got)], final=True, past=line.past(False),
    )
    return (*joined, *totals)


def solution(mesh):
    rows = P("dp", "seq", None)
    grads = P(None, "dp", "seq")
    norms = P(None, None, "dp")
    return jax.shard_map(
        local,
        mesh=mesh,
        in_specs=(rows, rows, P("dp"), P("dp")) + (P(),) * 7 + (rows, rows),
        out_specs=(rows,) * 4 + (grads,) * 5 + (norms, norms),
        check_vma=False,
    )
```

```python
import functools

import jax
import jax.numpy as jnp
from jax import lax
from jax.experimental import pallas as pl
from jax.experimental.pallas import tpu as pltpu
from jax.sharding import PartitionSpec as P

LAYERS = 2
HD = 64
F32 = jnp.float32
BF16 = jnp.bfloat16
NEG = -1000000000.0


def dot(left, right):
    return lax.dot_general(left, right, (((1,), (0,)), ((), ())), preferred_element_type=F32)


def dot_nt(left, right):
    return lax.dot_general(left, right, (((1,), (1,)), ((), ())), preferred_element_type=F32)


def dot_tn(left, right):
    return lax.dot_general(left, right, (((0,), (0,)), ((), ())), preferred_element_type=F32)


ME, LIVE, DP = 0, 1, 2


def aligned(value, step):
    return pl.multiple_of(value, step)


def block_start(info, block, core, size):
    is_long = info[ME] < 2
    return aligned(jnp.where(is_long, (2 * block + core) * size, block * size), size)


def norm_forward(values, gain, shift):
    centre = jnp.mean(values, axis=-1, keepdims=True)
    centred = values - centre
    spread = jnp.mean(centred * centred, axis=-1, keepdims=True)
    scale = lax.rsqrt(spread + 1e-05)
    unit = centred * scale
    return unit, scale, unit * gain + shift


def norm_backward(unit, scale, gain, gradient):
    d_gain = jnp.sum(gradient * unit, axis=0, keepdims=True)
    d_shift = jnp.sum(gradient, axis=0, keepdims=True)
    scaled = gradient * gain
    mean_one = jnp.mean(scaled, axis=-1, keepdims=True)
    mean_two = jnp.mean(scaled * unit, axis=-1, keepdims=True)
    return scale * (scaled - mean_one - unit * mean_two), d_gain, d_shift


def positions(info, rows, core, size):
    is_long = info[ME] < 2
    spread = (rows // size) * (2 * size) + core * size + rows % size
    return jnp.where(is_long, spread, rows)


def fill_bias(info, bias_near, bias_far, size):
    core = info[ME] % 2
    is_long = info[ME] < 2
    half = bias_near.shape[1]
    for at, ref in ((0, bias_near), (1, bias_far)):
        queries = positions(info, lax.broadcasted_iota(jnp.int32, (half, half), 1) + at * half, core, size)
        for part in range(2 * (at + 1)):
            rows = lax.broadcasted_iota(jnp.int32, (half, half), 0) + (part // 2) * half
            if part % 2 == 0:
                keys = positions(info, rows, core, size)
            else:
                keys = jnp.where(is_long, positions(info, rows, 1 - core, size), 1 << 20)
            allowed = (keys <= queries) & (keys < info[LIVE])
            ref[pl.ds(part * half, half), :] = jnp.where(allowed, 0.0, NEG)


def interleave(near, far, columns, half):
    return jnp.concatenate(
        [near[:half, columns], far[:half, columns], near[half:, columns], far[half:, columns]], axis=0
    )


def lane_masks(half):
    lanes = lax.broadcasted_iota(jnp.int32, (half, 2 * HD), 1)
    first = jnp.where(lanes < HD, 1.0, 0.0).astype(BF16)
    return first, (1.0 - first.astype(F32)).astype(BF16)


def both_heads(rows, masks):
    return jnp.concatenate([rows * masks[0], rows * masks[1]], axis=0)


def attend_forward(query, kv_near, kv_far, bias_near, bias_far, probs_near, probs_far, attended):
    width = query.shape[1]
    half = query.shape[0] // 2
    masks = lane_masks(half)

    def scores_of(pair, at):
        columns = slice(pair * 2 * HD, (pair + 1) * 2 * HD)
        bias = (bias_near, bias_far)[at]
        keys = interleave(kv_near, kv_far, columns, half)
        pair_query = both_heads(query[pl.ds(at * half, half), columns], masks)
        return dot_nt(keys[: bias.shape[0]], pair_query) + jnp.concatenate([bias[...], bias[...]], axis=1)

    def finish(pair, at, softened):
        columns = slice(pair * 2 * HD, (pair + 1) * 2 * HD)
        values = interleave(kv_near, kv_far, slice(columns.start + width, columns.stop + width), half)
        turned = dot_tn(values[: softened.shape[0]], softened)
        turned = jnp.concatenate([turned[:HD, :half], turned[HD:, half:]], axis=0)
        attended[pl.ds(at * half, half), columns] = turned.T.astype(BF16)

    units = [(pair, at) for pair in range(width // (2 * HD)) for at in range(2)]
    ready = scores_of(*units[0])
    waiting = None
    for index, (pair, at) in enumerate(units):
        scores = ready
        if index + 1 < len(units):
            ready = scores_of(*units[index + 1])
        if waiting is not None:
            finish(*waiting)
        peak = jnp.max(scores, axis=0, keepdims=True)
        lifted = jnp.exp(scores - peak)
        total = jnp.sum(lifted, axis=0, keepdims=True)
        softened = (lifted * (1.0 / total)).astype(BF16)
        (probs_near, probs_far)[at][pair] = softened
        waiting = (pair, at, softened)
    finish(*waiting)


def attend_backward(query, kv_near, kv_far, probs_near, probs_far, d_att, d_query, d_kv_near, d_kv_far):
    width = query.shape[1]
    half = query.shape[0] // 2
    masks = lane_masks(half)

    def d_probs_of(pair, at):
        columns = slice(pair * 2 * HD, (pair + 1) * 2 * HD)
        values = interleave(kv_near, kv_far, slice(columns.start + width, columns.stop + width), half)
        pair_grad = both_heads(d_att[pl.ds(at * half, half), columns], masks)
        return pair_grad, dot_nt(values[: (probs_near, probs_far)[at].shape[1]], pair_grad)

    def finish(pair, at, pair_grad, softened, d_scores):
        columns = slice(pair * 2 * HD, (pair + 1) * 2 * HD)
        keys = interleave(kv_near, kv_far, columns, half)
        pair_query = both_heads(query[pl.ds(at * half, half), columns], masks)
        parts[at] = (dot(d_scores, pair_query), dot(softened, pair_grad))
        turned = dot_tn(keys[: softened.shape[0]], d_scores)
        turned = jnp.concatenate([turned[:HD, :half], turned[HD:, half:]], axis=0)
        d_query[pl.ds(at * half, half), columns] = (turned.T * (1.0 / HD**0.5)).astype(BF16)
        if at == 1:
            for kind, start in ((0, columns.start), (1, columns.start + width)):
                place = slice(start, start + 2 * HD)
                first = (parts[0][kind] + parts[1][kind][: 2 * half]).astype(BF16)
                second = parts[1][kind][2 * half :].astype(BF16)
                d_kv_near[:half, place] = first[:half]
                d_kv_far[:half, place] = first[half:]
                d_kv_near[half:, place] = second[:half]
                d_kv_far[half:, place] = second[half:]

    units = [(pair, at) for pair in range(width // (2 * HD)) for at in range(2)]
    parts = {}
    ready = d_probs_of(*units[0])
    waiting = None
    for index, (pair, at) in enumerate(units):
        pair_grad, d_probs = ready
        if index + 1 < len(units):
            ready = d_probs_of(*units[index + 1])
        if waiting is not None:
            finish(*waiting)
        softened = (probs_near, probs_far)[at][pair]
        probs = softened.astype(F32)
        row_sum = jnp.sum(probs * d_probs, axis=0, keepdims=True)
        waiting = (pair, at, pair_grad, softened, (probs * (d_probs - row_sum)).astype(BF16))
    finish(*waiting)


def project(rounded, w_qkv, query, kv):
    width = query.shape[1]
    for at in range(3):
        mixed = dot(rounded, w_qkv[:, at * width : (at + 1) * width]).astype(BF16)
        if at == 0:
            query[...] = mixed * jnp.asarray(1.0 / HD**0.5, BF16)
        else:
            kv[:, (at - 1) * width : at * width] = mixed


def normal_area(value):
    area = 0.5 + 0.5 * lax.erf(value * (0.5**0.5))
    bell = jnp.exp(value * value * -0.5) * ((2.0 * jnp.pi) ** -0.5)
    return area, bell


def tail_forward(hidden, attended, w_out, w_up, w_down, gains, shifts, active, slope, settled_low, units, scales):
    inner_width = w_up.shape[1]
    step = 512
    pre_first = hidden[...] + dot(attended[...], w_out[...])
    unit, scale, settled = norm_forward(pre_first, gains[0], shifts[0])
    units[0], scales[0] = unit, scale
    rounded = settled.astype(BF16)
    settled_low[...] = rounded
    second = settled
    count = inner_width // step
    ready = dot(rounded, w_up[:, :step])
    for at in range(count):
        span = slice(at * step, (at + 1) * step)
        inner = ready
        if at + 1 < count:
            ready = dot(rounded, w_up[:, (at + 1) * step : (at + 2) * step])
        area, bell = normal_area(inner)
        glow = (inner * area).astype(BF16)
        active[:, span] = glow
        slope[:, span] = (area + inner * bell).astype(BF16)
        second = second + dot(glow, w_down[span, :])
    unit, scale, result = norm_forward(second, gains[1], shifts[1])
    units[1], scales[1] = unit, scale
    return result


def part_ways(info, every, kept, sent):
    core = info[ME] % 2
    for x in range(2):
        kept[x, : every.shape[1], :] = every[2 * x + core]
        sent[x, : every.shape[1], :] = every[2 * x + 1 - core]


def tail_backward(
    info, gradient, w_out, w_up, w_down, gains, slope, units, scales, kept, sent, norm_grads, d_first_out, d_att, every
):
    inner_width = w_up.shape[1]
    width = w_up.shape[0]
    shards = 4
    step, part = inner_width // shards, width // shards
    d_second, d_gain, d_shift = norm_backward(units[1], scales[1], gains[1], gradient)
    norm_grads[1:2, :] = d_gain
    norm_grads[3:4, :] = d_shift
    d_feed = d_second.astype(BF16)
    d_settled = d_second

    ready = dot_nt(d_feed, w_down[:step, :])
    for at in range(shards):
        span = slice(at * step, (at + 1) * step)
        d_active = ready
        if at + 1 < shards:
            ready = dot_nt(d_feed, w_down[(at + 1) * step : (at + 2) * step, :])
        d_inner = (d_active * slope[:, span].astype(F32)).astype(BF16)
        every[at, :, :step] = d_inner
        every[at, :, step : step + part] = d_feed[:, at * part : (at + 1) * part]
        d_settled = d_settled + dot_nt(d_inner, w_up[:, span])
    d_first, d_gain, d_shift = norm_backward(units[0], scales[0], gains[0], d_settled)
    norm_grads[0:1, :] = d_gain
    norm_grads[2:3, :] = d_shift
    d_first_out[...] = d_first
    d_branch = d_first.astype(BF16)
    for at in range(shards):
        every[at, :, step + part :] = d_branch[:, at * part : (at + 1) * part]
    d_att[...] = dot_nt(d_branch, w_out[...]).astype(BF16)
    part_ways(info, every, kept, sent)


def add_table(info, table, layer_at, get_rows, hidden):
    core = info[ME] % 2
    size = hidden.shape[0] // 4
    for block in range(4):
        start = block_start(info, block, core, size)
        rows = table[layer_at, pl.ds(start, size), :].astype(F32)
        hidden[block * size : (block + 1) * size, :] = get_rows(block) + rows


def split_rows(info, short, long, parts, sems):
    size = parts[0].shape[0]
    waits = []
    for delta, part in enumerate(parts):
        target = info[ME] ^ delta
        from_long = pltpu.make_async_copy(
            long.at[0, pl.ds(aligned(jnp.minimum(target, 1) * size, size), size), :], part, sems.at[delta]
        )
        from_short = pltpu.make_async_copy(short.at[jnp.maximum(target - 2, 0)], part, sems.at[delta])
        pl.when(target < 2)(from_long.start)
        pl.when(target >= 2)(from_short.start)
        waits.append(from_long.wait)
    return waits


def split_kernel(info, x_short, x_long, *refs):
    for wait in split_rows(info, x_short, x_long, refs[:-1], refs[-1]):
        wait()


def fetch(pairs, sems, parts, first):
    waits = []
    for source, target in pairs:
        step = target.shape[0] // parts
        for part in range(parts):
            rows = pl.ds(part * step, step)
            copy = pltpu.make_async_copy(source.at[rows], target.at[rows], sems.at[first + len(waits)])
            copy.start()
            waits.append(copy.wait)
    return waits


def load_kernel(info, table, w_qkv, w_out, w_up, w_down, cot_short, cot_long, *refs):
    sources = (table.at[0], table.at[1], *(w_qkv.at[0], w_out.at[0], w_up.at[0], w_down.at[0]))
    targets = (refs[0].at[0], refs[0].at[1], *refs[1:5])
    waits = fetch(zip(sources, targets), refs[11], 4, 0)
    late = zip((w_out.at[1], w_up.at[1]), refs[5:7])
    waits += fetch(late, refs[11], 4, len(waits))
    waits += split_rows(info, cot_short, cot_long, refs[7:11], refs[12])
    for wait in waits:
        wait()


def load_late_kernel(info, w_qkv, w_down, qkv, down, sems):
    for wait in fetch(((w_qkv.at[1], qkv), (w_down.at[1], down)), sems, 4, 0):
        wait()


def copy_kernel(info, *refs):
    count = len(refs) // 2
    for at in range(count):
        refs[count + at][...] = refs[at][...]


def pack_kernel(info, act, grad, kept, sent):
    size = kept.shape[1] // 2
    chip = info[ME] // 2
    for ref, target in ((sent, 1 - chip), (kept, chip)):
        for core in range(2):
            rows = pl.ds(aligned((2 * target + core) * size, size), size)
            ref[core, :size, :] = act[rows, :]
            ref[core, size:, :] = grad[rows, :]


def swap_kernel(info, kept, got, sent):
    core = info[ME] % 2
    sent[0] = kept[1 - core]
    sent[1] = got[1 - core]


def join_kernel(info, kept, got, swapped, act_short, act_long, grad_short, grad_long):
    size = kept.shape[1] // 2
    core = info[ME] % 2
    for delta, (part, at) in enumerate(((kept, core), (swapped, 0), (got, core), (swapped, 1))):
        source = info[ME] ^ delta
        for short, long, rows in ((act_short, act_long, slice(0, size)), (grad_short, grad_long, slice(size, 2 * size))):

            @pl.when(source < 2)
            def _():
                long[0, pl.ds(aligned(jnp.minimum(source, 1) * size, size), size), :] = part[at, rows, :]

            @pl.when(source >= 2)
            def _():
                short[jnp.maximum(source - 2, 0)] = part[at, rows, :]


def front_kernel(info, r0, r1, r2, r3, table, w_qkv, hidden, rounded, query, kv):
    size = r0.shape[0]
    core = info[ME] % 2
    for delta, ref in enumerate((r0, r1, r2, r3)):
        block = info[ME] ^ delta
        start = block_start(info, block, core, size)
        rows = ref[...].astype(F32) + table[0, pl.ds(start, size), :].astype(F32)
        hidden[pl.ds(aligned(block * size, size), size), :] = rows
    low = hidden[...].astype(BF16)
    rounded[...] = low
    project(low, w_qkv, query, kv)


def with_live(info, len_short, len_long):
    me = info[ME]
    live = jnp.where(me < 2, len_long[0], len_short[jnp.maximum(me - 2, 0)])
    return (me, live, info[DP])


def first_kernel(
    info, len_short, len_long, query, kv_near, kv_far, hidden, rounded, table, gains, shifts, w_out, w_up, w_down, w_next,
    probs_near, probs_far, slope, kept_x, units, scales, hidden_next, rounded_next, query_next, kv_next,
    bias_near, bias_far,
):
    width, inner = w_up.shape
    size = query.shape[0] // 4
    info = with_live(info, len_short, len_long)
    fill_bias(info, bias_near, bias_far, size)
    attended = kept_x.at[:, inner + width : inner + 2 * width]
    attend_forward(query, kv_near, kv_far, bias_near, bias_far, probs_near, probs_far, attended)
    kept_x[:, inner + 2 * width :] = rounded[...]
    result = tail_forward(
        hidden, attended, w_out, w_up, w_down, gains[0], shifts[0],
        kept_x.at[:, :inner], slope, kept_x.at[:, inner : inner + width], units, scales,
    ).astype(BF16).astype(F32)
    add_table(info, table, 1, lambda block: result[block * size : (block + 1) * size], hidden_next)
    low = hidden_next[...].astype(BF16)
    rounded_next[...] = low
    project(low, w_next, query_next, kv_next)


def second_kernel(
    info, len_short, len_long, query, kv_near, kv_far, hidden, rounded, gains, shifts, w_out, w_up, w_down,
    probs_near, probs_far, slope, kept_x, units, scales, result, bias_near, bias_far,
):
    width, inner = w_up.shape
    info = with_live(info, len_short, len_long)
    fill_bias(info, bias_near, bias_far, query.shape[0] // 4)
    attended = kept_x.at[:, inner + width : inner + 2 * width]
    attend_forward(query, kv_near, kv_far, bias_near, bias_far, probs_near, probs_far, attended)
    kept_x[:, inner + 2 * width :] = rounded[...]
    result[...] = tail_forward(
        hidden, attended, w_out, w_up, w_down, gains[1], shifts[1],
        kept_x.at[:, :inner], slope, kept_x.at[:, inner : inner + width], units, scales,
    ).astype(BF16)


def turn_kernel(
    info, c0, c1, c2, c3, gains, slope, units, scales, w_out, w_up, w_down,
    bx_kept, bx_sent, norm_grads, d_first, d_att, cot, every,
):
    size = c0.shape[0]
    for delta, cot_part in enumerate((c0, c1, c2, c3)):
        rows = pl.ds(aligned((info[ME] ^ delta) * size, size), size)
        cot[rows, :] = cot_part[...].astype(F32)
    tail_backward(
        info, cot[...], w_out, w_up, w_down, gains[1], slope, units, scales,
        bx_kept, bx_sent, norm_grads, d_first, d_att, every,
    )


def attend_back_kernel(unused, query, kv_near, kv_far, probs_near, probs_far, d_att, d_query, d_kv_near, d_kv_far):
    attend_backward(query, kv_near, kv_far, probs_near, probs_far, d_att, d_query, d_kv_near, d_kv_far)


def close_layer(info, d_query, d_kv, d_kv_far, d_first, w_qkv, kept, sent, every):
    shards = 4
    width = d_query.shape[1]
    total = (d_kv[...].astype(F32) + d_kv_far[...].astype(F32)).astype(BF16)
    d_qkv = jnp.concatenate([d_query[...], total], axis=1)
    d_hidden = d_first[...] + dot_nt(d_qkv, w_qkv[...])
    low = d_hidden.astype(BF16)
    step, part = 3 * width // shards, width // shards
    for at in range(shards):
        every[at, :, :step] = d_qkv[:, at * step : (at + 1) * step]
        every[at, :, step:] = low[:, at * part : (at + 1) * part]
    part_ways(info, every, kept, sent)
    return d_hidden, low


def middle_kernel(
    info, d_query, d_kv, d_kv_far, d_first, w_qkv, gains, slope, units, scales, w_out, w_up, w_down, norms_late,
    qx_kept, qx_sent, bx_kept, bx_sent, norm_grads, d_first_out, d_att, every_qx, every_bx,
):
    d_hidden, unused = close_layer(info, d_query, d_kv, d_kv_far, d_first, w_qkv, qx_kept, qx_sent, every_qx)
    norm_grads[4:, :] = norms_late[...]
    tail_backward(
        info, d_hidden, w_out, w_up, w_down, gains[0], slope, units, scales,
        bx_kept, bx_sent, norm_grads, d_first_out, d_att, every_bx,
    )


def last_kernel(info, d_query, d_kv, d_kv_far, d_first, w_qkv, norms, qx_kept, qx_sent, grad, every):
    unused, low = close_layer(info, d_query, d_kv, d_kv_far, d_first, w_qkv, qx_kept, qx_sent, every)
    grad[...] = low
    tokens = d_query.shape[0]
    padded = jnp.concatenate([norms[...], jnp.zeros(norms.shape, F32)], axis=0)
    qx_sent[0, tokens:, :] = padded.astype(BF16)
    qx_sent[1, tokens:, :] = jnp.zeros(padded.shape, BF16)


def split_blocks(info, places, whole_ref, kept, sent):
    def split(place):
        bit, axis, at = place
        mine = (info[axis] >> at) & 1
        for ref, value in ((sent, 1 - mine), (kept, mine)):
            for index in range(ref.shape[0]):
                low = index & ((1 << bit) - 1)
                source = ((index >> bit) << (bit + 1)) + low + (value << bit)
                total = whole_ref[0][source]
                for other in whole_ref[1:]:
                    total = total + other[source]
                ref[index] = total

    if places[0] == places[1]:
        split(places[0])
    else:
        for core in range(2):
            pl.when(info[ME] % 2 == core)(functools.partial(split, places[core]))


def fold_kernel(places, info, kept, got, new_kept, new_sent):
    split_blocks(info, places, (kept, got), new_kept, new_sent)


def put(pieces, whole, name, x, value):
    for at, (tiles, unused) in enumerate(pieces):
        if name in tiles:
            lanes = value.shape[2]
            start = tiles.index(name) * lanes
            n_dp = value.shape[0]
            whole[at][x * n_dp : (x + 1) * n_dp, :, start : start + lanes] = value.astype(BF16)


def by_blocks(value, n_dp):
    return value.reshape(n_dp, value.shape[0] // n_dp, value.shape[1])


def feed_grad_kernel(pieces, info, x_near, x_far, b_near, b_far, *refs):
    count = len(pieces)
    outs, whole = refs[: 2 * count], refs[2 * count :]
    n_dp, rows = outs[0].shape[0], outs[0].shape[1]
    width = n_dp * rows
    inner = x_near.shape[1] - 3 * width
    step, part = inner // 4, width // 4
    for x in range(2):
        total = dot_tn(x_near[:, inner : inner + width], b_near[x, :, :step])
        total = total + dot_tn(x_far[:, inner : inner + width], b_far[x, :, :step])
        for tile in range(step // part):
            put(pieces, whole, ("up", tile), x, by_blocks(total[:, tile * part : (tile + 1) * part], n_dp))
    feeds = [
        jnp.concatenate([ref[0, :, step : step + part], ref[1, :, step : step + part]], axis=1)
        for ref in (b_near, b_far)
    ]
    span_size = 512
    fold = inner // width
    for at in range(inner // span_size):
        span = slice(at * span_size, (at + 1) * span_size)
        total = dot_tn(feeds[0], x_near[:, span]) + dot_tn(feeds[1], x_far[:, span])
        total = total.astype(BF16).T if rows % 16 == 0 else total.T
        for group in range(span_size // rows):
            block, tile = divmod(at * (span_size // rows) + group, fold)
            for index, (tiles, unused) in enumerate(pieces):
                if ("down", tile) in tiles:
                    start = tiles.index(("down", tile)) * part
                    for x in range(2):
                        value = total[group * rows : (group + 1) * rows, x * part : (x + 1) * part]
                        whole[index][x * n_dp + block, :, start : start + part] = value.astype(BF16)
    for at, (unused, places) in enumerate(pieces):
        split_blocks(info, places, (whole[at],), outs[2 * at], outs[2 * at + 1])


def attend_grad_kernel(pieces, with_norms, info, x_near, x_far, b_near, b_far, q_near, q_far, *refs):
    count = len(pieces)
    norms = None
    if with_norms:
        norms, refs = refs[0], refs[1:]
    outs, whole, table = refs[: 2 * count], refs[2 * count : -1], refs[-1]
    n_dp, rows = outs[0].shape[0], outs[0].shape[1]
    width = n_dp * rows
    part = width // 4
    tokens = x_near.shape[0]
    inner = x_near.shape[1] - 3 * width
    step = 3 * part
    feed = inner // 4 + part
    skip = q_near.shape[2] - width
    core = info[ME] % 2
    size = tokens // 4
    for x in range(2):
        lows = slice(inner + 2 * width, inner + 3 * width)
        total = dot_tn(x_near[:, lows], q_near[x, :, skip : skip + step])
        total = total + dot_tn(x_far[:, lows], q_far[x, :tokens, skip : skip + step])
        for tile in range(step // part):
            put(pieces, whole, ("qkv", tile), x, by_blocks(total[:, tile * part : (tile + 1) * part], n_dp))
        outs_at = slice(inner + width, inner + 2 * width)
        total = dot_tn(x_near[:, outs_at], b_near[x, :, feed : feed + part])
        total = total + dot_tn(x_far[:, outs_at], b_far[x, :, feed : feed + part])
        put(pieces, whole, ("out", 0), x, by_blocks(total, n_dp))
        table[...] = jnp.zeros_like(table)
        for source, place in ((q_near, core), (q_far, 1 - core)):
            for block in range(4):
                span = pl.ds(block_start(info, block, place, size), size)
                table[span, :] += source[x, block * size : (block + 1) * size, skip + step :].astype(F32)
        put(pieces, whole, ("pos", 0), x, by_blocks(table[...], n_dp))
    if with_norms:
        sums = norms[...] + q_far[0, tokens:, :].astype(F32)[: norms.shape[0]]
        share = width // n_dp
        for block in range(n_dp):
            value = sums[:, block * share : (block + 1) * share]
            value = jnp.concatenate([value, jnp.zeros((value.shape[0], part - share), F32)], axis=1)
            if rows > value.shape[0]:
                value = jnp.concatenate([value, jnp.zeros((rows - value.shape[0], part), F32)], axis=0)
            for at, (tiles, unused) in enumerate(pieces):
                if ("norm", 0) in tiles:
                    start = tiles.index(("norm", 0)) * part
                    for x in range(2):
                        whole[at][x * n_dp + block, :, start : start + part] = value.astype(BF16)
    for at, (unused, places) in enumerate(pieces):
        split_blocks(info, places, (whole[at],), outs[2 * at], outs[2 * at + 1])


def final_kernel(pieces, info, *refs):
    ins, (*sums, gain, shift) = refs[: 2 * len(pieces)], refs[2 * len(pieces) :]
    outs = dict(zip(("qkv", "out", "up", "down", "pos"), sums))
    for at, (layer_at, tiles) in enumerate(pieces):
        kept, got = ins[2 * at], ins[2 * at + 1]
        rows = kept.shape[1]
        part = outs["out"].shape[2]
        for index, (name, tile) in enumerate(tiles):
            lanes = slice(index * part, (index + 1) * part)
            total = kept[0, :, lanes].astype(F32) + got[0, :, lanes].astype(F32)
            if name == "norm":
                share = gain.shape[2]
                for row in range(8):
                    ref = (gain, shift)[row // 2 % 2]
                    ref[row // 4, row % 2 : row % 2 + 1, :] = total[row : row + 1, :share]
            elif name == "down":
                outs[name][layer_at, tile * rows : (tile + 1) * rows, :] = total
            else:
                outs[name][layer_at, :, tile * part : (tile + 1) * part] = total


MB = 1024 * 1024
TOKEN = ((8, 128), F32)
SMEM = pl.BlockSpec(memory_space=pltpu.SMEM)
VMEM = pl.BlockSpec(memory_space=pltpu.VMEM)
HBM = pl.BlockSpec(memory_space=pltpu.HBM)

FLOPS = 10**10
COSTS = dict(feed1=0, middle=0, back=0, rest1=0, feed0=0, last=0, rest0=0, fold=10000000000, pack=0, tick=0)


def pin(array):
    return pltpu.with_memory_space_constraint(array, pltpu.VMEM)


class Line:
    def __init__(self):
        self.token = None
        self.trail = []
        self.used = set()

    def flip(self, array, axis, bit):
        size = lax.axis_size(axis)
        self.trail.append(lax.ppermute(array, axis, [(at, at ^ bit) for at in range(size)]))
        return self.trail[-1]

    def cross(self, array, steps):
        n_dp, n_seq = lax.axis_size("dp"), lax.axis_size("seq")
        pairs = []
        for dp in range(n_dp):
            for seq in range(n_seq):
                step = steps[seq % 2]
                other = (dp, seq ^ 2) if step == "x" else (dp ^ (1 << step), seq)
                pairs.append((dp * n_seq + seq, other[0] * n_seq + other[1]))
        self.trail.append(lax.ppermute(array, ("dp", "seq"), pairs))
        return self.trail[-1]

    def near(self, array):
        return self.flip(array, "seq", 1)

    def gather(self, parts):
        return [parts[0]] + [self.flip(parts[delta], "seq", delta) for delta in (1, 2, 3)]

    def past(self, used=True):
        return [array for array in self.trail if (id(array) in self.used) == used]

    def tick(self, after=()):
        self.call("tick", lambda info: None, [], (), after=after)

    def call(self, name, kernel, outs, args, scratch=(), limit=8, smem=0, hbm=0, final=False, after=(), past=()):
        self.used.update(id(arg) for arg in (*args, *after))
        tokens = [] if self.token is None else [self.token]
        skip = len(past)
        shapes = [jax.ShapeDtypeStruct(*kind) if final else pltpu.VMEM(*kind) for kind in outs] + [pltpu.VMEM(*TOKEN)]
        count, extra = len(args), len(tokens) + len(after)

        def body(*refs):
            refs = refs[skip:]
            given = refs[:count]
            made = refs[count + extra : count + extra + len(outs)]
            refs[count + extra + len(outs)][...] = jnp.zeros(TOKEN[0], F32)
            info = (lax.axis_index("seq"), None, lax.axis_index("dp"))
            kernel(info, *given, *made, *refs[count + extra + len(outs) + 1 :])

        far = smem + hbm
        operands = [pin(array) for array in past] + list(args[:smem]) + [pltpu.with_memory_space_constraint(arg, pltpu.HBM) for arg in args[smem:far]]
        operands += [pin(arg) for arg in args[far:]]
        operands += [pin(array) for array in (*after, *tokens)]
        results = pl.pallas_call(
            body,
            in_specs=[VMEM] * skip + [SMEM] * smem + [HBM] * hbm + [VMEM] * (count - far + extra),
            out_specs=[VMEM] * (len(outs) + 1),
            out_shape=shapes,
            scratch_shapes=list(scratch),
            compiler_params=pltpu.CompilerParams(vmem_limit_bytes=limit * MB),
            cost_estimate=pl.CostEstimate(flops=COSTS.get(name, FLOPS), bytes_accessed=0, transcendentals=0),
            name=name,
        )(*operands)
        self.token = results[-1]
        return list(results[:-1])


FEED = tuple(("up", at) for at in range(4)) + tuple(("down", at) for at in range(4))
REST = (("qkv", 0), ("qkv", 1), ("qkv", 2), ("out", 0), ("pos", 0))
LAST = REST + (("norm", 0),)
PIECES = dict(
    a=(1, "feed1", FEED, "xyhl", "lhyx"),
    b=(1, "rest1", REST, "yxhl", "yhlx"),
    c=(0, "feed0", FEED, "lxyh", "xlhy"),
    d=(0, "rest0", LAST, "yxlh", "xlyh"),
)
ORDER = (
    "feed1", "middle", "back", "feed0", "rest1", "last", "a", "rest0", "c", "b", "a", "pack", "d", "c", "swap", "b",
    "d", "c", "a", "d", "take", "b",
)


class Sum:
    def __init__(self, name, n_bits):
        self.layer_at, self.maker, self.tiles, *paths = PIECES[name]
        letters = {"x": ["x"], "y": [0], "l": [1], "h": list(range(2, n_bits))}
        self.steps = [[bit for letter in path for bit in letters[letter] if bit == "x" or bit < n_bits] for path in paths]
        self.bits = [[*range(n_bits), "x"] for unused in paths]

    def left(self):
        return len(self.steps[0])

    def place(self):
        places = []
        for steps, bits in zip(self.steps, self.bits):
            where = bits.index(steps[0])
            places.append((where, ME, 1) if steps[0] == "x" else (where, DP, steps[0]))
        return places

    def start(self, line, kept, sent):
        now = [steps.pop(0) for steps in self.steps]
        for bits, step in zip(self.bits, now):
            bits.remove(step)
        self.kept = kept
        self.got = line.cross(sent, now)

    def fold(self, line):
        blocks, rows, columns = self.kept.shape
        kind = ((blocks // 2, rows, columns), BF16)
        self.start(line, *line.call("fold", functools.partial(fold_kernel, self.place()), [kind, kind], (self.kept, self.got)))


def local(
    x_short, x_long, len_short, len_long, w_qkv, w_out, w_up, w_down, pos_table, norm_gain, norm_bias, cot_short, cot_long
):
    n_dp = lax.axis_size("dp")
    n_bits = n_dp.bit_length() - 1
    width = x_short.shape[2]
    size = x_short.shape[1]
    tokens = 4 * size
    half = tokens // 2
    inner = w_up.shape[2]
    pairs = width // (2 * HD)
    rows = width // n_dp
    part = ((size, width), BF16)
    hidden_kind = ((tokens, width), F32)
    low_kind = ((tokens, width), BF16)
    kv_kind = ((tokens, 2 * width), BF16)
    probs_kinds = [((pairs, 2 * half, 2 * half), BF16), ((pairs, 4 * half, 2 * half), BF16)]
    slope_kind = ((tokens, inner), BF16)
    x_kind = ((tokens, inner + 3 * width), BF16)
    units_kind = ((2, tokens, width), F32)
    scales_kind = ((2, tokens, 1), F32)
    bx_kind = ((2, tokens, inner // 4 + width // 2), BF16)
    qx_kind = ((2, tokens, width), BF16)
    every_bx = pltpu.VMEM((4, *bx_kind[0][1:]), BF16)
    every_qx = pltpu.VMEM((4, *qx_kind[0][1:]), BF16)
    biases = [pltpu.VMEM((2 * half, half), F32), pltpu.VMEM((4 * half, half), F32)]
    lens = (len_short, len_long)
    line = Line()
    sums = {name: Sum(name, n_bits) for name in PIECES}

    four = [pltpu.SemaphoreType.DMA((4,))]
    rows_in = line.gather(line.call("split", split_kernel, [part] * 4, (x_short, x_long), four, hbm=2))
    stacks = (w_qkv, w_out, w_up, w_down)
    kinds = [(array.shape[1:], BF16) for array in stacks]
    loaded = line.call(
        "load", load_kernel, [(pos_table.shape, BF16)] + kinds + kinds[1:3] + [part] * 4,
        (pos_table, *stacks, cot_short, cot_long), [pltpu.SemaphoreType.DMA((36,))] + four, hbm=7,
    )
    table, w_qkv0, w_out0, w_up0, w_down0, w_out1, w_up1, *cots = loaded
    hidden0, rounded0, query0, kv0 = line.call(
        "front", front_kernel, [hidden_kind, low_kind, low_kind, kv_kind], (*rows_in, table, w_qkv0)
    )
    kv0_far = line.near(kv0)
    w_qkv1, w_down1 = line.call(
        "load", load_late_kernel, [kinds[0], kinds[3]], (w_qkv, w_down), [pltpu.SemaphoreType.DMA((8,))], hbm=2
    )
    layer_kinds = probs_kinds + [slope_kind, x_kind, units_kind, scales_kind]
    probs_near0, probs_far0, slope0, x0, units0, scales0, hidden1, rounded1, query1, kv1 = line.call(
        "first", first_kernel, layer_kinds + [hidden_kind, low_kind, low_kind, kv_kind],
        (
            *lens, query0, kv0, kv0_far, hidden0, rounded0, table, norm_gain, norm_bias,
            w_out0, w_up0, w_down0, w_qkv1,
        ),
        biases, limit=16, smem=2,
    )
    kv1_far = line.near(kv1)
    cot_in = line.gather(line.call("copy", copy_kernel, [part] * 4, cots))
    x0_far = line.near(x0)
    probs_near1, probs_far1, slope1, x1, units1, scales1, act = line.call(
        "second", second_kernel, layer_kinds + [low_kind],
        (*lens, query1, kv1, kv1_far, hidden1, rounded1, norm_gain, norm_bias, w_out1, w_up1, w_down1),
        biases, limit=16, smem=2,
    )
    x1_far = line.near(x1)
    bx1, bx1_sent, norms1, d_first1, d_att1 = line.call(
        "turn", turn_kernel, [bx_kind, bx_kind, ((4, width), F32), hidden_kind, low_kind],
        (*cot_in, norm_gain, slope1, units1, scales1, w_out1, w_up1, w_down1), [pltpu.VMEM(*hidden_kind), every_bx],
    )
    bx1_far = line.near(bx1_sent)

    def grads(maker, kernel, args, scratch=()):
        made = [each for each in sums.values() if each.maker == maker]
        pieces = [(each.tiles, each.place()) for each in made]
        columns = [len(each.tiles) * (width // 4) for each in made]
        outs = line.call(
            maker, functools.partial(kernel, pieces),
            [((n_dp, rows, count), BF16) for count in columns for unused in range(2)],
            args, [pltpu.VMEM((2 * n_dp, rows, count), BF16) for count in columns] + list(scratch), limit=12,
        )
        for at, each in enumerate(made):
            each.start(line, outs[2 * at], outs[2 * at + 1])

    table = [pltpu.VMEM((width, width // 4), F32)]
    back_kinds = [low_kind, kv_kind, kv_kind]
    d_query1, d_kv1, d_kv1_sent = line.call(
        "attend_back", attend_back_kernel, back_kinds, (query1, kv1, kv1_far, probs_near1, probs_far1, d_att1), after=[x0_far]
    )
    d_kv1_far = line.near(d_kv1_sent)
    latest = None
    order = list(ORDER)
    while order or any(each.left() for each in sums.values()):
        if not order:
            order = [name for name, each in sums.items() if each.left()]
        task = order.pop(0)
        if task in sums:
            if sums[task].left():
                if task == latest:
                    line.tick()
                sums[task].fold(line)
                latest = task
        elif task == "tick":
            line.tick()
        elif task == "feed1":
            grads("feed1", feed_grad_kernel, (x1, x1_far, bx1, bx1_far))
        elif task == "middle":
            qx1, qx1_sent, bx0, bx0_sent, norms, d_first0, d_att0 = line.call(
                "middle", middle_kernel, [qx_kind, qx_kind, bx_kind, bx_kind, ((8, width), F32), hidden_kind, low_kind],
                (
                    d_query1, d_kv1, d_kv1_far, d_first1, w_qkv1, norm_gain, slope0, units0, scales0, w_out0, w_up0, w_down0,
                    norms1,
                ),
                [every_qx, every_bx],
            )
            bx0_far = line.near(bx0_sent)
            qx1_far = line.near(qx1_sent)
        elif task == "back":
            d_query0, d_kv0, d_kv0_sent = line.call(
                "back", attend_back_kernel, back_kinds, (query0, kv0, kv0_far, probs_near0, probs_far0, d_att0)
            )
            d_kv0_far = line.near(d_kv0_sent)
        elif task == "rest1":
            grads(
                "rest1", lambda pieces, *refs: attend_grad_kernel(pieces, False, *refs),
                (x1, x1_far, bx1, bx1_far, qx1, qx1_far), table,
            )
        elif task == "feed0":
            grads("feed0", feed_grad_kernel, (x0, x0_far, bx0, bx0_far))
        elif task == "last":
            longer = ((2, tokens + 16, width), BF16)
            qx0, qx0_sent, grad = line.call(
                "last", last_kernel, [qx_kind, longer, low_kind], (d_query0, d_kv0, d_kv0_far, d_first0, w_qkv0, norms),
                [every_qx],
            )
            qx0_far = line.near(qx0_sent)
        elif task == "rest0":
            grads(
                "rest0", lambda pieces, *refs: attend_grad_kernel(pieces, True, *refs),
                (x0, x0_far, bx0, bx0_far, qx0, qx0_far, norms), table,
            )
        elif task == "pack":
            own_rows, rows_sent = line.call("pack", pack_kernel, [((2, 2 * size, width), BF16)] * 2, (act, grad))
            chip_rows = line.flip(rows_sent, "seq", 2)
        elif task == "swap":
            (rows_sent,) = line.call("pack", swap_kernel, [((2, 2 * size, width), BF16)], (own_rows, chip_rows))
            core_rows = line.near(rows_sent)
        elif task == "take":
            line.tick(after=[core_rows])
    joined = line.call(
        "join", join_kernel, [(x_short.shape, BF16), (x_long.shape, BF16)] * 2, (own_rows, chip_rows, core_rows), final=True,
        past=line.past(),
    )
    shard = ((LAYERS, rows, width // 4), F32)
    totals = line.call(
        "final", functools.partial(final_kernel, [(each.layer_at, each.tiles) for each in sums.values()]),
        [
            ((LAYERS, rows, 3 * width // 4), F32), shard, ((LAYERS, rows, inner // 4), F32),
            ((LAYERS, inner // n_dp, width // 4), F32), shard,
            ((LAYERS, 2, rows), F32), ((LAYERS, 2, rows), F32),
        ],
        [array for each in sums.values() for array in (each.kept, each.got)], final=True, past=line.past(False),
    )
    return (*joined, *totals)


def solution(mesh):
    rows = P("dp", "seq", None)
    grads = P(None, "dp", "seq")
    norms = P(None, None, "dp")
    return jax.shard_map(
        local,
        mesh=mesh,
        in_specs=(rows, rows, P("dp"), P("dp")) + (P(),) * 7 + (rows, rows),
        out_specs=(rows,) * 4 + (grads,) * 5 + (norms, norms),
        check_vma=False,
    )
```
